32 devices in a mesh: plane: 2 (over x), coil: 16 (over z, y, core).
Axes of the slice: x: 2, y: 2, z: 4, core: 2. Of those that a mesh axis runs over, the one named last changes fastest.
Arguments:
- image: float32 [512, 8, 512], P(('plane', 'coil')), parts along dimension 0, may hold values from -6 to 6
- sens: float32 [512, 32, 512], P(('plane', 'coil')), parts along dimension 0, may hold values from -0.75 to 0.75
- kspace: float32 [512, 256, 512], P('plane', 'coil'), parts along dimension 0, may hold values from -6 to 6
- mask: int32 [8, 256], replicated, may hold values 0 or 1
Outputs:
- recon: float32 [512, 8, 512], P(('plane', 'coil')), parts along dimension 0
The draws below stay inside these ranges and needn't reach their ends.
There are 2 independent parts, one for each index of `plane`. The reference program is written for one: setup_inputs(seed, part) draws one part's arguments, and reference() takes and returns one part's arrays. A program takes and returns all parts, laid end to end along the dimension named above; an argument that names none is the same for every part. Nothing has to cross between parts.
Inputs may be any that keep to these rules, and one draw needn't show every extreme that they name: mask[f, ky] is 1 where phase-encode line ky is sampled in frame f, else 0.
All inputs are finite; a program needn't handle non-finite values.
Results may differ from the reference program's by a relative error of at most 0.0001.
Values sent between devices are 32-bit elements; how exact they have to be, the bound alone decides.
No kernel may reach another device: no remote copies, remote signals or barrier semaphores. Data moves between devices by JAX's collectives and lax.ppermute only.
A program may use at most 128 MiB of HBM per device.

```python
import jax
import jax.numpy as jnp
from jax import lax

NY = 256
NZ = 256
COILS = 32
FRAMES = 8
OUTER = 2
INNER = 2


def plant(array, rng, least, top_value):
    spot = [jax.random.randint(jax.random.fold_in(rng, axis), (), 0, length) for axis, length in enumerate(array.shape)]
    longest = array.shape.index(max(array.shape))
    neighbour = spot[:longest] + [(spot[longest] + 1) % array.shape[longest]] + spot[longest + 1:]
    return array.at[tuple(spot)].set(least).at[tuple(neighbour)].set(top_value)


def steps_of(rng, extent, shards, low, top_value):
    level, own = 1.0, jax.random.fold_in(rng, 6)
    for axis_at, parts in shards:
        steps = jnp.exp(jax.random.uniform(jax.random.fold_in(own, axis_at), (parts,), jnp.float32, low / len(shards), top_value / len(shards)))
        level = level * jnp.repeat(steps, extent[axis_at] // parts).reshape([-1 if axis == axis_at else 1 for axis in range(len(extent))])
    return level


def centred(rng, dims, width, limit, cuts=(), held_as=jnp.bfloat16):
    level = steps_of(rng, dims, cuts, -0.22, 0.18) if cuts else 1.0
    values = jax.random.normal(rng, dims, jnp.float32) * width * level
    return jnp.minimum(jnp.maximum(values, -limit), limit).astype(held_as)


def setup_inputs(seed: int = 0, part: int = 0) -> dict:
    splits = jax.random.split(jax.random.key(seed), 5)
    part_splits = jax.random.split(jax.random.fold_in(splits[4], part), 5)
    return {
        "image": centred(part_splits[0], (NY, FRAMES, 2 * NZ), 1.0, 6.0, ((0, 16),), jnp.float32),
        "sens": centred(part_splits[1], (NY, COILS, 2 * NZ), 0.125, 0.75, ((0, 16),), jnp.float32),
        "kspace": centred(part_splits[2], (NY, COILS * FRAMES, 2 * NZ), 1.0, 6.0, ((1, 16),), jnp.float32),
        "mask": plant((jax.random.randint(splits[3], (FRAMES, NY), 0, 3) < 1).astype(jnp.int32), jax.random.fold_in(splits[3], 1), 0, 1),
    }


step_size = 0.5
tv_weight = 0.1
dual_step = 1.25


def unpack_complex(packed):
    half = packed.shape[-1] // 2
    return lax.complex(packed[..., :half], packed[..., half:])


def pack_complex(values):
    return jnp.concatenate([jnp.real(values), jnp.imag(values)], -1)


def forward_diff(field):
    diff_rows = jnp.concatenate([field[1:] - field[:-1], jnp.zeros_like(field[:1])], 0)
    diff_time = jnp.concatenate([field[:, 1:] - field[:, :-1], jnp.zeros_like(field[:, :1])], 1)
    return diff_time, diff_rows


def adjoint_diff(dual_time, dual_rows):
    keep_time = (lax.iota(jnp.int32, dual_time.shape[1]) < dual_time.shape[1] - 1)[None, :, None]
    keep_rows = (lax.iota(jnp.int32, dual_rows.shape[0]) < dual_rows.shape[0] - 1)[:, None, None]
    from_time = jnp.concatenate([jnp.zeros_like(dual_time[:, :1]), dual_time[:, :-1]], 1) - jnp.where(keep_time, dual_time, 0.0)
    from_rows = jnp.concatenate([jnp.zeros_like(dual_rows[:1]), dual_rows[:-1]], 0) - jnp.where(keep_rows, dual_rows, 0.0)
    return from_time + from_rows


def reference(image, sens, kspace, mask):
    maps = jnp.transpose(unpack_complex(sens), (1, 0, 2))
    data = jnp.transpose(unpack_complex(kspace).reshape(NY, COILS, FRAMES, NZ), (1, 2, 0, 3))
    sampled = mask.astype(jnp.float32)[:, :, None]
    field = image
    for sweep in range(OUTER):
        frames_now = jnp.transpose(unpack_complex(field), (1, 0, 2))

        def add_coil(total, coil_input):
            coil_map, coil_data = coil_input
            spectrum = jnp.fft.fft2(coil_map[None] * frames_now, axes=(1, 2), norm="ortho")
            residual = sampled * (spectrum - coil_data)
            term = jnp.conj(coil_map)[None] * jnp.fft.ifft2(residual, axes=(1, 2), norm="ortho")
            return total + term, None

        total, unused = lax.scan(add_coil, jnp.zeros_like(frames_now), (maps, data))
        gradient = pack_complex(jnp.transpose(total, (1, 0, 2)))
        target = field - step_size * gradient
        dual_time = jnp.zeros_like(target)
        dual_rows = jnp.zeros_like(target)
        for repeat in range(INNER):
            primal = target - tv_weight * adjoint_diff(dual_time, dual_rows)
            diff_time, diff_rows = forward_diff(primal)
            dual_time = jnp.clip(dual_time + dual_step * diff_time, -1.0, 1.0)
            dual_rows = jnp.clip(dual_rows + dual_step * diff_rows, -1.0, 1.0)
        field = target - tv_weight * adjoint_diff(dual_time, dual_rows)
    return field
```

```python
import functools

import jax
import jax.numpy as jnp
import ml_dtypes
import numpy as np
from jax import lax
from jax.experimental import pallas as pl
from jax.experimental.pallas import tpu as pltpu
from jax.sharding import PartitionSpec as P

OUTER = 2
INNER = 2
LANES = 128
VMEM_LIMIT = 48 * 1024 * 1024

step_size = 0.5
tv_weight = 0.1
dual_step = 1.25
highest = lax.Precision.HIGHEST


def two_terms(table):
    first = table.astype(ml_dtypes.bfloat16)
    second = (table - first.astype(np.float64)).astype(ml_dtypes.bfloat16)
    return first, second


def dft(out_index, in_index, length):
    product = np.outer(out_index, in_index) % length
    return np.exp(2j * np.pi / length * product)


def packed_left(matrix):
    return np.block([[matrix.real, -matrix.imag], [matrix.imag, matrix.real]])


def packed_right(matrix):
    return packed_left(matrix).T


def split(value):
    first = value.astype(jnp.bfloat16)
    second = (value - first.astype(jnp.float32)).astype(jnp.bfloat16)
    return first, second


def dot3(left, right, contract=((1,), (0,))):
    dims = (contract, ((), ()))

    def dot(a, b):
        return lax.dot_general(a, b, dims, preferred_element_type=jnp.float32)

    return dot(left[0], right[0]) + (dot(left[0], right[1]) + dot(left[1], right[0]))


def lane_exchange(parts, width):
    parts = list(parts)
    lane = lax.broadcasted_iota(jnp.int32, parts[0].shape, parts[0].ndim - 1)
    axis = parts[0].ndim - 1
    bit = 1
    while bit < len(parts):
        odd = (lane // width) & bit != 0
        for s in range(len(parts)):
            if s & bit:
                continue
            low, high = parts[s], parts[s | bit]
            parts[s] = jnp.where(odd, pltpu.roll(high, width * bit, axis), low)
            parts[s | bit] = jnp.where(odd, high, pltpu.roll(low, LANES - width * bit, axis))
        bit *= 2
    return parts


def roll_last(value, distance):
    shape = value.shape
    flat = value.reshape(-1, shape[-1])
    return pltpu.roll(flat, distance % shape[-1], 1).reshape(shape)


def tv_step(target):
    length = target.shape[-1]
    row = lax.broadcasted_iota(jnp.int32, target.shape, target.ndim - 1)
    last, first = row == length - 1, row == 0
    nothing = jnp.zeros_like(target[:1])

    def adjoint(dual_time, dual_rows):
        from_time = jnp.concatenate([nothing, dual_time[:-1]], 0) - jnp.concatenate(
            [dual_time[:-1], nothing], 0
        )
        from_rows = jnp.where(first, 0.0, roll_last(dual_rows, 1)) - jnp.where(last, 0.0, dual_rows)
        return from_time + from_rows

    dual_time = jnp.zeros_like(target)
    dual_rows = jnp.zeros_like(target)
    primal = target
    for repeat in range(INNER):
        diff_time = jnp.concatenate([primal[1:] - primal[:-1], nothing], 0)
        diff_rows = jnp.where(last, 0.0, roll_last(primal, -1) - primal)
        dual_time = jnp.clip(dual_time + dual_step * diff_time, -1.0, 1.0)
        dual_rows = jnp.clip(dual_rows + dual_step * diff_rows, -1.0, 1.0)
        primal = target - tv_weight * adjoint(dual_time, dual_rows)
    return primal


def normal_frame(maps_ref, field_re, field_im, tables):
    coils, _, cols, length = maps_ref.shape
    half = length // 2
    maps_re, maps_im = maps_ref[:, 0], maps_ref[:, 1]
    u_re = maps_re * field_re[None] - maps_im * field_im[None]
    u_im = maps_re * field_im[None] + maps_im * field_re[None]
    flat_re = u_re.reshape(coils * cols, length)
    flat_im = u_im.reshape(coils * cols, length)
    outs = []
    for sign, table in zip((1.0, -1.0), tables):
        packed = jnp.concatenate(
            [
                flat_re[:, :half] + sign * flat_re[:, half:],
                flat_im[:, :half] + sign * flat_im[:, half:],
            ],
            1,
        )
        outs.append(dot3(split(packed), table))
    plus, minus = outs
    v_re = jnp.concatenate(
        [plus[:, :half] + minus[:, :half], plus[:, :half] - minus[:, :half]], 1
    ).reshape(coils, cols, length)
    v_im = jnp.concatenate(
        [plus[:, half:] + minus[:, half:], plus[:, half:] - minus[:, half:]], 1
    ).reshape(coils, cols, length)
    return (
        jnp.sum(maps_re * v_re + maps_im * v_im, 0),
        jnp.sum(maps_re * v_im - maps_im * v_re, 0),
    )


def coil_blocks_kernel(coils, *refs):
    *tiles, out_ref = refs
    devices, own, rows, _ = out_ref.shape
    for d in range(devices):
        for c in range(own):
            for t, ref in enumerate(tiles):
                out_ref[d, c, :, t * LANES : (t + 1) * LANES] = ref[
                    pl.ds(d * own + c, rows, stride=coils), :
                ]


def column_blocks_kernel(coils, frames, chunk_of, *refs):
    *tiles, out_ref = refs
    sens_tiles, image_tiles = tiles[: len(tiles) // 2], tiles[len(tiles) // 2 :]
    devices, groups, _, cols, _ = out_ref.shape
    rows = sens_tiles[0].shape[0] // coils
    per = LANES // rows
    half = len(sens_tiles) // 2
    for g in range(groups):
        if g * per < coils:
            tiles, count, base = sens_tiles, coils, g * per
        else:
            tiles, count, base = image_tiles, frames, g * per - coils
        for t, ref in enumerate(tiles):
            turned = jnp.concatenate(
                [ref[pl.ds(base + c, rows, stride=count), :] for c in range(per)], 0
            ).T
            for d in range(devices):
                at = chunk_of[d] * cols - t % half * LANES
                if 0 <= at < LANES:
                    out_ref[d, g, t // half] = turned[at : at + cols]


def mask_tables_kernel(mask_ref, in_hi, in_lo, out_hi, out_lo, hi_ref, lo_ref):
    for side in range(2):
        row = mask_ref[0, side : side + 1, :].astype(jnp.bfloat16)
        left = (in_hi[side] * row, in_lo[side] * row)
        hi_ref[0, side], lo_ref[0, side] = split(dot3(left, (out_hi[side], out_lo[side])))


def base_kernel(pairs, *refs):
    *tiles, mask_ref, col_hi, col_lo, row_hi, row_lo, out_ref = refs
    p = pl.program_id(0)
    length = out_ref.shape[-1]
    half_cols = out_ref.shape[-2]
    half = length // 2
    data = jnp.concatenate(
        [
            jnp.concatenate([ref[pl.ds(at + p, half, stride=2 * pairs), :] for ref in tiles], 1)
            for at in (0, pairs)
        ],
        0,
    )
    columns = dot3((col_hi[...], col_lo[...]), split(data), ((1,), (1,)))
    columns = columns * mask_ref[0]
    re, im = columns[:half_cols], columns[half_cols:]
    even, odd = [
        dot3(
            split(jnp.concatenate([re[:, at : at + half], im[:, at : at + half]], 1)),
            (row_hi[side], row_lo[side]),
        )
        for side, at in enumerate((0, half))
    ]
    out_ref[0, 0] = jnp.concatenate([even[:, :half] + odd[:, :half], even[:, :half] - odd[:, :half]], 1)
    out_ref[0, 1] = jnp.concatenate([even[:, half:] + odd[:, half:], even[:, half:] - odd[:, half:]], 1)


def weigh_kernel(bit_ref, maps_ref, base_ref, keep_ref, send_ref, turned):
    devices, own, rows, packed = maps_ref.shape
    half_cols = packed // 2
    length = devices * rows

    @pl.when(pl.program_id(0) == 0)
    def _():
        for c in range(own):
            whole = maps_ref[:, c].reshape(length, packed).T
            turned[c, 0] = whole[:half_cols]
            turned[c, 1] = whole[half_cols:]

    bit = bit_ref[0]
    span = half_cols // 2
    blocks = devices // 2
    for ref, which in ((send_ref, 1 - bit), (keep_ref, bit)):
        at = pl.ds(pl.multiple_of(which * span, span), span)
        total_re = total_im = None
        for c in range(own):
            s_re, s_im = turned[c, 0, at, :], turned[c, 1, at, :]
            b_re, b_im = base_ref[c, 0, 0, at, :], base_ref[c, 0, 1, at, :]
            t_re = s_re * b_re + s_im * b_im
            t_im = s_re * b_im - s_im * b_re
            total_re = t_re if c == 0 else total_re + t_re
            total_im = t_im if c == 0 else total_im + t_im
        ref[:, 0, 0] = total_re.reshape(blocks, span // blocks, length)
        ref[:, 0, 1] = total_im.reshape(blocks, span // blocks, length)


def first_normal_kernel(coils, got_ref, hi_ref, lo_ref, maps_out, field_out, grad_out):
    devices, groups, _, cols, lanes = got_ref.shape
    frames = field_out.shape[0]
    per = (coils + frames) // groups
    width = lanes // per
    for g in range(groups):
        out, base = (maps_out, g * per) if g * per < coils else (field_out, g * per - coils)
        for h in range(devices // per):
            exchanged = lane_exchange([got_ref[h * per + s, g] for s in range(per)], width)
            for c in range(per):
                out[base + c, :, :, h * lanes : (h + 1) * lanes] = exchanged[c]

    def one(f, _):
        tables = [(hi_ref[f, side], lo_ref[f, side]) for side in range(2)]
        grad_out[f, 0], grad_out[f, 1] = normal_frame(
            maps_out, field_out[f, 0], field_out[f, 1], tables
        )
        return 0

    lax.fori_loop(0, frames, one, 0)


def steps_kernel(field_ref, grad_ref, b0_ref, b1_ref, maps_ref, hi_ref, lo_ref, out_ref, field, grad):
    frames, _, cols, length = field_ref.shape
    devices, _, _, lanes = out_ref.shape
    data_term = jnp.concatenate([b0_ref[...], b1_ref[...]], 0)
    field[...] = tv_step(field_ref[...] - step_size * (grad_ref[...] - data_term))
    for sweep in range(1, OUTER):

        def one(f, _):
            tables = [(hi_ref[f, side], lo_ref[f, side]) for side in range(2)]
            grad[f, 0], grad[f, 1] = normal_frame(maps_ref, field[f, 0], field[f, 1], tables)
            return 0

        lax.fori_loop(0, frames, one, 0)
        field[...] = tv_step(field[...] - step_size * (grad[...] - data_term))
    per = frames
    for h in range(devices // per):
        parts = [field[f, :, :, h * lanes : (h + 1) * lanes] for f in range(per)]
        exchanged = lane_exchange(parts, lanes // per)
        for s in range(per):
            out_ref[h * per + s] = exchanged[s]


def rows_out_kernel(chunk_of, frames, got_ref, out_ref, tiles):
    devices, _, cols, lanes = got_ref.shape
    count = tiles.shape[0]
    rows = lanes // frames
    order = sorted(range(devices), key=lambda d: chunk_of[d])
    each = LANES // cols
    for t in range(count):
        at = t % (count // 2) * each
        turned = jnp.concatenate([got_ref[d, t // (count // 2)] for d in order[at : at + each]], 0).T
        for f in range(frames):
            tiles[t, pl.ds(f, rows, stride=frames), :] = turned[f * rows : (f + 1) * rows]
        out_ref[:, t * LANES : (t + 1) * LANES] = tiles[t]


def params(**more):
    return pltpu.CompilerParams(vmem_limit_bytes=VMEM_LIMIT, **more)


def cost(flops, moved):
    return pl.CostEstimate(flops=int(flops), bytes_accessed=int(moved), transcendentals=0)


def whole(shape):
    return pl.BlockSpec(shape, lambda *_: (0,) * len(shape))


def lane_tiles(rows, lanes):
    return [
        pl.BlockSpec((rows, LANES), lambda *_, t=t: (0, t), pipeline_mode=pl.Buffered(1))
        for t in range(lanes // LANES)
    ]


def f32(*shape):
    return jax.ShapeDtypeStruct(shape, jnp.float32)


def scatter_sum(keep, send, order, device):
    devices = lax.axis_size("coil")
    bits = len(order)
    rest = keep.shape[1:]
    lead = [2] * bits
    lead[order[0]] = 1
    route = lambda bit: [(i, i ^ (1 << bit)) for i in range(devices)]
    value = (keep + lax.ppermute(send, "coil", route(order[0]))).reshape(*lead, *rest)
    for bit in order[1:]:
        mine = (device >> bit) & 1
        keep = lax.dynamic_index_in_dim(value, mine, bit, keepdims=True)
        send = lax.dynamic_index_in_dim(value, 1 - mine, bit, keepdims=True)
        value = keep + lax.ppermute(send, "coil", route(bit))
    return value.reshape(rest)


def kernel_path(image, sens, kspace, mask):
    rows, frames, packed = image.shape
    coils = sens.shape[1]
    length, pairs, _ = kspace.shape
    half = packed // 2
    hl = length // 2
    devices = lax.axis_size("coil")
    device = lax.axis_index("coil")
    bits = devices.bit_length() - 1
    own = pairs // frames
    cols = half // devices
    per = LANES // rows
    groups = (coils + frames) // per
    chunk_of = [sum(((d >> b) & 1) << (bits - 1 - b) for b in range(bits)) for d in range(devices)]

    k = np.arange(length)
    z = np.arange(half)
    y = np.arange(hl)
    col_hi, col_lo = two_terms(packed_left(dft(z, z, half) / np.sqrt(half)))
    lanes_k = [k[0::2], k[1::2]]
    inverse = [packed_right(dft(y, ks, length)) for ks in lanes_k]
    row_hi, row_lo = two_terms(np.stack(inverse) / np.sqrt(length))
    forward = [packed_right(dft(ks, y, length).conj()) for ks in lanes_k]
    in_hi, in_lo = two_terms(np.stack(forward) / np.sqrt(hl))
    out_hi, out_lo = two_terms(np.stack(inverse) / np.sqrt(hl) * 0.5)

    sampled = mask.astype(jnp.float32)
    mask_even, mask_odd = sampled[:, 0::2], sampled[:, 1::2]
    mask_lanes = jnp.concatenate([mask_even, mask_odd], 1)[:, None, :]
    mask_packed = jnp.stack(
        [jnp.concatenate([mask_even] * 2, 1), jnp.concatenate([mask_odd] * 2, 1)], 1
    )

    sens_rows = sens.reshape(rows * coils, packed)
    image_rows = image.reshape(rows * frames, packed)

    with jax.named_scope("coil_maps"):
        blocks = pl.pallas_call(
            functools.partial(coil_blocks_kernel, coils),
            grid=(1,),
            out_shape=f32(devices, own, rows, packed),
            in_specs=lane_tiles(rows * coils, packed),
            out_specs=whole((devices, own, rows, packed)),
            compiler_params=params(),
            cost_estimate=cost(0, 2 * sens.size * 4),
        )(*[sens_rows] * (packed // LANES))
        coil_maps = lax.all_to_all(blocks, "coil", 0, 0, tiled=True)

    with jax.named_scope("column_maps"):
        blocks = pl.pallas_call(
            functools.partial(column_blocks_kernel, coils, frames, chunk_of),
            grid=(1,),
            out_shape=f32(devices, groups, 2, cols, LANES),
            in_specs=lane_tiles(rows * coils, packed) + lane_tiles(rows * frames, packed),
            out_specs=whole((devices, groups, 2, cols, LANES)),
            compiler_params=params(),
            cost_estimate=cost(0, 2 * (sens.size + image.size) * 4),
        )(*[sens_rows] * (packed // LANES), *[image_rows] * (packed // LANES))
        column_maps = lax.all_to_all(blocks, "coil", 0, 0, tiled=True)

    with jax.named_scope("mask_tables"):
        table = jax.ShapeDtypeStruct((frames, 2, length, length), jnp.bfloat16)
        block = pl.BlockSpec((1, 2, length, length), lambda f: (f, 0, 0, 0))
        table_hi, table_lo = pl.pallas_call(
            mask_tables_kernel,
            grid=(frames,),
            out_shape=(table, table),
            in_specs=[pl.BlockSpec((1, 2, length), lambda f: (f, 0, 0))]
            + [whole((2, length, length))] * 4,
            out_specs=(block, block),
            compiler_params=params(),
            cost_estimate=cost(2 * 3 * 2 * frames * length**3, frames * 8 * length**2),
        )(mask_packed, in_hi, in_lo, out_hi, out_lo)

    with jax.named_scope("data_transform"):
        base = pl.pallas_call(
            functools.partial(base_kernel, pairs),
            grid=(pairs,),
            out_shape=f32(pairs, 2, half, length),
            in_specs=lane_tiles(length * pairs, packed)
            + [
                pl.BlockSpec((1, 1, length), lambda p: (p % frames, 0, 0)),
                whole((packed, packed)),
                whole((packed, packed)),
                whole((2, length, length)),
                whole((2, length, length)),
            ],
            out_specs=pl.BlockSpec((1, 2, half, length), lambda p: (p, 0, 0, 0)),
            compiler_params=params(),
            cost_estimate=cost(pairs * 6 * 6 * half * half * length, 2 * kspace.size * 4),
        )(
            *[kspace.reshape(length * pairs, packed)] * (packed // LANES),
            mask_lanes,
            col_hi,
            col_lo,
            row_hi,
            row_lo,
        )
        base = base.reshape(own, frames, 2, half, length)

    with jax.named_scope("data_term"):
        bit = (device & 1).astype(jnp.int32)[None]
        streams = 2
        count = frames // streams
        orders = [list(range(bits)), [0] + list(range(2, bits)) + [1]]
        terms = []
        for stream in range(streams):
            start = stream * count
            out = f32(devices // 2, count, 2, cols, length)
            block = pl.BlockSpec((devices // 2, 1, 2, cols, length), lambda i: (0, i, 0, 0, 0))
            keep, send = pl.pallas_call(
                weigh_kernel,
                grid=(count,),
                out_shape=(out, out),
                in_specs=[
                    pl.BlockSpec(memory_space=pltpu.SMEM),
                    whole((devices, own, rows, packed)),
                    pl.BlockSpec(
                        (own, 1, 2, half, length), lambda i, start=start: (0, start + i, 0, 0, 0)
                    ),
                ],
                out_specs=(block, block),
                scratch_shapes=[pltpu.VMEM((own, 2, half, length), jnp.float32)],
                compiler_params=params(),
                cost_estimate=cost(0, base.size * 4 // 2 + 2 * out.size * 4),
            )(bit, coil_maps, base)
            terms.append(scatter_sum(keep, send, orders[stream], device))

    with jax.named_scope("first_gradient"):
        field = f32(frames, 2, cols, length)
        normal_cost = 6 * 2 * frames * coils * cols * length * length
        maps, field0, grad0 = pl.pallas_call(
            functools.partial(first_normal_kernel, coils),
            out_shape=(f32(coils, 2, cols, length), field, field),
            compiler_params=params(),
            cost_estimate=cost(normal_cost, 4 * sens.size * 4),
        )(column_maps, table_hi, table_lo)

    with jax.named_scope("outer_steps"):
        blocks = pl.pallas_call(
            steps_kernel,
            out_shape=f32(devices, 2, cols, LANES),
            scratch_shapes=[pltpu.VMEM(field.shape, jnp.float32)] * 2,
            compiler_params=params(),
            cost_estimate=cost(normal_cost, 4 * sens.size * 4),
        )(field0, grad0, terms[0], terms[1], maps, table_hi, table_lo)

    with jax.named_scope("result_rows"):
        got = lax.all_to_all(blocks, "coil", 0, 0, tiled=True)
        recon = pl.pallas_call(
            functools.partial(rows_out_kernel, chunk_of, frames),
            out_shape=f32(rows * frames, packed),
            scratch_shapes=[pltpu.VMEM((packed // LANES, rows * frames, LANES), jnp.float32)],
            compiler_params=params(),
            cost_estimate=cost(0, 2 * image.size * 4),
        )(got)
    return recon.reshape(rows, frames, packed)


def einsum(form, left, right):
    return jnp.einsum(form, left, right, precision=highest, preferred_element_type=jnp.float32)


def complex_einsum(form, left, right):
    (a, b), (c, d) = left, right
    return (
        einsum(form, a, c) - einsum(form, b, d),
        einsum(form, a, d) + einsum(form, b, c),
    )


def general_path(image, sens, kspace, mask):
    rows, frames, packed = image.shape
    coils = sens.shape[1]
    length, pairs, _ = kspace.shape
    half = packed // 2
    devices = lax.axis_size("coil")
    device = lax.axis_index("coil")
    cols = half // devices

    def table(size):
        values = dft(np.arange(size), np.arange(size), size) / np.sqrt(size)
        return jnp.asarray(values.real, jnp.float32), jnp.asarray(values.imag, jnp.float32)

    inverse_rows, inverse_cols = table(length), table(half)
    forward_rows = (inverse_rows[0], -inverse_rows[1])

    both = jnp.concatenate([sens, image], 1).reshape(rows, coils + frames, 2, devices, cols)
    both = lax.all_to_all(both.transpose(3, 1, 2, 4, 0), "coil", 0, 0, tiled=True)
    both = both.transpose(1, 2, 3, 0, 4).reshape(coils + frames, 2, cols, length)
    maps, field = both[:coils], both[coils:]

    own = max(1, pairs // frames)
    repeats = devices * own // coils
    spread = jnp.repeat(sens.reshape(rows, coils // own, own, packed), repeats, axis=1)
    spread = spread.transpose(1, 0, 2, 3)
    coil_maps = lax.all_to_all(spread, "coil", 0, 0, tiled=True).reshape(length, own, packed)

    ids = device * pairs + lax.iota(jnp.int32, pairs)
    onehot = (ids[:, None] % frames == lax.iota(jnp.int32, frames)[None, :]).astype(jnp.float32)
    sampled = mask.astype(jnp.float32)
    data = einsum("pf,fk->kp", onehot, sampled)[:, :, None] * kspace
    data = (data[..., :half], data[..., half:])
    data = complex_einsum("kpz,zx->kpx", data, inverse_cols)
    data = complex_einsum("yk,kpx->ypx", inverse_rows, data)
    pair_maps = jnp.repeat(coil_maps, pairs // own, axis=1)
    m_re, m_im = pair_maps[..., :half], pair_maps[..., half:]
    weighted = jnp.stack(
        [m_re * data[0] + m_im * data[1], m_re * data[1] - m_im * data[0]], 2
    ).reshape(length, pairs, 2, devices, cols)
    term = einsum("ypcdx,pf->dfcxy", weighted, onehot)
    term = lax.psum_scatter(term, "coil", scatter_dimension=0, tiled=True)[0]

    masked = (
        sampled[:, :, None] * forward_rows[0][None],
        sampled[:, :, None] * forward_rows[1][None],
    )
    project = complex_einsum("yk,fkv->fyv", inverse_rows, masked)
    for sweep in range(OUTER):
        u_re = maps[:, None, 0] * field[None, :, 0] - maps[:, None, 1] * field[None, :, 1]
        u_im = maps[:, None, 0] * field[None, :, 1] + maps[:, None, 1] * field[None, :, 0]
        v_re, v_im = complex_einsum("fyv,cfxv->cfxy", project, (u_re, u_im))
        grad = jnp.stack(
            [
                jnp.sum(maps[:, None, 0] * v_re + maps[:, None, 1] * v_im, 0),
                jnp.sum(maps[:, None, 0] * v_im - maps[:, None, 1] * v_re, 0),
            ],
            1,
        )
        target = field - step_size * (grad - term)
        dual_time = jnp.zeros_like(target)
        dual_rows = jnp.zeros_like(target)
        field = target
        for repeat in range(INNER):
            diff_time = jnp.concatenate([field[1:] - field[:-1], jnp.zeros_like(field[:1])], 0)
            diff_rows = jnp.concatenate(
                [field[..., 1:] - field[..., :-1], jnp.zeros_like(field[..., :1])], -1
            )
            dual_time = jnp.clip(dual_time + dual_step * diff_time, -1.0, 1.0)
            dual_rows = jnp.clip(dual_rows + dual_step * diff_rows, -1.0, 1.0)
            inner_time, inner_rows = dual_time[:-1], dual_rows[..., :-1]
            none_time, none_rows = jnp.zeros_like(field[:1]), jnp.zeros_like(field[..., :1])
            divergence = (
                jnp.concatenate([none_time, inner_time], 0)
                - jnp.concatenate([inner_time, none_time], 0)
                + jnp.concatenate([none_rows, inner_rows], -1)
                - jnp.concatenate([inner_rows, none_rows], -1)
            )
            field = target - tv_weight * divergence

    result = field.reshape(frames, 2, cols, devices, rows).transpose(3, 0, 1, 2, 4)
    result = lax.all_to_all(result, "coil", 0, 0, tiled=True)
    return result.transpose(4, 1, 2, 0, 3).reshape(rows, frames, packed)


def fits_kernels(image, sens, kspace, devices):
    rows, frames, packed = image.shape
    coils = sens.shape[1]
    length, pairs, _ = kspace.shape
    per = LANES // rows
    return (
        devices & (devices - 1) == 0
        and devices >= 4
        and rows % 8 == 0
        and rows * per == LANES
        and frames == per
        and frames % 2 == 0
        and coils % per == 0
        and devices % per == 0
        and pairs % frames == 0
        and pairs * devices == coils * frames
        and length == 2 * LANES
        and packed % (16 * devices) == 0
        and packed % (4 * LANES) == 0
    )


def per_device(image, sens, kspace, mask):
    if fits_kernels(image, sens, kspace, lax.axis_size("coil")):
        return kernel_path(image, sens, kspace, mask)
    return general_path(image, sens, kspace, mask)


def solution(mesh):
    return jax.shard_map(
        per_device,
        mesh=mesh,
        in_specs=(
            P(("plane", "coil"), None, None),
            P(("plane", "coil"), None, None),
            P("plane", "coil", None),
            P(),
        ),
        out_specs=P(("plane", "coil"), None, None),
        check_vma=False,
    )
```

```python
import functools

import jax
import jax.numpy as jnp
import ml_dtypes
import numpy as np
from jax import lax
from jax.experimental import pallas as pl
from jax.experimental.pallas import tpu as pltpu
from jax.sharding import PartitionSpec as P

OUTER = 2
INNER = 2
LANES = 128
VMEM_LIMIT = 48 * 1024 * 1024

step_size = 0.5
tv_weight = 0.1
dual_step = 1.25
highest = lax.Precision.HIGHEST


def two_terms(table):
    first = table.astype(ml_dtypes.bfloat16)
    second = (table - first.astype(np.float64)).astype(ml_dtypes.bfloat16)
    return first, second


def dft(out_index, in_index, length):
    product = np.outer(out_index, in_index) % length
    return np.exp(2j * np.pi / length * product)


def packed_left(matrix):
    return np.block([[matrix.real, -matrix.imag], [matrix.imag, matrix.real]])


def packed_right(matrix):
    return packed_left(matrix).T


def split(value):
    first = value.astype(jnp.bfloat16)
    second = (value - first.astype(jnp.float32)).astype(jnp.bfloat16)
    return first, second


def dot3(left, right, contract=((1,), (0,))):
    dims = (contract, ((), ()))

    def dot(a, b):
        return lax.dot_general(a, b, dims, preferred_element_type=jnp.float32)

    return dot(left[0], right[0]) + (dot(left[0], right[1]) + dot(left[1], right[0]))


def lane_exchange(parts, width):
    parts = list(parts)
    lane = lax.broadcasted_iota(jnp.int32, parts[0].shape, parts[0].ndim - 1)
    axis = parts[0].ndim - 1
    bit = 1
    while bit < len(parts):
        odd = (lane // width) & bit != 0
        for s in range(len(parts)):
            if s & bit:
                continue
            low, high = parts[s], parts[s | bit]
            parts[s] = jnp.where(odd, pltpu.roll(high, width * bit, axis), low)
            parts[s | bit] = jnp.where(odd, high, pltpu.roll(low, LANES - width * bit, axis))
        bit *= 2
    return parts


def roll_last(value, distance):
    shape = value.shape
    flat = value.reshape(-1, shape[-1])
    return pltpu.roll(flat, distance % shape[-1], 1).reshape(shape)


def tv_step(target):
    length = target.shape[-1]
    row = lax.broadcasted_iota(jnp.int32, target.shape, target.ndim - 1)
    last, first = row == length - 1, row == 0
    nothing = jnp.zeros_like(target[:1])

    def adjoint(dual_time, dual_rows):
        from_time = jnp.concatenate([nothing, dual_time[:-1]], 0) - jnp.concatenate(
            [dual_time[:-1], nothing], 0
        )
        from_rows = jnp.where(first, 0.0, roll_last(dual_rows, 1)) - jnp.where(last, 0.0, dual_rows)
        return from_time + from_rows

    dual_time = jnp.zeros_like(target)
    dual_rows = jnp.zeros_like(target)
    primal = target
    for repeat in range(INNER):
        diff_time = jnp.concatenate([primal[1:] - primal[:-1], nothing], 0)
        diff_rows = jnp.where(last, 0.0, roll_last(primal, -1) - primal)
        dual_time = jnp.clip(dual_time + dual_step * diff_time, -1.0, 1.0)
        dual_rows = jnp.clip(dual_rows + dual_step * diff_rows, -1.0, 1.0)
        primal = target - tv_weight * adjoint(dual_time, dual_rows)
    return primal


def normal_frame(maps_ref, field_re, field_im, tables):
    coils, _, cols, length = maps_ref.shape
    half = length // 2
    maps_re, maps_im = maps_ref[:, 0], maps_ref[:, 1]
    u_re = maps_re * field_re[None] - maps_im * field_im[None]
    u_im = maps_re * field_im[None] + maps_im * field_re[None]
    flat_re = u_re.reshape(coils * cols, length)
    flat_im = u_im.reshape(coils * cols, length)
    outs = []
    for sign, table in zip((1.0, -1.0), tables):
        packed = jnp.concatenate(
            [
                flat_re[:, :half] + sign * flat_re[:, half:],
                flat_im[:, :half] + sign * flat_im[:, half:],
            ],
            1,
        )
        outs.append(dot3(split(packed), table))
    plus, minus = outs
    v_re = jnp.concatenate(
        [plus[:, :half] + minus[:, :half], plus[:, :half] - minus[:, :half]], 1
    ).reshape(coils, cols, length)
    v_im = jnp.concatenate(
        [plus[:, half:] + minus[:, half:], plus[:, half:] - minus[:, half:]], 1
    ).reshape(coils, cols, length)
    return (
        jnp.sum(maps_re * v_re + maps_im * v_im, 0),
        jnp.sum(maps_re * v_im - maps_im * v_re, 0),
    )


def coil_blocks_kernel(coils, *refs):
    *tiles, out_ref = refs
    devices, own, rows, _ = out_ref.shape
    for d in range(devices):
        for c in range(own):
            for t, ref in enumerate(tiles):
                out_ref[d, c, :, t * LANES : (t + 1) * LANES] = ref[
                    pl.ds(d * own + c, rows, stride=coils), :
                ]


def column_blocks_kernel(coils, frames, chunk_of, *refs):
    *tiles, out_ref = refs
    sens_tiles, image_tiles = tiles[: len(tiles) // 2], tiles[len(tiles) // 2 :]
    devices, groups, _, cols, _ = out_ref.shape
    rows = sens_tiles[0].shape[0] // coils
    per = LANES // rows
    half = len(sens_tiles) // 2
    for g in range(groups):
        if g * per < coils:
            tiles, count, base = sens_tiles, coils, g * per
        else:
            tiles, count, base = image_tiles, frames, g * per - coils
        for t, ref in enumerate(tiles):
            turned = jnp.concatenate(
                [ref[pl.ds(base + c, rows, stride=count), :] for c in range(per)], 0
            ).T
            for d in range(devices):
                at = chunk_of[d] * cols - t % half * LANES
                if 0 <= at < LANES:
                    out_ref[d, g, t // half] = turned[at : at + cols]


def mask_tables_kernel(mask_ref, in_hi, in_lo, out_hi, out_lo, hi_ref, lo_ref):
    for side in range(2):
        row = mask_ref[0, side : side + 1, :].astype(jnp.bfloat16)
        left = (in_hi[side] * row, in_lo[side] * row)
        hi_ref[0, side], lo_ref[0, side] = split(dot3(left, (out_hi[side], out_lo[side])))


def base_kernel(kspace_ref, mask_ref, col_hi, col_lo, row_hi, row_lo, out_ref, data, arrived):
    own, _, _, half_cols, length = out_ref.shape
    half = length // 2
    frame, frames = pl.program_id(0), pl.num_programs(0)

    def fetch(f, slot):
        return [
            pltpu.make_async_copy(
                kspace_ref.at[:, odd, f + c * frames, :],
                data.at[slot, c, pl.ds(odd * half, half)],
                arrived.at[slot, c, odd],
            )
            for c in range(own)
            for odd in range(2)
        ]

    @pl.when(frame == 0)
    def _():
        for copy in fetch(0, 0):
            copy.start()

    @pl.when(frame + 1 < frames)
    def _():
        for copy in fetch(frame + 1, (frame + 1) % 2):
            copy.start()

    slot = frame % 2
    for copy in fetch(frame, slot):
        copy.wait()
    columns = [
        dot3((col_hi[...], col_lo[...]), split(data[slot, c]), ((1,), (1,))) * mask_ref[0]
        for c in range(own)
    ]
    sides = []
    for odd in range(2):
        at = odd * half
        stacked = jnp.concatenate(
            [
                jnp.concatenate([v[:half_cols, at : at + half], v[half_cols:, at : at + half]], 1)
                for v in columns
            ],
            0,
        )
        sides.append(dot3(split(stacked), (row_hi[odd], row_lo[odd])))
    for c in range(own):
        even, odd = [side[c * half_cols : (c + 1) * half_cols] for side in sides]
        for part in range(2):
            e = even[:, part * half : (part + 1) * half]
            o = odd[:, part * half : (part + 1) * half]
            out_ref[c, 0, part] = jnp.concatenate([e + o, e - o], 1)


def weigh_kernel(bit_ref, maps_ref, base_ref, keep_ref, send_ref, turned):
    devices, own, rows, packed = maps_ref.shape
    half_cols = packed // 2
    length = devices * rows

    @pl.when(pl.program_id(0) == 0)
    def _():
        for c in range(own):
            whole = maps_ref[:, c].reshape(length, packed).T
            turned[c, 0] = whole[:half_cols]
            turned[c, 1] = whole[half_cols:]

    bit = bit_ref[0]
    span = half_cols // 2
    blocks = devices // 2
    for ref, which in ((send_ref, 1 - bit), (keep_ref, bit)):
        at = pl.ds(pl.multiple_of(which * span, span), span)
        total_re = total_im = None
        for c in range(own):
            s_re, s_im = turned[c, 0, at, :], turned[c, 1, at, :]
            b_re, b_im = base_ref[c, 0, 0, at, :], base_ref[c, 0, 1, at, :]
            t_re = s_re * b_re + s_im * b_im
            t_im = s_re * b_im - s_im * b_re
            total_re = t_re if c == 0 else total_re + t_re
            total_im = t_im if c == 0 else total_im + t_im
        ref[:, 0, 0] = total_re.reshape(blocks, span // blocks, length)
        ref[:, 0, 1] = total_im.reshape(blocks, span // blocks, length)


def first_normal_kernel(coils, got_ref, hi_ref, lo_ref, maps_out, field_out, grad_out):
    devices, groups, _, cols, lanes = got_ref.shape
    frames = field_out.shape[0]
    per = (coils + frames) // groups
    width = lanes // per
    for g in range(groups):
        out, base = (maps_out, g * per) if g * per < coils else (field_out, g * per - coils)
        for h in range(devices // per):
            exchanged = lane_exchange([got_ref[h * per + s, g] for s in range(per)], width)
            for c in range(per):
                out[base + c, :, :, h * lanes : (h + 1) * lanes] = exchanged[c]

    def one(f, _):
        tables = [(hi_ref[f, side], lo_ref[f, side]) for side in range(2)]
        grad_out[f, 0], grad_out[f, 1] = normal_frame(
            maps_out, field_out[f, 0], field_out[f, 1], tables
        )
        return 0

    lax.fori_loop(0, frames, one, 0)


def steps_kernel(field_ref, grad_ref, b0_ref, b1_ref, maps_ref, hi_ref, lo_ref, out_ref, field, grad):
    frames, _, cols, length = field_ref.shape
    devices, _, _, lanes = out_ref.shape
    data_term = jnp.concatenate([b0_ref[...], b1_ref[...]], 0)
    field[...] = tv_step(field_ref[...] - step_size * (grad_ref[...] - data_term))
    for sweep in range(1, OUTER):

        def one(f, _):
            tables = [(hi_ref[f, side], lo_ref[f, side]) for side in range(2)]
            grad[f, 0], grad[f, 1] = normal_frame(maps_ref, field[f, 0], field[f, 1], tables)
            return 0

        lax.fori_loop(0, frames, one, 0)
        field[...] = tv_step(field[...] - step_size * (grad[...] - data_term))
    per = frames
    for h in range(devices // per):
        parts = [field[f, :, :, h * lanes : (h + 1) * lanes] for f in range(per)]
        exchanged = lane_exchange(parts, lanes // per)
        for s in range(per):
            out_ref[h * per + s] = exchanged[s]


def rows_out_kernel(chunk_of, frames, got_ref, out_ref, tiles):
    devices, _, cols, lanes = got_ref.shape
    count = tiles.shape[0]
    rows = lanes // frames
    order = sorted(range(devices), key=lambda d: chunk_of[d])
    each = LANES // cols
    for t in range(count):
        at = t % (count // 2) * each
        turned = jnp.concatenate([got_ref[d, t // (count // 2)] for d in order[at : at + each]], 0).T
        for f in range(frames):
            tiles[t, pl.ds(f, rows, stride=frames), :] = turned[f * rows : (f + 1) * rows]
        out_ref[:, t * LANES : (t + 1) * LANES] = tiles[t]


def params(**more):
    return pltpu.CompilerParams(vmem_limit_bytes=VMEM_LIMIT, **more)


def cost(flops, moved):
    return pl.CostEstimate(flops=int(flops), bytes_accessed=int(moved), transcendentals=0)


def whole(shape):
    return pl.BlockSpec(shape, lambda *_: (0,) * len(shape))


def lane_tiles(rows, lanes):
    return [
        pl.BlockSpec((rows, LANES), lambda *_, t=t: (0, t), pipeline_mode=pl.Buffered(1))
        for t in range(lanes // LANES)
    ]


def f32(*shape):
    return jax.ShapeDtypeStruct(shape, jnp.float32)


def scatter_sum(keep, send, order, device):
    devices = lax.axis_size("coil")
    bits = len(order)
    rest = keep.shape[1:]
    lead = [2] * bits
    lead[order[0]] = 1
    route = lambda bit: [(i, i ^ (1 << bit)) for i in range(devices)]
    value = (keep + lax.ppermute(send, "coil", route(order[0]))).reshape(*lead, *rest)
    for bit in order[1:]:
        mine = (device >> bit) & 1
        keep = lax.dynamic_index_in_dim(value, mine, bit, keepdims=True)
        send = lax.dynamic_index_in_dim(value, 1 - mine, bit, keepdims=True)
        value = keep + lax.ppermute(send, "coil", route(bit))
    return value.reshape(rest)


def kernel_path(image, sens, kspace, mask):
    rows, frames, packed = image.shape
    coils = sens.shape[1]
    length, pairs, _ = kspace.shape
    half = packed // 2
    hl = length // 2
    devices = lax.axis_size("coil")
    device = lax.axis_index("coil")
    bits = devices.bit_length() - 1
    own = pairs // frames
    cols = half // devices
    per = LANES // rows
    groups = (coils + frames) // per
    chunk_of = [sum(((d >> b) & 1) << (bits - 1 - b) for b in range(bits)) for d in range(devices)]

    k = np.arange(length)
    z = np.arange(half)
    y = np.arange(hl)
    col_hi, col_lo = two_terms(packed_left(dft(z, z, half) / np.sqrt(half)))
    lanes_k = [k[0::2], k[1::2]]
    inverse = [packed_right(dft(y, ks, length)) for ks in lanes_k]
    row_hi, row_lo = two_terms(np.stack(inverse) / np.sqrt(length))
    forward = [packed_right(dft(ks, y, length).conj()) for ks in lanes_k]
    in_hi, in_lo = two_terms(np.stack(forward) / np.sqrt(hl))
    out_hi, out_lo = two_terms(np.stack(inverse) / np.sqrt(hl) * 0.5)

    sampled = mask.astype(jnp.float32)
    mask_even, mask_odd = sampled[:, 0::2], sampled[:, 1::2]
    mask_lanes = jnp.concatenate([mask_even, mask_odd], 1)[:, None, :]
    mask_packed = jnp.stack(
        [jnp.concatenate([mask_even] * 2, 1), jnp.concatenate([mask_odd] * 2, 1)], 1
    )

    sens_rows = sens.reshape(rows * coils, packed)
    image_rows = image.reshape(rows * frames, packed)

    with jax.named_scope("coil_maps"):
        blocks = pl.pallas_call(
            functools.partial(coil_blocks_kernel, coils),
            grid=(1,),
            out_shape=f32(devices, own, rows, packed),
            in_specs=lane_tiles(rows * coils, packed),
            out_specs=whole((devices, own, rows, packed)),
            compiler_params=params(),
            cost_estimate=cost(0, 2 * sens.size * 4),
        )(*[sens_rows] * (packed // LANES))
        coil_maps = lax.all_to_all(blocks, "coil", 0, 0, tiled=True)

    with jax.named_scope("column_maps"):
        column_blocks = pl.pallas_call(
            functools.partial(column_blocks_kernel, coils, frames, chunk_of),
            grid=(1,),
            out_shape=f32(devices, groups, 2, cols, LANES),
            in_specs=lane_tiles(rows * coils, packed) + lane_tiles(rows * frames, packed),
            out_specs=whole((devices, groups, 2, cols, LANES)),
            compiler_params=params(),
            cost_estimate=cost(0, 2 * (sens.size + image.size) * 4),
        )(*[sens_rows] * (packed // LANES), *[image_rows] * (packed // LANES))

    with jax.named_scope("mask_tables"):
        table = jax.ShapeDtypeStruct((frames, 2, length, length), jnp.bfloat16)
        block = pl.BlockSpec((1, 2, length, length), lambda f: (f, 0, 0, 0))
        table_hi, table_lo = pl.pallas_call(
            mask_tables_kernel,
            grid=(frames,),
            out_shape=(table, table),
            in_specs=[pl.BlockSpec((1, 2, length), lambda f: (f, 0, 0))]
            + [whole((2, length, length))] * 4,
            out_specs=(block, block),
            compiler_params=params(),
            cost_estimate=cost(2 * 3 * 2 * frames * length**3, frames * 8 * length**2),
        )(mask_packed, in_hi, in_lo, out_hi, out_lo)

    with jax.named_scope("data_transform"):
        base = pl.pallas_call(
            base_kernel,
            grid=(frames,),
            out_shape=f32(own, frames, 2, half, length),
            in_specs=[
                pl.BlockSpec(memory_space=pl.ANY),
                pl.BlockSpec((1, 1, length), lambda f: (f, 0, 0)),
                whole((packed, packed)),
                whole((packed, packed)),
                whole((2, length, length)),
                whole((2, length, length)),
            ],
            out_specs=pl.BlockSpec((own, 1, 2, half, length), lambda f: (0, f, 0, 0, 0)),
            scratch_shapes=[
                pltpu.VMEM((2, own, length, packed), jnp.float32),
                pltpu.SemaphoreType.DMA((2, own, 2)),
            ],
            compiler_params=params(),
            cost_estimate=cost(pairs * 6 * 6 * half * half * length, 2 * kspace.size * 4),
        )(
            kspace.reshape(hl, 2, pairs, packed), mask_lanes, col_hi, col_lo, row_hi, row_lo
        )

    column_blocks, base, table_hi, table_lo = lax.optimization_barrier(
        (column_blocks, base, table_hi, table_lo)
    )
    with jax.named_scope("column_maps"):
        column_maps = lax.all_to_all(column_blocks, "coil", 0, 0, tiled=True)

    with jax.named_scope("data_term"):
        bit = (device & 1).astype(jnp.int32)[None]
        streams = 2
        count = frames // streams
        orders = [list(range(bits)), [0] + list(range(2, bits)) + [1]]
        terms = []
        for stream in range(streams):
            start = stream * count
            out = f32(devices // 2, count, 2, cols, length)
            block = pl.BlockSpec((devices // 2, 1, 2, cols, length), lambda i: (0, i, 0, 0, 0))
            keep, send = pl.pallas_call(
                weigh_kernel,
                grid=(count,),
                out_shape=(out, out),
                in_specs=[
                    pl.BlockSpec(memory_space=pltpu.SMEM),
                    whole((devices, own, rows, packed)),
                    pl.BlockSpec(
                        (own, 1, 2, half, length), lambda i, start=start: (0, start + i, 0, 0, 0)
                    ),
                ],
                out_specs=(block, block),
                scratch_shapes=[pltpu.VMEM((own, 2, half, length), jnp.float32)],
                compiler_params=params(),
                cost_estimate=cost(0, base.size * 4 // 2 + 2 * out.size * 4),
            )(bit, coil_maps, base)
            terms.append(scatter_sum(keep, send, orders[stream], device))

    with jax.named_scope("first_gradient"):
        field = f32(frames, 2, cols, length)
        normal_cost = 6 * 2 * frames * coils * cols * length * length
        maps, field0, grad0 = pl.pallas_call(
            functools.partial(first_normal_kernel, coils),
            out_shape=(f32(coils, 2, cols, length), field, field),
            compiler_params=params(),
            cost_estimate=cost(normal_cost, 4 * sens.size * 4),
        )(column_maps, table_hi, table_lo)

    with jax.named_scope("outer_steps"):
        blocks = pl.pallas_call(
            steps_kernel,
            out_shape=f32(devices, 2, cols, LANES),
            scratch_shapes=[pltpu.VMEM(field.shape, jnp.float32)] * 2,
            compiler_params=params(),
            cost_estimate=cost(normal_cost, 4 * sens.size * 4),
        )(field0, grad0, terms[0], terms[1], maps, table_hi, table_lo)

    with jax.named_scope("result_rows"):
        got = lax.all_to_all(blocks, "coil", 0, 0, tiled=True)
        recon = pl.pallas_call(
            functools.partial(rows_out_kernel, chunk_of, frames),
            out_shape=f32(rows * frames, packed),
            scratch_shapes=[pltpu.VMEM((packed // LANES, rows * frames, LANES), jnp.float32)],
            compiler_params=params(),
            cost_estimate=cost(0, 2 * image.size * 4),
        )(got)
    return recon.reshape(rows, frames, packed)


def einsum(form, left, right):
    return jnp.einsum(form, left, right, precision=highest, preferred_element_type=jnp.float32)


def complex_einsum(form, left, right):
    (a, b), (c, d) = left, right
    return (
        einsum(form, a, c) - einsum(form, b, d),
        einsum(form, a, d) + einsum(form, b, c),
    )


def general_path(image, sens, kspace, mask):
    rows, frames, packed = image.shape
    coils = sens.shape[1]
    length, pairs, _ = kspace.shape
    half = packed // 2
    devices = lax.axis_size("coil")
    device = lax.axis_index("coil")
    cols = half // devices

    def table(size):
        values = dft(np.arange(size), np.arange(size), size) / np.sqrt(size)
        return jnp.asarray(values.real, jnp.float32), jnp.asarray(values.imag, jnp.float32)

    inverse_rows, inverse_cols = table(length), table(half)
    forward_rows = (inverse_rows[0], -inverse_rows[1])

    both = jnp.concatenate([sens, image], 1).reshape(rows, coils + frames, 2, devices, cols)
    both = lax.all_to_all(both.transpose(3, 1, 2, 4, 0), "coil", 0, 0, tiled=True)
    both = both.transpose(1, 2, 3, 0, 4).reshape(coils + frames, 2, cols, length)
    maps, field = both[:coils], both[coils:]

    own = max(1, pairs // frames)
    repeats = devices * own // coils
    spread = jnp.repeat(sens.reshape(rows, coils // own, own, packed), repeats, axis=1)
    spread = spread.transpose(1, 0, 2, 3)
    coil_maps = lax.all_to_all(spread, "coil", 0, 0, tiled=True).reshape(length, own, packed)

    ids = device * pairs + lax.iota(jnp.int32, pairs)
    onehot = (ids[:, None] % frames == lax.iota(jnp.int32, frames)[None, :]).astype(jnp.float32)
    sampled = mask.astype(jnp.float32)
    data = einsum("pf,fk->kp", onehot, sampled)[:, :, None] * kspace
    data = (data[..., :half], data[..., half:])
    data = complex_einsum("kpz,zx->kpx", data, inverse_cols)
    data = complex_einsum("yk,kpx->ypx", inverse_rows, data)
    pair_maps = jnp.repeat(coil_maps, pairs // own, axis=1)
    m_re, m_im = pair_maps[..., :half], pair_maps[..., half:]
    weighted = jnp.stack(
        [m_re * data[0] + m_im * data[1], m_re * data[1] - m_im * data[0]], 2
    ).reshape(length, pairs, 2, devices, cols)
    term = einsum("ypcdx,pf->dfcxy", weighted, onehot)
    term = lax.psum_scatter(term, "coil", scatter_dimension=0, tiled=True)[0]

    masked = (
        sampled[:, :, None] * forward_rows[0][None],
        sampled[:, :, None] * forward_rows[1][None],
    )
    project = complex_einsum("yk,fkv->fyv", inverse_rows, masked)
    for sweep in range(OUTER):
        u_re = maps[:, None, 0] * field[None, :, 0] - maps[:, None, 1] * field[None, :, 1]
        u_im = maps[:, None, 0] * field[None, :, 1] + maps[:, None, 1] * field[None, :, 0]
        v_re, v_im = complex_einsum("fyv,cfxv->cfxy", project, (u_re, u_im))
        grad = jnp.stack(
            [
                jnp.sum(maps[:, None, 0] * v_re + maps[:, None, 1] * v_im, 0),
                jnp.sum(maps[:, None, 0] * v_im - maps[:, None, 1] * v_re, 0),
            ],
            1,
        )
        target = field - step_size * (grad - term)
        dual_time = jnp.zeros_like(target)
        dual_rows = jnp.zeros_like(target)
        field = target
        for repeat in range(INNER):
            diff_time = jnp.concatenate([field[1:] - field[:-1], jnp.zeros_like(field[:1])], 0)
            diff_rows = jnp.concatenate(
                [field[..., 1:] - field[..., :-1], jnp.zeros_like(field[..., :1])], -1
            )
            dual_time = jnp.clip(dual_time + dual_step * diff_time, -1.0, 1.0)
            dual_rows = jnp.clip(dual_rows + dual_step * diff_rows, -1.0, 1.0)
            inner_time, inner_rows = dual_time[:-1], dual_rows[..., :-1]
            none_time, none_rows = jnp.zeros_like(field[:1]), jnp.zeros_like(field[..., :1])
            divergence = (
                jnp.concatenate([none_time, inner_time], 0)
                - jnp.concatenate([inner_time, none_time], 0)
                + jnp.concatenate([none_rows, inner_rows], -1)
                - jnp.concatenate([inner_rows, none_rows], -1)
            )
            field = target - tv_weight * divergence

    result = field.reshape(frames, 2, cols, devices, rows).transpose(3, 0, 1, 2, 4)
    result = lax.all_to_all(result, "coil", 0, 0, tiled=True)
    return result.transpose(4, 1, 2, 0, 3).reshape(rows, frames, packed)


def fits_kernels(image, sens, kspace, devices):
    rows, frames, packed = image.shape
    coils = sens.shape[1]
    length, pairs, _ = kspace.shape
    per = LANES // rows
    return (
        devices & (devices - 1) == 0
        and devices >= 4
        and rows % 8 == 0
        and rows * per == LANES
        and frames == per
        and frames % 2 == 0
        and coils % per == 0
        and devices % per == 0
        and pairs % frames == 0
        and pairs * devices == coils * frames
        and length == 2 * LANES
        and packed % (16 * devices) == 0
        and packed % (4 * LANES) == 0
    )


def per_device(image, sens, kspace, mask):
    if fits_kernels(image, sens, kspace, lax.axis_size("coil")):
        return kernel_path(image, sens, kspace, mask)
    return general_path(image, sens, kspace, mask)


def solution(mesh):
    return jax.shard_map(
        per_device,
        mesh=mesh,
        in_specs=(
            P(("plane", "coil"), None, None),
            P(("plane", "coil"), None, None),
            P("plane", "coil", None),
            P(),
        ),
        out_specs=P(("plane", "coil"), None, None),
        check_vma=False,
    )
```

```python
import functools

import jax
import jax.numpy as jnp
import ml_dtypes
import numpy as np
from jax import lax
from jax.experimental import pallas as pl
from jax.experimental.pallas import tpu as pltpu
from jax.sharding import PartitionSpec as P

OUTER = 2
INNER = 2
LANES = 128
VMEM_LIMIT = 16 * 1024 * 1024
TRANSFORM_LIMIT = 52 * 1024 * 1024

step_size = 0.5
tv_weight = 0.1
dual_step = 1.25
highest = lax.Precision.HIGHEST


def two_terms(table):
    first = table.astype(ml_dtypes.bfloat16)
    second = (table - first.astype(np.float64)).astype(ml_dtypes.bfloat16)
    return first, second


def dft(out_index, in_index, length):
    product = np.outer(out_index, in_index) % length
    return np.exp(2j * np.pi / length * product)


def packed_left(matrix):
    return np.block([[matrix.real, -matrix.imag], [matrix.imag, matrix.real]])


def packed_right(matrix):
    return packed_left(matrix).T


def split(value):
    first = value.astype(jnp.bfloat16)
    second = (value - first.astype(jnp.float32)).astype(jnp.bfloat16)
    return first, second


def dot3(left, right, contract=((1,), (0,))):
    dims = (contract, ((), ()))

    def dot(a, b):
        return lax.dot_general(a, b, dims, preferred_element_type=jnp.float32)

    return dot(left[0], right[0]) + (dot(left[0], right[1]) + dot(left[1], right[0]))


def lane_exchange(parts, width):
    parts = list(parts)
    lane = lax.broadcasted_iota(jnp.int32, parts[0].shape, parts[0].ndim - 1)
    axis = parts[0].ndim - 1
    bit = 1
    while bit < len(parts):
        odd = (lane // width) & bit != 0
        for s in range(len(parts)):
            if s & bit:
                continue
            low, high = parts[s], parts[s | bit]
            parts[s] = jnp.where(odd, pltpu.roll(high, width * bit, axis), low)
            parts[s | bit] = jnp.where(odd, high, pltpu.roll(low, LANES - width * bit, axis))
        bit *= 2
    return parts


def roll_last(value, distance):
    shape = value.shape
    flat = value.reshape(-1, shape[-1])
    return pltpu.roll(flat, distance % shape[-1], 1).reshape(shape)


def tv_step(target):
    length = target.shape[-1]
    row = lax.broadcasted_iota(jnp.int32, target.shape, target.ndim - 1)
    last, first = row == length - 1, row == 0
    nothing = jnp.zeros_like(target[:1])

    def adjoint(dual_time, dual_rows):
        from_time = jnp.concatenate([nothing, dual_time[:-1]], 0) - jnp.concatenate(
            [dual_time[:-1], nothing], 0
        )
        from_rows = jnp.where(first, 0.0, roll_last(dual_rows, 1)) - jnp.where(last, 0.0, dual_rows)
        return from_time + from_rows

    dual_time = jnp.zeros_like(target)
    dual_rows = jnp.zeros_like(target)
    primal = target
    for repeat in range(INNER):
        diff_time = jnp.concatenate([primal[1:] - primal[:-1], nothing], 0)
        diff_rows = jnp.where(last, 0.0, roll_last(primal, -1) - primal)
        dual_time = jnp.clip(dual_time + dual_step * diff_time, -1.0, 1.0)
        dual_rows = jnp.clip(dual_rows + dual_step * diff_rows, -1.0, 1.0)
        primal = target - tv_weight * adjoint(dual_time, dual_rows)
    return primal


def mask_responses(mask_ref, wave_hi, wave_lo, out_ref):
    for side in range(2):
        mask = mask_ref[side].astype(jnp.bfloat16)
        terms = [
            jnp.dot(mask, wave[side], preferred_element_type=jnp.float32)
            for wave in (wave_hi, wave_lo)
        ]
        out_ref[side] = terms[0] + terms[1]


def frame_tables(response_ref, f):
    half = response_ref.shape[-1] // 2
    tables = []
    for side in range(2):
        row = response_ref[side, pl.ds(f, 1), :]
        parts = []
        for at in (0, half):
            spread = jnp.broadcast_to(row[:, at : at + half], (half, half))
            turned = pltpu.roll(spread, 0, 1, stride=1, stride_axis=0)
            if side:
                before = lax.broadcasted_iota(jnp.int32, (half, half), 1) < (
                    lax.broadcasted_iota(jnp.int32, (half, half), 0)
                )
                turned = jnp.where(before, -turned, turned)
            parts.append(turned)
        re, im = parts
        tables.append(
            split(jnp.concatenate([jnp.concatenate([re, im], 1), jnp.concatenate([-im, re], 1)], 0))
        )
    return tables


def normal_frame(maps_ref, field_re, field_im, tables):
    coils, _, cols, length = maps_ref.shape
    half = length // 2
    maps_re, maps_im = maps_ref[:, 0], maps_ref[:, 1]
    u_re = maps_re * field_re[None] - maps_im * field_im[None]
    u_im = maps_re * field_im[None] + maps_im * field_re[None]
    flat_re = u_re.reshape(coils * cols, length)
    flat_im = u_im.reshape(coils * cols, length)
    outs = []
    for sign, table in zip((1.0, -1.0), tables):
        packed = jnp.concatenate(
            [
                flat_re[:, :half] + sign * flat_re[:, half:],
                flat_im[:, :half] + sign * flat_im[:, half:],
            ],
            1,
        )
        outs.append(dot3(split(packed), table))
    plus, minus = outs
    v_re = jnp.concatenate(
        [plus[:, :half] + minus[:, :half], plus[:, :half] - minus[:, :half]], 1
    ).reshape(coils, cols, length)
    v_im = jnp.concatenate(
        [plus[:, half:] + minus[:, half:], plus[:, half:] - minus[:, half:]], 1
    ).reshape(coils, cols, length)
    return (
        jnp.sum(maps_re * v_re + maps_im * v_im, 0),
        jnp.sum(maps_re * v_im - maps_im * v_re, 0),
    )


def coil_blocks_kernel(coils, *refs):
    *tiles, out_ref = refs
    devices, own, rows, _ = out_ref.shape
    for d in range(devices):
        for c in range(own):
            for t, ref in enumerate(tiles):
                out_ref[d, c, :, t * LANES : (t + 1) * LANES] = ref[
                    pl.ds(d * own + c, rows, stride=coils), :
                ]


def column_blocks_kernel(coils, frames, chunk_of, *refs):
    *tiles, out_ref = refs
    sens_tiles, image_tiles = tiles[: len(tiles) // 2], tiles[len(tiles) // 2 :]
    devices, groups, _, cols, _ = out_ref.shape
    rows = sens_tiles[0].shape[0] // coils
    per = LANES // rows
    half = len(sens_tiles) // 2
    for g in range(groups):
        if g * per < coils:
            tiles, count, base = sens_tiles, coils, g * per
        else:
            tiles, count, base = image_tiles, frames, g * per - coils
        for t, ref in enumerate(tiles):
            turned = jnp.concatenate(
                [ref[pl.ds(base + c, rows, stride=count), :] for c in range(per)], 0
            ).T
            for d in range(devices):
                at = chunk_of[d] * cols - t % half * LANES
                if 0 <= at < LANES:
                    out_ref[d, g, t // half] = turned[at : at + cols]


def base_kernel(
    start, frames, kspace_ref, mask_ref, col_hi, col_lo, row_hi, row_lo, out_ref, data, arrived
):
    own, _, _, half_cols, length = out_ref.shape
    half = length // 2
    frame = pl.program_id(0)

    def fetch(f, slot):
        return [
            pltpu.make_async_copy(
                kspace_ref.at[:, odd, start + f + c * frames, :],
                data.at[slot, c, pl.ds(odd * half, half)],
                arrived.at[slot, c, odd],
            )
            for c in range(own)
            for odd in range(2)
        ]

    @pl.when(frame == 0)
    def _():
        for copy in fetch(0, 0):
            copy.start()

    @pl.when(frame + 1 < pl.num_programs(0))
    def _():
        for copy in fetch(frame + 1, (frame + 1) % 2):
            copy.start()

    slot = frame % 2
    for copy in fetch(frame, slot):
        copy.wait()
    columns = [
        dot3((col_hi[...], col_lo[...]), split(data[slot, c]), ((1,), (1,))) * mask_ref[0]
        for c in range(own)
    ]
    sides = []
    for odd in range(2):
        at = odd * half
        stacked = jnp.concatenate(
            [
                jnp.concatenate([v[:half_cols, at : at + half], v[half_cols:, at : at + half]], 1)
                for v in columns
            ],
            0,
        )
        sides.append(dot3(split(stacked), (row_hi[odd], row_lo[odd])))
    for c in range(own):
        even, odd = [side[c * half_cols : (c + 1) * half_cols] for side in sides]
        for part in range(2):
            e = even[:, part * half : (part + 1) * half]
            o = odd[:, part * half : (part + 1) * half]
            out_ref[c, 0, part] = jnp.concatenate([e + o, e - o], 1)


def weigh_kernel(bit_ref, maps_ref, base_ref, keep_ref, send_ref, turned):
    devices, own, rows, packed = maps_ref.shape
    half_cols = packed // 2
    length = devices * rows

    @pl.when(pl.program_id(0) == 0)
    def _():
        for c in range(own):
            whole = maps_ref[:, c].reshape(length, packed).T
            turned[c, 0] = whole[:half_cols]
            turned[c, 1] = whole[half_cols:]

    bit = bit_ref[0]
    span = half_cols // 2
    blocks = devices // 2
    for ref, which in ((send_ref, 1 - bit), (keep_ref, bit)):
        at = pl.ds(pl.multiple_of(which * span, span), span)
        total_re = total_im = None
        for c in range(own):
            s_re, s_im = turned[c, 0, at, :], turned[c, 1, at, :]
            b_re, b_im = base_ref[c, 0, 0, at, :], base_ref[c, 0, 1, at, :]
            t_re = s_re * b_re + s_im * b_im
            t_im = s_re * b_im - s_im * b_re
            total_re = t_re if c == 0 else total_re + t_re
            total_im = t_im if c == 0 else total_im + t_im
        ref[:, 0, 0] = total_re.reshape(blocks, span // blocks, length)
        ref[:, 0, 1] = total_im.reshape(blocks, span // blocks, length)


def first_normal_kernel(
    coils, got_ref, mask_ref, wave_hi, wave_lo, maps_out, field_out, grad_out, responses
):
    mask_responses(mask_ref, wave_hi, wave_lo, responses)
    devices, groups, _, cols, lanes = got_ref.shape
    frames = field_out.shape[0]
    per = (coils + frames) // groups
    width = lanes // per
    for g in range(groups):
        out, base = (maps_out, g * per) if g * per < coils else (field_out, g * per - coils)
        for h in range(devices // per):
            exchanged = lane_exchange([got_ref[h * per + s, g] for s in range(per)], width)
            for c in range(per):
                out[base + c, :, :, h * lanes : (h + 1) * lanes] = exchanged[c]

    def one(f, _):
        grad_out[f, 0], grad_out[f, 1] = normal_frame(
            maps_out, field_out[f, 0], field_out[f, 1], frame_tables(responses, f)
        )
        return 0

    lax.fori_loop(0, frames, one, 0)


def steps_kernel(field_ref, grad_ref, b0_ref, b1_ref, maps_ref, mask_ref, *refs):
    wave_hi, wave_lo, out_ref, field, grad, responses = refs
    frames, _, cols, length = field_ref.shape
    devices, _, _, lanes = out_ref.shape
    mask_responses(mask_ref, wave_hi, wave_lo, responses)
    data_term = jnp.concatenate([b0_ref[...], b1_ref[...]], 0)
    field[...] = tv_step(field_ref[...] - step_size * (grad_ref[...] - data_term))
    for sweep in range(1, OUTER):

        def one(f, _):
            grad[f, 0], grad[f, 1] = normal_frame(
                maps_ref, field[f, 0], field[f, 1], frame_tables(responses, f)
            )
            return 0

        lax.fori_loop(0, frames, one, 0)
        field[...] = tv_step(field[...] - step_size * (grad[...] - data_term))
    per = frames
    for h in range(devices // per):
        parts = [field[f, :, :, h * lanes : (h + 1) * lanes] for f in range(per)]
        exchanged = lane_exchange(parts, lanes // per)
        for s in range(per):
            out_ref[h * per + s] = exchanged[s]


def rows_out_kernel(chunk_of, frames, got_ref, out_ref, tiles):
    devices, _, cols, lanes = got_ref.shape
    count = tiles.shape[0]
    rows = lanes // frames
    order = sorted(range(devices), key=lambda d: chunk_of[d])
    each = LANES // cols
    for t in range(count):
        at = t % (count // 2) * each
        turned = jnp.concatenate([got_ref[d, t // (count // 2)] for d in order[at : at + each]], 0).T
        for f in range(frames):
            tiles[t, pl.ds(f, rows, stride=frames), :] = turned[f * rows : (f + 1) * rows]
        out_ref[:, t * LANES : (t + 1) * LANES] = tiles[t]


def params(limit=VMEM_LIMIT):
    return pltpu.CompilerParams(vmem_limit_bytes=limit)


def cost(flops, moved):
    return pl.CostEstimate(flops=int(flops), bytes_accessed=int(moved), transcendentals=0)


def whole(shape):
    return pl.BlockSpec(shape, lambda *_: (0,) * len(shape))


def lane_tiles(rows, lanes):
    return [
        pl.BlockSpec((rows, LANES), lambda *_, t=t: (0, t), pipeline_mode=pl.Buffered(1))
        for t in range(lanes // LANES)
    ]


def f32(*shape):
    return jax.ShapeDtypeStruct(shape, jnp.float32)


def exchange(send, bit):
    devices = lax.axis_size("coil")
    return lax.ppermute(send, "coil", [(i, i ^ (1 << bit)) for i in range(devices)])


def halve(keep, got, bit, device):
    mine = (device >> bit) & 1

    def part(which):
        return lax.dynamic_index_in_dim(
            keep, which, bit, keepdims=True
        ) + lax.dynamic_index_in_dim(got, which, bit, keepdims=True)

    send = part(1 - mine)
    return part(mine), send


def kernel_path(image, sens, kspace, mask):
    rows, frames, packed = image.shape
    coils = sens.shape[1]
    length, pairs, _ = kspace.shape
    half = packed // 2
    hl = length // 2
    devices = lax.axis_size("coil")
    device = lax.axis_index("coil")
    bits = devices.bit_length() - 1
    own = pairs // frames
    cols = half // devices
    per = LANES // rows
    groups = (coils + frames) // per
    chunk_of = [sum(((d >> b) & 1) << (bits - 1 - b) for b in range(bits)) for d in range(devices)]

    k = np.arange(length)
    z = np.arange(half)
    y = np.arange(hl)
    col_hi, col_lo = two_terms(packed_left(dft(z, z, half) / np.sqrt(half)))
    lanes_k = [k[0::2], k[1::2]]
    inverse = [packed_right(dft(y, ks, length)) for ks in lanes_k]
    row_hi, row_lo = two_terms(np.stack(inverse) / np.sqrt(length))
    waves = [dft(ks, y, length) * 0.5 / hl for ks in lanes_k]
    wave_hi, wave_lo = two_terms(np.stack([np.concatenate([w.real, w.imag], 1) for w in waves]))

    sampled = mask.astype(jnp.float32)
    mask_sides = jnp.stack([sampled[:, 0::2], sampled[:, 1::2]])
    mask_lanes = jnp.concatenate([mask_sides[0], mask_sides[1]], 1)[:, None, :]

    sens_rows = sens.reshape(rows * coils, packed)
    image_rows = image.reshape(rows * frames, packed)

    with jax.named_scope("coil_maps"):
        blocks = pl.pallas_call(
            functools.partial(coil_blocks_kernel, coils),
            grid=(1,),
            out_shape=f32(devices, own, rows, packed),
            in_specs=lane_tiles(rows * coils, packed),
            out_specs=whole((devices, own, rows, packed)),
            compiler_params=params(),
            cost_estimate=cost(0, 2 * sens.size * 4),
        )(*[sens_rows] * (packed // LANES))
        coil_maps = lax.all_to_all(blocks, "coil", 0, 0, tiled=True)

    with jax.named_scope("column_maps"):
        column_blocks = pl.pallas_call(
            functools.partial(column_blocks_kernel, coils, frames, chunk_of),
            grid=(1,),
            out_shape=f32(devices, groups, 2, cols, LANES),
            in_specs=lane_tiles(rows * coils, packed) + lane_tiles(rows * frames, packed),
            out_specs=whole((devices, groups, 2, cols, LANES)),
            compiler_params=params(),
            cost_estimate=cost(0, 2 * (sens.size + image.size) * 4),
        )(*[sens_rows] * (packed // LANES), *[image_rows] * (packed // LANES))

    streams = 2
    count = frames // streams
    with jax.named_scope("data_transform"):
        bases = [
            pl.pallas_call(
                functools.partial(base_kernel, start, frames),
                grid=(count,),
                out_shape=f32(own, count, 2, half, length),
                in_specs=[
                    pl.BlockSpec(memory_space=pl.ANY),
                    pl.BlockSpec((1, 1, length), lambda f, start=start: (start + f, 0, 0)),
                    whole((packed, packed)),
                    whole((packed, packed)),
                    whole((2, length, length)),
                    whole((2, length, length)),
                ],
                out_specs=pl.BlockSpec((own, 1, 2, half, length), lambda f: (0, f, 0, 0, 0)),
                scratch_shapes=[
                    pltpu.VMEM((2, own, length, packed), jnp.float32),
                    pltpu.SemaphoreType.DMA((2, own, 2)),
                ],
                compiler_params=params(TRANSFORM_LIMIT),
                cost_estimate=cost(
                    pairs * 6 * 6 * half * half * length // streams, 2 * kspace.size * 4 // streams
                ),
            )(kspace.reshape(hl, 2, pairs, packed), mask_lanes, col_hi, col_lo, row_hi, row_lo)
            for start in range(0, frames, count)
        ]

    field = f32(frames, 2, cols, length)
    normal_cost = 6 * 2 * frames * coils * cols * length * length

    responses = pltpu.VMEM((2, frames, length), jnp.float32)

    def first_gradient(column_maps):
        return pl.pallas_call(
            functools.partial(first_normal_kernel, coils),
            out_shape=(f32(coils, 2, cols, length), field, field),
            scratch_shapes=[responses],
            compiler_params=params(),
            cost_estimate=cost(normal_cost, 4 * sens.size * 4),
            name="first_gradient",
        )(column_maps, mask_sides, wave_hi, wave_lo)

    column_blocks, bases = lax.optimization_barrier((column_blocks, bases))
    with jax.named_scope("column_maps"):
        column_maps = lax.all_to_all(column_blocks, "coil", 0, 0, tiled=True)

    with jax.named_scope("data_term"):
        bit = (device & 1).astype(jnp.int32)[None]
        orders = [list(range(bits)), [0] + list(range(2, bits)) + [1]]
        terms = []
        for stream in range(streams):
            out = f32(devices // 2, count, 2, cols, length)
            block = pl.BlockSpec((devices // 2, 1, 2, cols, length), lambda i: (0, i, 0, 0, 0))
            keep, send = pl.pallas_call(
                weigh_kernel,
                grid=(count,),
                out_shape=(out, out),
                in_specs=[
                    pl.BlockSpec(memory_space=pltpu.SMEM),
                    whole((devices, own, rows, packed)),
                    pl.BlockSpec((own, 1, 2, half, length), lambda i: (0, i, 0, 0, 0)),
                ],
                out_specs=(block, block),
                scratch_shapes=[pltpu.VMEM((own, 2, half, length), jnp.float32)],
                compiler_params=params(),
                cost_estimate=cost(0, bases[stream].size * 4 + 2 * out.size * 4),
            )(bit, coil_maps, bases[stream])
            lead = [1] + [2] * (bits - 1)
            got = exchange(send, 0).reshape(*lead, *keep.shape[1:])
            terms.append((keep.reshape(got.shape), got))
        for step in range(1, bits):
            halves = [halve(*terms[i], orders[i][step], device) for i in range(streams)]
            if step == 2:
                column_maps, halves = lax.optimization_barrier((column_maps, halves))
            terms = [
                (keep, exchange(send, orders[i][step])) for i, (keep, send) in enumerate(halves)
            ]
            if step == 2:
                maps, field0, grad0 = first_gradient(column_maps)
                terms, grad0 = lax.optimization_barrier((terms, grad0))
        terms = [(keep + got).reshape(count, 2, cols, length) for keep, got in terms]

    with jax.named_scope("outer_steps"):
        blocks = pl.pallas_call(
            steps_kernel,
            out_shape=f32(devices, 2, cols, LANES),
            scratch_shapes=[pltpu.VMEM(field.shape, jnp.float32)] * 2 + [responses],
            compiler_params=params(),
            cost_estimate=cost(normal_cost, 4 * sens.size * 4),
        )(field0, grad0, terms[0], terms[1], maps, mask_sides, wave_hi, wave_lo)

    with jax.named_scope("result_rows"):
        got = lax.all_to_all(blocks, "coil", 0, 0, tiled=True)
        recon = pl.pallas_call(
            functools.partial(rows_out_kernel, chunk_of, frames),
            out_shape=f32(rows * frames, packed),
            scratch_shapes=[pltpu.VMEM((packed // LANES, rows * frames, LANES), jnp.float32)],
            compiler_params=params(),
            cost_estimate=cost(0, 2 * image.size * 4),
        )(got)
    return recon.reshape(rows, frames, packed)


def einsum(form, left, right):
    return jnp.einsum(form, left, right, precision=highest, preferred_element_type=jnp.float32)


def complex_einsum(form, left, right):
    (a, b), (c, d) = left, right
    return (
        einsum(form, a, c) - einsum(form, b, d),
        einsum(form, a, d) + einsum(form, b, c),
    )


def general_path(image, sens, kspace, mask):
    rows, frames, packed = image.shape
    coils = sens.shape[1]
    length, pairs, _ = kspace.shape
    half = packed // 2
    devices = lax.axis_size("coil")
    device = lax.axis_index("coil")
    cols = half // devices

    def table(size):
        values = dft(np.arange(size), np.arange(size), size) / np.sqrt(size)
        return jnp.asarray(values.real, jnp.float32), jnp.asarray(values.imag, jnp.float32)

    inverse_rows, inverse_cols = table(length), table(half)
    forward_rows = (inverse_rows[0], -inverse_rows[1])

    both = jnp.concatenate([sens, image], 1).reshape(rows, coils + frames, 2, devices, cols)
    both = lax.all_to_all(both.transpose(3, 1, 2, 4, 0), "coil", 0, 0, tiled=True)
    both = both.transpose(1, 2, 3, 0, 4).reshape(coils + frames, 2, cols, length)
    maps, field = both[:coils], both[coils:]

    own = max(1, pairs // frames)
    repeats = devices * own // coils
    spread = jnp.repeat(sens.reshape(rows, coils // own, own, packed), repeats, axis=1)
    spread = spread.transpose(1, 0, 2, 3)
    coil_maps = lax.all_to_all(spread, "coil", 0, 0, tiled=True).reshape(length, own, packed)

    ids = device * pairs + lax.iota(jnp.int32, pairs)
    onehot = (ids[:, None] % frames == lax.iota(jnp.int32, frames)[None, :]).astype(jnp.float32)
    sampled = mask.astype(jnp.float32)
    data = einsum("pf,fk->kp", onehot, sampled)[:, :, None] * kspace
    data = (data[..., :half], data[..., half:])
    data = complex_einsum("kpz,zx->kpx", data, inverse_cols)
    data = complex_einsum("yk,kpx->ypx", inverse_rows, data)
    pair_maps = jnp.repeat(coil_maps, pairs // own, axis=1)
    m_re, m_im = pair_maps[..., :half], pair_maps[..., half:]
    weighted = jnp.stack(
        [m_re * data[0] + m_im * data[1], m_re * data[1] - m_im * data[0]], 2
    ).reshape(length, pairs, 2, devices, cols)
    term = einsum("ypcdx,pf->dfcxy", weighted, onehot)
    term = lax.psum_scatter(term, "coil", scatter_dimension=0, tiled=True)[0]

    masked = (
        sampled[:, :, None] * forward_rows[0][None],
        sampled[:, :, None] * forward_rows[1][None],
    )
    project = complex_einsum("yk,fkv->fyv", inverse_rows, masked)
    for sweep in range(OUTER):
        u_re = maps[:, None, 0] * field[None, :, 0] - maps[:, None, 1] * field[None, :, 1]
        u_im = maps[:, None, 0] * field[None, :, 1] + maps[:, None, 1] * field[None, :, 0]
        v_re, v_im = complex_einsum("fyv,cfxv->cfxy", project, (u_re, u_im))
        grad = jnp.stack(
            [
                jnp.sum(maps[:, None, 0] * v_re + maps[:, None, 1] * v_im, 0),
                jnp.sum(maps[:, None, 0] * v_im - maps[:, None, 1] * v_re, 0),
            ],
            1,
        )
        target = field - step_size * (grad - term)
        dual_time = jnp.zeros_like(target)
        dual_rows = jnp.zeros_like(target)
        field = target
        for repeat in range(INNER):
            diff_time = jnp.concatenate([field[1:] - field[:-1], jnp.zeros_like(field[:1])], 0)
            diff_rows = jnp.concatenate(
                [field[..., 1:] - field[..., :-1], jnp.zeros_like(field[..., :1])], -1
            )
            dual_time = jnp.clip(dual_time + dual_step * diff_time, -1.0, 1.0)
            dual_rows = jnp.clip(dual_rows + dual_step * diff_rows, -1.0, 1.0)
            inner_time, inner_rows = dual_time[:-1], dual_rows[..., :-1]
            none_time, none_rows = jnp.zeros_like(field[:1]), jnp.zeros_like(field[..., :1])
            divergence = (
                jnp.concatenate([none_time, inner_time], 0)
                - jnp.concatenate([inner_time, none_time], 0)
                + jnp.concatenate([none_rows, inner_rows], -1)
                - jnp.concatenate([inner_rows, none_rows], -1)
            )
            field = target - tv_weight * divergence

    result = field.reshape(frames, 2, cols, devices, rows).transpose(3, 0, 1, 2, 4)
    result = lax.all_to_all(result, "coil", 0, 0, tiled=True)
    return result.transpose(4, 1, 2, 0, 3).reshape(rows, frames, packed)


def fits_kernels(image, sens, kspace, devices):
    rows, frames, packed = image.shape
    coils = sens.shape[1]
    length, pairs, _ = kspace.shape
    per = LANES // rows
    return (
        devices & (devices - 1) == 0
        and devices >= 4
        and rows % 8 == 0
        and rows * per == LANES
        and frames == per
        and frames % 2 == 0
        and coils % per == 0
        and devices % per == 0
        and pairs % frames == 0
        and pairs * devices == coils * frames
        and length == 2 * LANES
        and packed % (16 * devices) == 0
        and packed % (4 * LANES) == 0
    )


def per_device(image, sens, kspace, mask):
    if fits_kernels(image, sens, kspace, lax.axis_size("coil")):
        return kernel_path(image, sens, kspace, mask)
    return general_path(image, sens, kspace, mask)


def solution(mesh):
    return jax.shard_map(
        per_device,
        mesh=mesh,
        in_specs=(
            P(("plane", "coil"), None, None),
            P(("plane", "coil"), None, None),
            P("plane", "coil", None),
            P(),
        ),
        out_specs=P(("plane", "coil"), None, None),
        check_vma=False,
    )
```

```python
import functools

import jax
import jax.numpy as jnp
import ml_dtypes
import numpy as np
from jax import lax
from jax.experimental import pallas as pl
from jax.experimental.pallas import tpu as pltpu
from jax.sharding import PartitionSpec as P

OUTER = 2
INNER = 2
LANES = 128
VMEM_LIMIT = 16 * 1024 * 1024
TRANSFORM_LIMIT = 52 * 1024 * 1024
WEIGH_LIMIT = 60 * 1024 * 1024

step_size = 0.5
tv_weight = 0.1
dual_step = 1.25
highest = lax.Precision.HIGHEST


def two_terms(table):
    first = table.astype(ml_dtypes.bfloat16)
    second = (table - first.astype(np.float64)).astype(ml_dtypes.bfloat16)
    return first, second


def dft(out_index, in_index, length):
    product = np.outer(out_index, in_index) % length
    return np.exp(2j * np.pi / length * product)


def packed_left(matrix):
    return np.block([[matrix.real, -matrix.imag], [matrix.imag, matrix.real]])


def packed_right(matrix):
    return packed_left(matrix).T


def split(value):
    first = value.astype(jnp.bfloat16)
    second = (value - first.astype(jnp.float32)).astype(jnp.bfloat16)
    return first, second


def dot3(left, right, contract=((1,), (0,))):
    dims = (contract, ((), ()))

    def dot(a, b):
        return lax.dot_general(a, b, dims, preferred_element_type=jnp.float32)

    return dot(left[0], right[0]) + (dot(left[0], right[1]) + dot(left[1], right[0]))


def lane_exchange(parts, width):
    parts = list(parts)
    lane = lax.broadcasted_iota(jnp.int32, parts[0].shape, parts[0].ndim - 1)
    axis = parts[0].ndim - 1
    bit = 1
    while bit < len(parts):
        odd = (lane // width) & bit != 0
        for s in range(len(parts)):
            if s & bit:
                continue
            low, high = parts[s], parts[s | bit]
            parts[s] = jnp.where(odd, pltpu.roll(high, width * bit, axis), low)
            parts[s | bit] = jnp.where(odd, high, pltpu.roll(low, LANES - width * bit, axis))
        bit *= 2
    return parts


def roll_last(value, distance):
    shape = value.shape
    flat = value.reshape(-1, shape[-1])
    return pltpu.roll(flat, distance % shape[-1], 1).reshape(shape)


def tv_step(target):
    length = target.shape[-1]
    row = lax.broadcasted_iota(jnp.int32, target.shape, target.ndim - 1)
    last, first = row == length - 1, row == 0
    nothing = jnp.zeros_like(target[:1])

    def adjoint(dual_time, dual_rows):
        from_time = jnp.concatenate([nothing, dual_time[:-1]], 0) - jnp.concatenate(
            [dual_time[:-1], nothing], 0
        )
        from_rows = jnp.where(first, 0.0, roll_last(dual_rows, 1)) - jnp.where(last, 0.0, dual_rows)
        return from_time + from_rows

    dual_time = jnp.zeros_like(target)
    dual_rows = jnp.zeros_like(target)
    primal = target
    for repeat in range(INNER):
        diff_time = jnp.concatenate([primal[1:] - primal[:-1], nothing], 0)
        diff_rows = jnp.where(last, 0.0, roll_last(primal, -1) - primal)
        dual_time = jnp.clip(dual_time + dual_step * diff_time, -1.0, 1.0)
        dual_rows = jnp.clip(dual_rows + dual_step * diff_rows, -1.0, 1.0)
        primal = target - tv_weight * adjoint(dual_time, dual_rows)
    return primal


def mask_responses(mask_ref, wave_hi, wave_lo, out_ref):
    for side in range(2):
        mask = mask_ref[side].astype(jnp.bfloat16)
        terms = [
            jnp.dot(mask, wave[side], preferred_element_type=jnp.float32)
            for wave in (wave_hi, wave_lo)
        ]
        out_ref[side] = terms[0] + terms[1]


def frame_tables(response_ref, f):
    half = response_ref.shape[-1] // 2
    tables = []
    for side in range(2):
        row = response_ref[side, pl.ds(f, 1), :]
        parts = []
        for at in (0, half):
            spread = jnp.broadcast_to(row[:, at : at + half], (half, half))
            turned = pltpu.roll(spread, 0, 1, stride=1, stride_axis=0)
            if side:
                before = lax.broadcasted_iota(jnp.int32, (half, half), 1) < (
                    lax.broadcasted_iota(jnp.int32, (half, half), 0)
                )
                turned = jnp.where(before, -turned, turned)
            parts.append(turned)
        re, im = parts
        tables.append(
            split(jnp.concatenate([jnp.concatenate([re, im], 1), jnp.concatenate([-im, re], 1)], 0))
        )
    return tables


def normal_frame(maps_ref, field_re, field_im, tables):
    coils, _, cols, length = maps_ref.shape
    half = length // 2
    maps_re, maps_im = maps_ref[:, 0], maps_ref[:, 1]
    u_re = maps_re * field_re[None] - maps_im * field_im[None]
    u_im = maps_re * field_im[None] + maps_im * field_re[None]
    flat_re = u_re.reshape(coils * cols, length)
    flat_im = u_im.reshape(coils * cols, length)
    outs = []
    for sign, table in zip((1.0, -1.0), tables):
        packed = jnp.concatenate(
            [
                flat_re[:, :half] + sign * flat_re[:, half:],
                flat_im[:, :half] + sign * flat_im[:, half:],
            ],
            1,
        )
        outs.append(dot3(split(packed), table))
    plus, minus = outs
    v_re = jnp.concatenate(
        [plus[:, :half] + minus[:, :half], plus[:, :half] - minus[:, :half]], 1
    ).reshape(coils, cols, length)
    v_im = jnp.concatenate(
        [plus[:, half:] + minus[:, half:], plus[:, half:] - minus[:, half:]], 1
    ).reshape(coils, cols, length)
    return (
        jnp.sum(maps_re * v_re + maps_im * v_im, 0),
        jnp.sum(maps_re * v_im - maps_im * v_re, 0),
    )


def coil_blocks_kernel(coils, *refs):
    *tiles, before, out_ref = refs
    del before
    devices, pair_coils, rows, lanes = out_ref.shape
    halves = len(tiles) // 2
    each = lanes // (2 * LANES)
    for d in range(devices):
        for c in range(pair_coils):
            for part in range(2):
                for t in range(each):
                    at = (part * each + t) * LANES
                    out_ref[d, c, :, at : at + LANES] = tiles[part * halves + (d & 1) * each + t][
                        pl.ds((d >> 1) * pair_coils + c, rows, stride=coils), :
                    ]


def with_bit(index, bit, value):
    return ((index >> bit) << (bit + 1)) | (value << bit) | (index & ((1 << bit) - 1))


def column_blocks_kernel(coils, frames, chunk_of, level, device_ref, *refs):
    *tiles, keep_ref, send_ref, turned = refs
    sens_tiles, image_tiles = tiles[: len(tiles) // 2], tiles[len(tiles) // 2 :]
    blocks, groups, _, cols, _ = keep_ref.shape
    rows = sens_tiles[0].shape[0] // coils
    per = LANES // rows
    half = len(sens_tiles) // 2
    mine = (device_ref[0] >> level) & 1
    far = chunk_of[1 << level] * cols
    for g in range(groups):
        if g * per < coils:
            tiles, count, base = sens_tiles, coils, g * per
        else:
            tiles, count, base = image_tiles, frames, g * per - coils
        for t, ref in enumerate(tiles):
            turned[t // half, pl.ds(t % half * LANES, LANES)] = jnp.concatenate(
                [ref[pl.ds(base + c, rows, stride=count), :] for c in range(per)], 0
            ).T
        for out, side in ((keep_ref, mine), (send_ref, 1 - mine)):
            for e in range(blocks):
                at = pl.multiple_of(chunk_of[with_bit(e, level, 0)] * cols + side * far, cols)
                for part in range(2):
                    out[e, g, part] = turned[part, pl.ds(at, cols)]


def base_kernel(start, frames, device_ref, kspace_ref, mask_ref, *refs):
    col_hi, col_lo, row_hi, row_lo, keep_ref, send_ref, data, near_hi, near_lo, arrived = refs
    own, _, _, span, length = keep_ref.shape
    bit = device_ref[0] & 1
    half = length // 2
    frame = pl.program_id(0)

    def fetch(f, slot):
        return [
            pltpu.make_async_copy(
                kspace_ref.at[:, odd, start + f + c * frames, :],
                data.at[slot, c, pl.ds(odd * half, half)],
                arrived.at[slot, c, odd],
            )
            for c in range(own)
            for odd in range(2)
        ]

    @pl.when(frame == 0)
    def _():
        for copy in fetch(0, 0):
            copy.start()
        for far, near in ((col_hi, near_hi), (col_lo, near_lo)):
            for i, which in enumerate((bit, 1 - bit)):
                for part in range(2):
                    at = pl.multiple_of((2 * part + which) * span, span)
                    near[pl.ds((2 * i + part) * span, span)] = far[pl.ds(at, span)]

    @pl.when(frame + 1 < pl.num_programs(0))
    def _():
        for copy in fetch(frame + 1, (frame + 1) % 2):
            copy.start()

    slot = frame % 2
    for copy in fetch(frame, slot):
        copy.wait()
    columns = [
        dot3((near_hi[...], near_lo[...]), split(data[slot, c]), ((1,), (1,))) * mask_ref[0]
        for c in range(own)
    ]
    blocks = [v[2 * i * span : (2 * i + 2) * span] for v in columns for i in range(2)]
    sides = []
    for odd in range(2):
        at = odd * half
        stacked = jnp.concatenate(
            [
                jnp.concatenate([v[:span, at : at + half], v[span:, at : at + half]], 1)
                for v in blocks
            ],
            0,
        )
        sides.append(dot3(split(stacked), (row_hi[odd], row_lo[odd])))
    for c in range(own):
        for i, ref in enumerate((keep_ref, send_ref)):
            rows = (2 * c + i) * span
            even, odd = [side[rows : rows + span] for side in sides]
            for part in range(2):
                e = even[:, part * half : (part + 1) * half]
                o = odd[:, part * half : (part + 1) * half]
                ref[c, 0, part] = jnp.concatenate([e + o, e - o], 1)


def weigh_kernel(outer, level, device_ref, maps_ref, kept_ref, got_ref, keep_out, send_out, *refs):
    turned, kept, got, keep, send, arrived, left = refs
    devices, pair_coils, rows, lanes = maps_ref.shape
    own, count = got_ref.shape[:2]
    inner, _, _, cols, length = keep.shape
    inner //= outer

    copies = [
        [
            pltpu.make_async_copy(src.at[:, f], dst.at[:, f], arrived.at[i, f])
            for i, (src, dst) in enumerate(((kept_ref, kept), (got_ref, got)))
        ]
        for f in range(count)
    ]
    for pair in copies:
        for copy in pair:
            copy.start()
    for c in range(pair_coils):
        one = maps_ref[:, c].reshape(length, lanes).T
        turned[c, 0] = one[: lanes // 2]
        turned[c, 1] = one[lanes // 2 :]

    bit, mine = device_ref[0] & 1, (device_ref[0] >> level) & 1
    span = inner * cols
    results = []
    for f in range(count):
        for copy in copies[f]:
            copy.wait()
        for ref, which in ((send, 1 - mine), (keep, mine)):
            for i in range(outer):
                at = pl.ds(pl.multiple_of((2 * i + which) * span, span), span)
                total_re = total_im = 0.0
                for base, first in ((kept, bit * own), (got, (1 - bit) * own)):
                    for c in range(own):
                        s_re, s_im = turned[first + c, 0, at, :], turned[first + c, 1, at, :]
                        b_re, b_im = base[c, f, 0, at, :], base[c, f, 1, at, :]
                        total_re += s_re * b_re + s_im * b_im
                        total_im += s_re * b_im - s_im * b_re
                here = slice(i * inner, (i + 1) * inner)
                ref[here, f, 0] = total_re.reshape(inner, cols, length)
                ref[here, f, 1] = total_im.reshape(inner, cols, length)
        for i, (src, dst) in enumerate(((send, send_out), (keep, keep_out))):
            results.append(pltpu.make_async_copy(src.at[:, f], dst.at[:, f], left.at[i, f]))
            results[-1].start()
    for copy in results:
        copy.wait()


def first_normal_kernel(coils, level, device_ref, got_ref, mask_ref, wave_hi, wave_lo, *refs):
    maps_out, field_out, grad_out, responses = refs[-4:]
    mask_responses(mask_ref, wave_hi, wave_lo, responses)
    blocks, _, groups, _, cols, lanes = got_ref.shape
    devices = 2 * blocks
    mine = (device_ref[0] >> level) & 1
    frames = field_out.shape[0]

    def block(s, g):
        e = ((s >> (level + 1)) << level) | (s & ((1 << level) - 1))
        return got_ref[e, ((s >> level) & 1) ^ mine, g]

    per = (coils + frames) // groups
    width = lanes // per
    for g in range(groups):
        out, base = (maps_out, g * per) if g * per < coils else (field_out, g * per - coils)
        for h in range(devices // per):
            exchanged = lane_exchange([block(h * per + s, g) for s in range(per)], width)
            for c in range(per):
                out[base + c, :, :, h * lanes : (h + 1) * lanes] = exchanged[c]

    gradient_frames(0, maps_out, field_out, responses, grad_out)


def gradient_frames(start, maps_ref, field_ref, responses, grad_out):
    def one(i, _):
        f = start + i
        grad_out[i, 0], grad_out[i, 1] = normal_frame(
            maps_ref, field_ref[f, 0], field_ref[f, 1], frame_tables(responses, f)
        )
        return 0

    lax.fori_loop(0, grad_out.shape[0], one, 0)


def second_normal_kernel(start, maps_ref, field_ref, mask_ref, wave_hi, wave_lo, *refs):
    grad_out, responses = refs[-2:]
    mask_responses(mask_ref, wave_hi, wave_lo, responses)
    gradient_frames(start, maps_ref, field_ref, responses, grad_out)


def steps_kernel(field_ref, grad0_ref, grad1_ref, maps_ref, mask_ref, *refs):
    wave_hi, wave_lo, *terms, out_ref, field, grad, responses = refs
    frames, _, cols, length = field_ref.shape
    devices, _, _, lanes = out_ref.shape
    mask_responses(mask_ref, wave_hi, wave_lo, responses)
    data_term = jnp.concatenate(
        [keep[...] + got[...] for keep, got in zip(terms[0::2], terms[1::2])], 0
    )
    first = jnp.concatenate([grad0_ref[...], grad1_ref[...]], 0)
    field[...] = tv_step(field_ref[...] - step_size * (first - data_term))
    for sweep in range(1, OUTER):

        def one(f, _):
            grad[f, 0], grad[f, 1] = normal_frame(
                maps_ref, field[f, 0], field[f, 1], frame_tables(responses, f)
            )
            return 0

        lax.fori_loop(0, frames, one, 0)
        field[...] = tv_step(field[...] - step_size * (grad[...] - data_term))
    per = frames
    for h in range(devices // per):
        parts = [field[f, :, :, h * lanes : (h + 1) * lanes] for f in range(per)]
        exchanged = lane_exchange(parts, lanes // per)
        for s in range(per):
            out_ref[h * per + s] = exchanged[s]


def rows_out_kernel(chunk_of, frames, got_ref, out_ref, tiles):
    devices, _, cols, lanes = got_ref.shape
    count = tiles.shape[0]
    rows = lanes // frames
    order = sorted(range(devices), key=lambda d: chunk_of[d])
    each = LANES // cols
    for t in range(count):
        at = t % (count // 2) * each
        turned = jnp.concatenate([got_ref[d, t // (count // 2)] for d in order[at : at + each]], 0).T
        for f in range(frames):
            tiles[t, pl.ds(f, rows, stride=frames), :] = turned[f * rows : (f + 1) * rows]
        out_ref[:, t * LANES : (t + 1) * LANES] = tiles[t]


def params(limit=VMEM_LIMIT):
    return pltpu.CompilerParams(vmem_limit_bytes=limit)


def cost(flops, moved):
    return pl.CostEstimate(flops=int(flops), bytes_accessed=int(moved), transcendentals=0)


def whole(shape):
    return pl.BlockSpec(shape, lambda *_: (0,) * len(shape))


def lane_tiles(rows, lanes):
    return [
        pl.BlockSpec((rows, LANES), lambda *_, t=t: (0, t), pipeline_mode=pl.Buffered(1))
        for t in range(lanes // LANES)
    ]


def f32(*shape):
    return jax.ShapeDtypeStruct(shape, jnp.float32)


def exchange(send, bit):
    devices = lax.axis_size("coil")
    return lax.ppermute(send, "coil", [(i, i ^ (1 << bit)) for i in range(devices)])


def halve(keep, got, bit, device):
    mine = (device >> bit) & 1

    def part(which):
        return lax.dynamic_index_in_dim(
            keep, which, bit - 1, keepdims=True
        ) + lax.dynamic_index_in_dim(got, which, bit - 1, keepdims=True)

    send = part(1 - mine)
    return part(mine), send


def kernel_path(image, sens, kspace, mask):
    rows, frames, packed = image.shape
    coils = sens.shape[1]
    length, pairs, _ = kspace.shape
    half = packed // 2
    hl = length // 2
    devices = lax.axis_size("coil")
    device = lax.axis_index("coil")
    bits = devices.bit_length() - 1
    own = pairs // frames
    cols = half // devices
    per = LANES // rows
    groups = (coils + frames) // per
    chunk_of = [sum(((d >> b) & 1) << (bits - 1 - b) for b in range(bits)) for d in range(devices)]

    k = np.arange(length)
    z = np.arange(half)
    y = np.arange(hl)
    col_hi, col_lo = two_terms(packed_left(dft(z, z, half) / np.sqrt(half)))
    lanes_k = [k[0::2], k[1::2]]
    inverse = [packed_right(dft(y, ks, length)) for ks in lanes_k]
    row_hi, row_lo = two_terms(np.stack(inverse) / np.sqrt(length))
    waves = [dft(ks, y, length) * 0.5 / hl for ks in lanes_k]
    wave_hi, wave_lo = two_terms(np.stack([np.concatenate([w.real, w.imag], 1) for w in waves]))

    sampled = mask.astype(jnp.float32)
    mask_sides = jnp.stack([sampled[:, 0::2], sampled[:, 1::2]])
    mask_lanes = jnp.concatenate([mask_sides[0], mask_sides[1]], 1)[:, None, :]

    sens_rows = sens.reshape(rows * coils, packed)
    image_rows = image.reshape(rows * frames, packed)

    with jax.named_scope("column_maps"):
        level = 1
        block = (devices // 2, groups, 2, cols, LANES)
        column_keep, column_send = pl.pallas_call(
            functools.partial(column_blocks_kernel, coils, frames, chunk_of, level),
            grid=(1,),
            out_shape=(f32(*block),) * 2,
            in_specs=[pl.BlockSpec(memory_space=pltpu.SMEM)]
            + lane_tiles(rows * coils, packed)
            + lane_tiles(rows * frames, packed),
            out_specs=(whole(block),) * 2,
            scratch_shapes=[pltpu.VMEM((2, half, LANES), jnp.float32)],
            compiler_params=params(),
            cost_estimate=cost(0, 2 * (sens.size + image.size) * 4),
        )(device[None], *[sens_rows] * (packed // LANES), *[image_rows] * (packed // LANES))
        column_blocks = jnp.stack([column_keep, exchange(column_send, level)], 1)
        sides = [[with_bit(e, level, side) for e in range(devices // 2)] for side in range(2)]

    with jax.named_scope("coil_maps"):
        blocks = pl.pallas_call(
            functools.partial(coil_blocks_kernel, coils),
            grid=(1,),
            out_shape=f32(devices, 2 * own, rows, half),
            in_specs=lane_tiles(rows * coils, packed) + [pl.BlockSpec(memory_space=pl.ANY)],
            out_specs=whole((devices, 2 * own, rows, half)),
            compiler_params=params(),
            cost_estimate=cost(0, 2 * sens.size * 4),
        )(*[sens_rows] * (packed // LANES), column_send)
        blocks, device = lax.optimization_barrier((blocks, device))
        coil_maps = lax.all_to_all(blocks, "coil", 0, 0, tiled=True)

    plans = [
        (frames // 2, list(range(1, bits))),
        (frames // 2, list(range(1, bits))),
    ]
    firsts = [sum(count for count, _ in plans[:i]) for i in range(len(plans))]
    span = half // 2
    smem = pl.BlockSpec(memory_space=pltpu.SMEM)
    kept, got = [], []
    for start, (count, _) in zip(firsts, plans):
        with jax.named_scope("data_transform"):
            block = pl.BlockSpec((own, 1, 2, span, length), lambda f: (0, f, 0, 0, 0))
            keep, send = pl.pallas_call(
                functools.partial(base_kernel, start, frames),
                grid=(count,),
                out_shape=(f32(own, count, 2, span, length),) * 2,
                in_specs=[
                    smem,
                    pl.BlockSpec(memory_space=pltpu.HBM),
                    pl.BlockSpec((1, 1, length), lambda f, start=start: (start + f, 0, 0)),
                    whole((packed, packed)),
                    whole((packed, packed)),
                    whole((2, length, length)),
                    whole((2, length, length)),
                ],
                out_specs=(block, block),
                scratch_shapes=[
                    pltpu.VMEM((2, own, length, packed), jnp.float32),
                    pltpu.VMEM((packed, packed), jnp.bfloat16),
                    pltpu.VMEM((packed, packed), jnp.bfloat16),
                    pltpu.SemaphoreType.DMA((2, own, 2)),
                ],
                compiler_params=params(TRANSFORM_LIMIT),
                cost_estimate=cost(
                    own * count * 36 * half * half * length, 16 * own * count * half * length
                ),
            )(
                device[None],
                kspace.reshape(hl, 2, pairs, packed),
                mask_lanes,
                col_hi,
                col_lo,
                row_hi,
                row_lo,
            )
        if len(kept) == len(plans) - 1:
            column_blocks, send = lax.optimization_barrier((column_blocks, send))
        kept.append(keep)
        got.append(exchange(send, 0))
    with jax.named_scope("column_maps"):
        column_maps = lax.all_to_all(
            column_blocks, "coil", 0, 0, tiled=True, axis_index_groups=sides
        )

    field = f32(frames, 2, cols, length)
    normal_cost = 6 * 2 * frames * coils * cols * length * length

    responses = pltpu.VMEM((2, frames, length), jnp.float32)

    part = f32(frames // 2, 2, cols, length)
    anywhere = pl.BlockSpec(memory_space=pl.ANY)

    def second_gradient(maps, field0, before):
        return pl.pallas_call(
            functools.partial(second_normal_kernel, frames // 2),
            in_specs=[pl.BlockSpec(memory_space=pltpu.VMEM)] * 5 + [anywhere] * len(before),
            out_shape=part,
            scratch_shapes=[responses],
            compiler_params=params(),
            cost_estimate=cost(normal_cost // 2, 2 * sens.size * 4),
            name="second_gradient",
        )(maps, field0, mask_sides, wave_hi, wave_lo, *before)

    def first_gradient(column_maps, before):
        return pl.pallas_call(
            functools.partial(first_normal_kernel, coils, level),
            in_specs=[smem]
            + [pl.BlockSpec(memory_space=pltpu.VMEM)] * 4
            + [pl.BlockSpec(memory_space=pl.ANY)] * len(before),
            out_shape=(f32(coils, 2, cols, length), field, part),
            scratch_shapes=[responses],
            compiler_params=params(),
            cost_estimate=cost(normal_cost // 2, 4 * sens.size * 4),
            name="first_gradient",
        )(device[None], column_maps, mask_sides, wave_hi, wave_lo, *before)

    with jax.named_scope("data_term"):
        terms = []
        for stream, (count, order) in enumerate(plans):
            outer = 2 ** (order[0] - 1)
            out = f32(devices // 4, count, 2, cols, length)
            vmem, anywhere = pl.BlockSpec(memory_space=pltpu.VMEM), pl.BlockSpec(memory_space=pl.ANY)
            base = pltpu.VMEM((own, count, 2, span, length), jnp.float32)
            term = pltpu.VMEM(out.shape, jnp.float32)
            keep, send = pl.pallas_call(
                functools.partial(weigh_kernel, outer, order[0]),
                out_shape=(out, out),
                in_specs=[smem, vmem, anywhere, anywhere],
                out_specs=(anywhere, anywhere),
                scratch_shapes=[
                    pltpu.VMEM((2 * own, 2, span, length), jnp.float32),
                    base,
                    base,
                    term,
                    term,
                    pltpu.SemaphoreType.DMA((2, count)),
                    pltpu.SemaphoreType.DMA((2, count)),
                ],
                compiler_params=params(WEIGH_LIMIT),
                cost_estimate=cost(0, 2 * kept[stream].size * 4 + 2 * out.size * 4),
            )(device[None], coil_maps, kept[stream], got[stream])
            dims = [2] * (bits - 1)
            dims[order[0] - 1] = 1
            received = exchange(send, order[0]).reshape(*dims, *keep.shape[1:])
            terms.append((keep.reshape(received.shape), received))
        sent = [None] * len(plans)

        def advance(stream, step):
            order = plans[stream][1]
            keep, sent[stream] = halve(*terms[stream], order[step], device)
            terms[stream] = (keep, exchange(sent[stream], order[step]))

        for step in range(1, bits - 2):
            for stream in range(len(plans)):
                advance(stream, step)
        advance(0, bits - 2)
        maps, field0, early = first_gradient(column_maps, sent)
        terms[1], early = lax.optimization_barrier((terms[1], early))
        advance(1, bits - 2)
        late = second_gradient(maps, field0, sent[1:])
        terms = [value.reshape(-1, 2, cols, length) for term in terms for value in term]

    with jax.named_scope("outer_steps"):
        blocks = pl.pallas_call(
            steps_kernel,
            out_shape=f32(devices, 2, cols, LANES),
            scratch_shapes=[pltpu.VMEM(field.shape, jnp.float32)] * 2 + [responses],
            compiler_params=params(),
            cost_estimate=cost(normal_cost, 4 * sens.size * 4),
        )(field0, early, late, maps, mask_sides, wave_hi, wave_lo, *terms)

    with jax.named_scope("result_rows"):
        got = lax.all_to_all(blocks, "coil", 0, 0, tiled=True)
        recon = pl.pallas_call(
            functools.partial(rows_out_kernel, chunk_of, frames),
            out_shape=f32(rows * frames, packed),
            scratch_shapes=[pltpu.VMEM((packed // LANES, rows * frames, LANES), jnp.float32)],
            compiler_params=params(),
            cost_estimate=cost(0, 2 * image.size * 4),
        )(got)
    return recon.reshape(rows, frames, packed)


def einsum(form, left, right):
    return jnp.einsum(form, left, right, precision=highest, preferred_element_type=jnp.float32)


def complex_einsum(form, left, right):
    (a, b), (c, d) = left, right
    return (
        einsum(form, a, c) - einsum(form, b, d),
        einsum(form, a, d) + einsum(form, b, c),
    )


def general_path(image, sens, kspace, mask):
    rows, frames, packed = image.shape
    coils = sens.shape[1]
    length, pairs, _ = kspace.shape
    half = packed // 2
    devices = lax.axis_size("coil")
    device = lax.axis_index("coil")
    cols = half // devices

    def table(size):
        values = dft(np.arange(size), np.arange(size), size) / np.sqrt(size)
        return jnp.asarray(values.real, jnp.float32), jnp.asarray(values.imag, jnp.float32)

    inverse_rows, inverse_cols = table(length), table(half)
    forward_rows = (inverse_rows[0], -inverse_rows[1])

    both = jnp.concatenate([sens, image], 1).reshape(rows, coils + frames, 2, devices, cols)
    both = lax.all_to_all(both.transpose(3, 1, 2, 4, 0), "coil", 0, 0, tiled=True)
    both = both.transpose(1, 2, 3, 0, 4).reshape(coils + frames, 2, cols, length)
    maps, field = both[:coils], both[coils:]

    own = max(1, pairs // frames)
    repeats = devices * own // coils
    spread = jnp.repeat(sens.reshape(rows, coils // own, own, packed), repeats, axis=1)
    spread = spread.transpose(1, 0, 2, 3)
    coil_maps = lax.all_to_all(spread, "coil", 0, 0, tiled=True).reshape(length, own, packed)

    ids = device * pairs + lax.iota(jnp.int32, pairs)
    onehot = (ids[:, None] % frames == lax.iota(jnp.int32, frames)[None, :]).astype(jnp.float32)
    sampled = mask.astype(jnp.float32)
    data = einsum("pf,fk->kp", onehot, sampled)[:, :, None] * kspace
    data = (data[..., :half], data[..., half:])
    data = complex_einsum("kpz,zx->kpx", data, inverse_cols)
    data = complex_einsum("yk,kpx->ypx", inverse_rows, data)
    pair_maps = jnp.repeat(coil_maps, pairs // own, axis=1)
    m_re, m_im = pair_maps[..., :half], pair_maps[..., half:]
    weighted = jnp.stack(
        [m_re * data[0] + m_im * data[1], m_re * data[1] - m_im * data[0]], 2
    ).reshape(length, pairs, 2, devices, cols)
    term = einsum("ypcdx,pf->dfcxy", weighted, onehot)
    term = lax.psum_scatter(term, "coil", scatter_dimension=0, tiled=True)[0]

    masked = (
        sampled[:, :, None] * forward_rows[0][None],
        sampled[:, :, None] * forward_rows[1][None],
    )
    project = complex_einsum("yk,fkv->fyv", inverse_rows, masked)
    for sweep in range(OUTER):
        u_re = maps[:, None, 0] * field[None, :, 0] - maps[:, None, 1] * field[None, :, 1]
        u_im = maps[:, None, 0] * field[None, :, 1] + maps[:, None, 1] * field[None, :, 0]
        v_re, v_im = complex_einsum("fyv,cfxv->cfxy", project, (u_re, u_im))
        grad = jnp.stack(
            [
                jnp.sum(maps[:, None, 0] * v_re + maps[:, None, 1] * v_im, 0),
                jnp.sum(maps[:, None, 0] * v_im - maps[:, None, 1] * v_re, 0),
            ],
            1,
        )
        target = field - step_size * (grad - term)
        dual_time = jnp.zeros_like(target)
        dual_rows = jnp.zeros_like(target)
        field = target
        for repeat in range(INNER):
            diff_time = jnp.concatenate([field[1:] - field[:-1], jnp.zeros_like(field[:1])], 0)
            diff_rows = jnp.concatenate(
                [field[..., 1:] - field[..., :-1], jnp.zeros_like(field[..., :1])], -1
            )
            dual_time = jnp.clip(dual_time + dual_step * diff_time, -1.0, 1.0)
            dual_rows = jnp.clip(dual_rows + dual_step * diff_rows, -1.0, 1.0)
            inner_time, inner_rows = dual_time[:-1], dual_rows[..., :-1]
            none_time, none_rows = jnp.zeros_like(field[:1]), jnp.zeros_like(field[..., :1])
            divergence = (
                jnp.concatenate([none_time, inner_time], 0)
                - jnp.concatenate([inner_time, none_time], 0)
                + jnp.concatenate([none_rows, inner_rows], -1)
                - jnp.concatenate([inner_rows, none_rows], -1)
            )
            field = target - tv_weight * divergence

    result = field.reshape(frames, 2, cols, devices, rows).transpose(3, 0, 1, 2, 4)
    result = lax.all_to_all(result, "coil", 0, 0, tiled=True)
    return result.transpose(4, 1, 2, 0, 3).reshape(rows, frames, packed)


def fits_kernels(image, sens, kspace, devices):
    rows, frames, packed = image.shape
    coils = sens.shape[1]
    length, pairs, _ = kspace.shape
    per = LANES // rows
    return (
        devices & (devices - 1) == 0
        and devices >= 4
        and rows % 8 == 0
        and rows * per == LANES
        and frames == per
        and frames % 2 == 0
        and coils % per == 0
        and devices % per == 0
        and pairs % frames == 0
        and pairs * devices == coils * frames
        and length == 2 * LANES
        and packed % (16 * devices) == 0
        and packed % (4 * LANES) == 0
    )


def per_device(image, sens, kspace, mask):
    if fits_kernels(image, sens, kspace, lax.axis_size("coil")):
        return kernel_path(image, sens, kspace, mask)
    return general_path(image, sens, kspace, mask)


def solution(mesh):
    return jax.shard_map(
        per_device,
        mesh=mesh,
        in_specs=(
            P(("plane", "coil"), None, None),
            P(("plane", "coil"), None, None),
            P("plane", "coil", None),
            P(),
        ),
        out_specs=P(("plane", "coil"), None, None),
        check_vma=False,
    )
```

```python
import functools

import jax
import jax.numpy as jnp
import ml_dtypes
import numpy as np
from jax import lax
from jax.experimental import pallas as pl
from jax.experimental.pallas import tpu as pltpu
from jax.sharding import PartitionSpec as P

OUTER = 2
INNER = 2
LANES = 128
VMEM_LIMIT = 16 * 1024 * 1024
TRANSFORM_LIMIT = 52 * 1024 * 1024
WEIGH_LIMIT = 60 * 1024 * 1024

step_size = 0.5
tv_weight = 0.1
dual_step = 1.25
highest = lax.Precision.HIGHEST


def two_terms(table):
    first = table.astype(ml_dtypes.bfloat16)
    second = (table - first.astype(np.float64)).astype(ml_dtypes.bfloat16)
    return first, second


def dft(out_index, in_index, length):
    product = np.outer(out_index, in_index) % length
    return np.exp(2j * np.pi / length * product)


def packed_left(matrix):
    return np.block([[matrix.real, -matrix.imag], [matrix.imag, matrix.real]])


def packed_right(matrix):
    return packed_left(matrix).T


def split(value):
    first = value.astype(jnp.bfloat16)
    second = (value - first.astype(jnp.float32)).astype(jnp.bfloat16)
    return first, second


def dot3(left, right, contract=((1,), (0,))):
    dims = (contract, ((), ()))

    return lax.dot_general(
        jnp.concatenate([left[0], left[0], left[1]], contract[0][0]),
        jnp.concatenate([right[0], right[1], right[0]], contract[1][0]),
        dims,
        preferred_element_type=jnp.float32,
    )


def lane_exchange(parts, width):
    parts = list(parts)
    lane = lax.broadcasted_iota(jnp.int32, parts[0].shape, parts[0].ndim - 1)
    axis = parts[0].ndim - 1
    bit = 1
    while bit < len(parts):
        odd = (lane // width) & bit != 0
        for s in range(len(parts)):
            if s & bit:
                continue
            low, high = parts[s], parts[s | bit]
            parts[s] = jnp.where(odd, pltpu.roll(high, width * bit, axis), low)
            parts[s | bit] = jnp.where(odd, high, pltpu.roll(low, LANES - width * bit, axis))
        bit *= 2
    return parts


def roll_last(value, distance):
    shape = value.shape
    flat = value.reshape(-1, shape[-1])
    return pltpu.roll(flat, distance % shape[-1], 1).reshape(shape)


def tv_step(target):
    length = target.shape[-1]
    row = lax.broadcasted_iota(jnp.int32, target.shape, target.ndim - 1)
    last, first = row == length - 1, row == 0
    nothing = jnp.zeros_like(target[:1])

    def adjoint(dual_time, dual_rows):
        from_time = jnp.concatenate([nothing, dual_time[:-1]], 0) - jnp.concatenate(
            [dual_time[:-1], nothing], 0
        )
        from_rows = jnp.where(first, 0.0, roll_last(dual_rows, 1)) - jnp.where(last, 0.0, dual_rows)
        return from_time + from_rows

    dual_time = jnp.zeros_like(target)
    dual_rows = jnp.zeros_like(target)
    primal = target
    for repeat in range(INNER):
        diff_time = jnp.concatenate([primal[1:] - primal[:-1], nothing], 0)
        diff_rows = jnp.where(last, 0.0, roll_last(primal, -1) - primal)
        dual_time = jnp.clip(dual_time + dual_step * diff_time, -1.0, 1.0)
        dual_rows = jnp.clip(dual_rows + dual_step * diff_rows, -1.0, 1.0)
        primal = target - tv_weight * adjoint(dual_time, dual_rows)
    return primal


def mask_responses(mask_ref, wave_hi, wave_lo, out_ref):
    for side in range(2):
        mask = mask_ref[side].astype(jnp.bfloat16)
        terms = [
            jnp.dot(mask, wave[side], preferred_element_type=jnp.float32)
            for wave in (wave_hi, wave_lo)
        ]
        out_ref[side] = terms[0] + terms[1]


def frame_tables(response_ref, f):
    half = response_ref.shape[-1] // 2
    tables = []
    for side in range(2):
        row = response_ref[side, pl.ds(f, 1), :]
        parts = []
        for at in (0, half):
            spread = jnp.broadcast_to(row[:, at : at + half], (half, half))
            turned = pltpu.roll(spread, 0, 1, stride=1, stride_axis=0)
            if side:
                before = lax.broadcasted_iota(jnp.int32, (half, half), 1) < (
                    lax.broadcasted_iota(jnp.int32, (half, half), 0)
                )
                turned = jnp.where(before, -turned, turned)
            parts.append(turned)
        re, im = parts
        tables.append(
            split(jnp.concatenate([jnp.concatenate([re, im], 1), jnp.concatenate([-im, re], 1)], 0))
        )
    return tables


def normal_frame(maps_ref, field_re, field_im, tables):
    coils, _, cols, length = maps_ref.shape
    half = length // 2
    maps_re, maps_im = maps_ref[:, 0], maps_ref[:, 1]
    u_re = maps_re * field_re[None] - maps_im * field_im[None]
    u_im = maps_re * field_im[None] + maps_im * field_re[None]
    flat_re = u_re.reshape(coils * cols, length)
    flat_im = u_im.reshape(coils * cols, length)
    outs = []
    for sign, table in zip((1.0, -1.0), tables):
        packed = jnp.concatenate(
            [
                flat_re[:, :half] + sign * flat_re[:, half:],
                flat_im[:, :half] + sign * flat_im[:, half:],
            ],
            1,
        )
        outs.append(dot3(split(packed), table))
    plus, minus = outs
    v_re = jnp.concatenate(
        [plus[:, :half] + minus[:, :half], plus[:, :half] - minus[:, :half]], 1
    ).reshape(coils, cols, length)
    v_im = jnp.concatenate(
        [plus[:, half:] + minus[:, half:], plus[:, half:] - minus[:, half:]], 1
    ).reshape(coils, cols, length)
    return (
        jnp.sum(maps_re * v_re + maps_im * v_im, 0),
        jnp.sum(maps_re * v_im - maps_im * v_re, 0),
    )


def coil_blocks_kernel(coils, *refs):
    *tiles, out_ref = refs
    devices, pair_coils, rows, lanes = out_ref.shape
    halves = len(tiles) // 2
    each = lanes // (2 * LANES)
    for d in range(devices):
        for c in range(pair_coils):
            for part in range(2):
                for t in range(each):
                    at = (part * each + t) * LANES
                    out_ref[d, c, :, at : at + LANES] = tiles[part * halves + (d & 1) * each + t][
                        pl.ds((d >> 1) * pair_coils + c, rows, stride=coils), :
                    ]


def with_bit(index, bit, value):
    return ((index >> bit) << (bit + 1)) | (value << bit) | (index & ((1 << bit) - 1))


def column_blocks_kernel(coils, frames, chunk_of, level, device_ref, *refs):
    *tiles, keep_ref, send_ref, turned = refs
    sens_tiles, image_tiles = tiles[: len(tiles) // 2], tiles[len(tiles) // 2 :]
    blocks, groups, _, cols, _ = keep_ref.shape
    rows = sens_tiles[0].shape[0] // coils
    per = LANES // rows
    half = len(sens_tiles) // 2
    mine = (device_ref[0] >> level) & 1
    far = chunk_of[1 << level] * cols
    for g in range(groups):
        if g * per < coils:
            tiles, count, base = sens_tiles, coils, g * per
        else:
            tiles, count, base = image_tiles, frames, g * per - coils
        for t, ref in enumerate(tiles):
            turned[t // half, pl.ds(t % half * LANES, LANES)] = jnp.concatenate(
                [ref[pl.ds(base + c, rows, stride=count), :] for c in range(per)], 0
            ).T
        for out, side in ((keep_ref, mine), (send_ref, 1 - mine)):
            for e in range(blocks):
                at = pl.multiple_of(chunk_of[with_bit(e, level, 0)] * cols + side * far, cols)
                for part in range(2):
                    out[e, g, part] = turned[part, pl.ds(at, cols)]


def base_kernel(start, frames, device_ref, kspace_ref, mask_ref, *refs):
    col_hi, col_lo, row_hi, row_lo, keep_ref, send_ref, data, near_hi, near_lo, arrived = refs
    own, _, _, span, length = keep_ref.shape
    bit = device_ref[0] & 1
    half = length // 2
    frame = pl.program_id(0)

    def fetch(f, slot):
        return [
            pltpu.make_async_copy(
                kspace_ref.at[:, odd, start + f + c * frames, :],
                data.at[slot, c, pl.ds(odd * half, half)],
                arrived.at[slot, c, odd],
            )
            for c in range(own)
            for odd in range(2)
        ]

    @pl.when(frame == 0)
    def _():
        for copy in fetch(0, 0):
            copy.start()
        for far, near in ((col_hi, near_hi), (col_lo, near_lo)):
            for i, which in enumerate((bit, 1 - bit)):
                for part in range(2):
                    at = pl.multiple_of((2 * part + which) * span, span)
                    near[pl.ds((2 * i + part) * span, span)] = far[pl.ds(at, span)]

    @pl.when(frame + 1 < pl.num_programs(0))
    def _():
        for copy in fetch(frame + 1, (frame + 1) % 2):
            copy.start()

    slot = frame % 2
    for copy in fetch(frame, slot):
        copy.wait()
    columns = [
        dot3((near_hi[...], near_lo[...]), split(data[slot, c]), ((1,), (1,))) * mask_ref[0]
        for c in range(own)
    ]
    blocks = [v[2 * i * span : (2 * i + 2) * span] for v in columns for i in range(2)]
    sides = []
    for odd in range(2):
        at = odd * half
        stacked = jnp.concatenate(
            [
                jnp.concatenate([v[:span, at : at + half], v[span:, at : at + half]], 1)
                for v in blocks
            ],
            0,
        )
        sides.append(dot3(split(stacked), (row_hi[odd], row_lo[odd])))
    for c in range(own):
        for i, ref in enumerate((keep_ref, send_ref)):
            rows = (2 * c + i) * span
            even, odd = [side[rows : rows + span] for side in sides]
            for part in range(2):
                e = even[:, part * half : (part + 1) * half]
                o = odd[:, part * half : (part + 1) * half]
                ref[c, 0, part] = jnp.concatenate([e + o, e - o], 1)


def weigh_kernel(outer, level, device_ref, maps_ref, kept_ref, got_ref, keep_out, send_out, *refs):
    turned, kept, got, keep, send, arrived, left = refs
    devices, pair_coils, rows, lanes = maps_ref.shape
    own, count = got_ref.shape[:2]
    inner, _, _, cols, length = keep.shape
    inner //= outer

    copies = [
        [
            pltpu.make_async_copy(src.at[:, f], dst.at[:, f], arrived.at[i, f])
            for i, (src, dst) in enumerate(((kept_ref, kept), (got_ref, got)))
        ]
        for f in range(count)
    ]
    for pair in copies:
        for copy in pair:
            copy.start()
    for c in range(pair_coils):
        one = maps_ref[:, c].reshape(length, lanes).T
        turned[c, 0] = one[: lanes // 2]
        turned[c, 1] = one[lanes // 2 :]

    bit, mine = device_ref[0] & 1, (device_ref[0] >> level) & 1
    span = inner * cols
    results = []
    for f in range(count):
        for copy in copies[f]:
            copy.wait()
        for ref, which in ((send, 1 - mine), (keep, mine)):
            for i in range(outer):
                at = pl.ds(pl.multiple_of((2 * i + which) * span, span), span)
                total_re = total_im = 0.0
                for base, first in ((kept, bit * own), (got, (1 - bit) * own)):
                    for c in range(own):
                        s_re, s_im = turned[first + c, 0, at, :], turned[first + c, 1, at, :]
                        b_re, b_im = base[c, f, 0, at, :], base[c, f, 1, at, :]
                        total_re += s_re * b_re + s_im * b_im
                        total_im += s_re * b_im - s_im * b_re
                here = slice(i * inner, (i + 1) * inner)
                ref[here, f, 0] = total_re.reshape(inner, cols, length)
                ref[here, f, 1] = total_im.reshape(inner, cols, length)
        for i, (src, dst) in enumerate(((send, send_out), (keep, keep_out))):
            results.append(pltpu.make_async_copy(src.at[:, f], dst.at[:, f], left.at[i, f]))
            results[-1].start()
    for copy in results:
        copy.wait()


def first_normal_kernel(coils, level, device_ref, got_ref, mask_ref, wave_hi, wave_lo, *refs):
    maps_out, field_out, grad_out, responses = refs[-4:]
    mask_responses(mask_ref, wave_hi, wave_lo, responses)
    blocks, _, groups, _, cols, lanes = got_ref.shape
    devices = 2 * blocks
    mine = (device_ref[0] >> level) & 1
    frames = field_out.shape[0]

    def block(s, g):
        e = ((s >> (level + 1)) << level) | (s & ((1 << level) - 1))
        return got_ref[e, ((s >> level) & 1) ^ mine, g]

    per = (coils + frames) // groups
    width = lanes // per
    for g in range(groups):
        out, base = (maps_out, g * per) if g * per < coils else (field_out, g * per - coils)
        for h in range(devices // per):
            exchanged = lane_exchange([block(h * per + s, g) for s in range(per)], width)
            for c in range(per):
                out[base + c, :, :, h * lanes : (h + 1) * lanes] = exchanged[c]

    gradient_frames(0, maps_out, field_out, responses, grad_out)


def gradient_frames(start, maps_ref, field_ref, responses, grad_out):
    def one(i, _):
        f = start + i
        grad_out[i, 0], grad_out[i, 1] = normal_frame(
            maps_ref, field_ref[f, 0], field_ref[f, 1], frame_tables(responses, f)
        )
        return 0

    lax.fori_loop(0, grad_out.shape[0], one, 0, unroll=2)


def second_normal_kernel(start, maps_ref, field_ref, mask_ref, wave_hi, wave_lo, *refs):
    grad_out, responses = refs[-2:]
    mask_responses(mask_ref, wave_hi, wave_lo, responses)
    gradient_frames(start, maps_ref, field_ref, responses, grad_out)


def steps_kernel(field_ref, grad0_ref, grad1_ref, maps_ref, mask_ref, *refs):
    wave_hi, wave_lo, *terms, out_ref, field, grad, responses = refs
    frames, _, cols, length = field_ref.shape
    devices, _, _, lanes = out_ref.shape
    mask_responses(mask_ref, wave_hi, wave_lo, responses)
    data_term = jnp.concatenate(
        [keep[...] + got[...] for keep, got in zip(terms[0::2], terms[1::2])], 0
    )
    first = jnp.concatenate([grad0_ref[...], grad1_ref[...]], 0)
    field[...] = tv_step(field_ref[...] - step_size * (first - data_term))
    for sweep in range(1, OUTER):

        def one(f, _):
            grad[f, 0], grad[f, 1] = normal_frame(
                maps_ref, field[f, 0], field[f, 1], frame_tables(responses, f)
            )
            return 0

        lax.fori_loop(0, frames, one, 0, unroll=2)
        field[...] = tv_step(field[...] - step_size * (grad[...] - data_term))
    per = frames
    for h in range(devices // per):
        parts = [field[f, :, :, h * lanes : (h + 1) * lanes] for f in range(per)]
        exchanged = lane_exchange(parts, lanes // per)
        for s in range(per):
            out_ref[h * per + s] = exchanged[s]


def rows_out_kernel(chunk_of, frames, got_ref, out_ref, tiles):
    devices, _, cols, lanes = got_ref.shape
    count = tiles.shape[0]
    rows = lanes // frames
    order = sorted(range(devices), key=lambda d: chunk_of[d])
    each = LANES // cols
    for t in range(count):
        at = t % (count // 2) * each
        turned = jnp.concatenate([got_ref[d, t // (count // 2)] for d in order[at : at + each]], 0).T
        for f in range(frames):
            tiles[t, pl.ds(f, rows, stride=frames), :] = turned[f * rows : (f + 1) * rows]
        out_ref[:, t * LANES : (t + 1) * LANES] = tiles[t]


def params(limit=VMEM_LIMIT):
    return pltpu.CompilerParams(vmem_limit_bytes=limit)


def cost(flops, moved):
    return pl.CostEstimate(flops=int(flops), bytes_accessed=int(moved), transcendentals=0)


def whole(shape):
    return pl.BlockSpec(shape, lambda *_: (0,) * len(shape))


def lane_tiles(rows, lanes):
    return [
        pl.BlockSpec((rows, LANES), lambda *_, t=t: (0, t), pipeline_mode=pl.Buffered(1))
        for t in range(lanes // LANES)
    ]


def f32(*shape):
    return jax.ShapeDtypeStruct(shape, jnp.float32)


def exchange(send, bit):
    devices = lax.axis_size("coil")
    return lax.ppermute(send, "coil", [(i, i ^ (1 << bit)) for i in range(devices)])


def halve(keep, got, bit, device):
    mine = (device >> bit) & 1

    def part(which):
        return lax.dynamic_index_in_dim(
            keep, which, bit - 1, keepdims=True
        ) + lax.dynamic_index_in_dim(got, which, bit - 1, keepdims=True)

    send = part(1 - mine)
    return part(mine), send


def kernel_path(image, sens, kspace, mask):
    rows, frames, packed = image.shape
    coils = sens.shape[1]
    length, pairs, _ = kspace.shape
    half = packed // 2
    hl = length // 2
    devices = lax.axis_size("coil")
    device = lax.axis_index("coil")
    bits = devices.bit_length() - 1
    own = pairs // frames
    cols = half // devices
    per = LANES // rows
    groups = (coils + frames) // per
    chunk_of = [sum(((d >> b) & 1) << (bits - 1 - b) for b in range(bits)) for d in range(devices)]

    k = np.arange(length)
    z = np.arange(half)
    y = np.arange(hl)
    col_hi, col_lo = two_terms(packed_left(dft(z, z, half) / np.sqrt(half)))
    lanes_k = [k[0::2], k[1::2]]
    inverse = [packed_right(dft(y, ks, length)) for ks in lanes_k]
    row_hi, row_lo = two_terms(np.stack(inverse) / np.sqrt(length))
    waves = [dft(ks, y, length) * 0.5 / hl for ks in lanes_k]
    wave_hi, wave_lo = two_terms(np.stack([np.concatenate([w.real, w.imag], 1) for w in waves]))

    sampled = mask.astype(jnp.float32)
    mask_sides = jnp.stack([sampled[:, 0::2], sampled[:, 1::2]])
    mask_lanes = jnp.concatenate([mask_sides[0], mask_sides[1]], 1)[:, None, :]

    sens_rows = sens.reshape(rows * coils, packed)
    image_rows = image.reshape(rows * frames, packed)

    with jax.named_scope("coil_maps"):
        blocks = pl.pallas_call(
            functools.partial(coil_blocks_kernel, coils),
            grid=(1,),
            out_shape=f32(devices, 2 * own, rows, half),
            in_specs=lane_tiles(rows * coils, packed),
            out_specs=whole((devices, 2 * own, rows, half)),
            compiler_params=params(),
            cost_estimate=cost(0, 2 * sens.size * 4),
        )(*[sens_rows] * (packed // LANES))
        blocks, device = lax.optimization_barrier((blocks, device))
        coil_maps = lax.all_to_all(blocks, "coil", 0, 0, tiled=True)

    with jax.named_scope("column_maps"):
        level = 1
        block = (devices // 2, groups, 2, cols, LANES)
        column_keep, column_send = pl.pallas_call(
            functools.partial(column_blocks_kernel, coils, frames, chunk_of, level),
            grid=(1,),
            out_shape=(f32(*block),) * 2,
            in_specs=[pl.BlockSpec(memory_space=pltpu.SMEM)]
            + lane_tiles(rows * coils, packed)
            + lane_tiles(rows * frames, packed),
            out_specs=(whole(block),) * 2,
            scratch_shapes=[pltpu.VMEM((2, half, LANES), jnp.float32)],
            compiler_params=params(),
            cost_estimate=cost(0, 2 * (sens.size + image.size) * 4),
        )(device[None], *[sens_rows] * (packed // LANES), *[image_rows] * (packed // LANES))
        column_blocks = jnp.stack([column_keep, exchange(column_send, level)], 1)
        sides = [[with_bit(e, level, side) for e in range(devices // 2)] for side in range(2)]

    plans = [
        (frames // 2, list(range(1, bits))),
        (frames // 2, list(range(1, bits))),
    ]
    firsts = [sum(count for count, _ in plans[:i]) for i in range(len(plans))]
    span = half // 2
    smem = pl.BlockSpec(memory_space=pltpu.SMEM)
    kept, got = [], []
    for start, (count, _) in zip(firsts, plans):
        with jax.named_scope("data_transform"):
            block = pl.BlockSpec((own, 1, 2, span, length), lambda f: (0, f, 0, 0, 0))
            keep, send = pl.pallas_call(
                functools.partial(base_kernel, start, frames),
                grid=(count,),
                out_shape=(f32(own, count, 2, span, length),) * 2,
                in_specs=[
                    smem,
                    pl.BlockSpec(memory_space=pltpu.HBM),
                    pl.BlockSpec((1, 1, length), lambda f, start=start: (start + f, 0, 0)),
                    whole((packed, packed)),
                    whole((packed, packed)),
                    whole((2, length, length)),
                    whole((2, length, length)),
                ],
                out_specs=(block, block),
                scratch_shapes=[
                    pltpu.VMEM((2, own, length, packed), jnp.float32),
                    pltpu.VMEM((packed, packed), jnp.bfloat16),
                    pltpu.VMEM((packed, packed), jnp.bfloat16),
                    pltpu.SemaphoreType.DMA((2, own, 2)),
                ],
                compiler_params=params(TRANSFORM_LIMIT),
                cost_estimate=cost(
                    own * count * 36 * half * half * length, 16 * own * count * half * length
                ),
            )(
                device[None],
                kspace.reshape(hl, 2, pairs, packed),
                mask_lanes,
                col_hi,
                col_lo,
                row_hi,
                row_lo,
            )
        if len(kept) == len(plans) - 1:
            column_blocks, send = lax.optimization_barrier((column_blocks, send))
        kept.append(keep)
        got.append(exchange(send, 0))
    with jax.named_scope("column_maps"):
        column_maps = lax.all_to_all(
            column_blocks, "coil", 0, 0, tiled=True, axis_index_groups=sides
        )

    field = f32(frames, 2, cols, length)
    normal_cost = 6 * 2 * frames * coils * cols * length * length

    responses = pltpu.VMEM((2, frames, length), jnp.float32)

    part = f32(frames // 2, 2, cols, length)
    anywhere = pl.BlockSpec(memory_space=pl.ANY)

    def second_gradient(maps, field0, before):
        return pl.pallas_call(
            functools.partial(second_normal_kernel, frames // 2),
            in_specs=[pl.BlockSpec(memory_space=pltpu.VMEM)] * 5 + [anywhere] * len(before),
            out_shape=part,
            scratch_shapes=[responses],
            compiler_params=params(),
            cost_estimate=cost(normal_cost // 2, 2 * sens.size * 4),
            name="second_gradient",
        )(maps, field0, mask_sides, wave_hi, wave_lo, *before)

    def first_gradient(column_maps, before):
        return pl.pallas_call(
            functools.partial(first_normal_kernel, coils, level),
            in_specs=[smem]
            + [pl.BlockSpec(memory_space=pltpu.VMEM)] * 4
            + [pl.BlockSpec(memory_space=pl.ANY)] * len(before),
            out_shape=(f32(coils, 2, cols, length), field, part),
            scratch_shapes=[responses],
            compiler_params=params(),
            cost_estimate=cost(normal_cost // 2, 4 * sens.size * 4),
            name="first_gradient",
        )(device[None], column_maps, mask_sides, wave_hi, wave_lo, *before)

    with jax.named_scope("data_term"):
        terms = []
        for stream, (count, order) in enumerate(plans):
            outer = 2 ** (order[0] - 1)
            out = f32(devices // 4, count, 2, cols, length)
            vmem, anywhere = pl.BlockSpec(memory_space=pltpu.VMEM), pl.BlockSpec(memory_space=pl.ANY)
            base = pltpu.VMEM((own, count, 2, span, length), jnp.float32)
            term = pltpu.VMEM(out.shape, jnp.float32)
            keep, send = pl.pallas_call(
                functools.partial(weigh_kernel, outer, order[0]),
                out_shape=(out, out),
                in_specs=[smem, vmem, anywhere, anywhere],
                out_specs=(anywhere, anywhere),
                scratch_shapes=[
                    pltpu.VMEM((2 * own, 2, span, length), jnp.float32),
                    base,
                    base,
                    term,
                    term,
                    pltpu.SemaphoreType.DMA((2, count)),
                    pltpu.SemaphoreType.DMA((2, count)),
                ],
                compiler_params=params(WEIGH_LIMIT),
                cost_estimate=cost(0, 2 * kept[stream].size * 4 + 2 * out.size * 4),
            )(device[None], coil_maps, kept[stream], got[stream])
            dims = [2] * (bits - 1)
            dims[order[0] - 1] = 1
            received = exchange(send, order[0]).reshape(*dims, *keep.shape[1:])
            terms.append((keep.reshape(received.shape), received))
        sent = [None] * len(plans)

        def advance(stream, step):
            order = plans[stream][1]
            keep, sent[stream] = halve(*terms[stream], order[step], device)
            terms[stream] = (keep, exchange(sent[stream], order[step]))

        for step in range(1, bits - 2):
            for stream in range(len(plans)):
                advance(stream, step)
        advance(0, bits - 2)
        maps, field0, early = first_gradient(column_maps, sent)
        terms[1], early = lax.optimization_barrier((terms[1], early))
        advance(1, bits - 2)
        late = second_gradient(maps, field0, sent[1:])
        terms = [value.reshape(-1, 2, cols, length) for term in terms for value in term]

    with jax.named_scope("outer_steps"):
        blocks = pl.pallas_call(
            steps_kernel,
            out_shape=f32(devices, 2, cols, LANES),
            scratch_shapes=[pltpu.VMEM(field.shape, jnp.float32)] * 2 + [responses],
            compiler_params=params(),
            cost_estimate=cost(normal_cost, 4 * sens.size * 4),
        )(field0, early, late, maps, mask_sides, wave_hi, wave_lo, *terms)

    with jax.named_scope("result_rows"):
        got = lax.all_to_all(blocks, "coil", 0, 0, tiled=True)
        recon = pl.pallas_call(
            functools.partial(rows_out_kernel, chunk_of, frames),
            out_shape=f32(rows * frames, packed),
            scratch_shapes=[pltpu.VMEM((packed // LANES, rows * frames, LANES), jnp.float32)],
            compiler_params=params(),
            cost_estimate=cost(0, 2 * image.size * 4),
        )(got)
    return recon.reshape(rows, frames, packed)


def einsum(form, left, right):
    return jnp.einsum(form, left, right, precision=highest, preferred_element_type=jnp.float32)


def complex_einsum(form, left, right):
    (a, b), (c, d) = left, right
    return (
        einsum(form, a, c) - einsum(form, b, d),
        einsum(form, a, d) + einsum(form, b, c),
    )


def general_path(image, sens, kspace, mask):
    rows, frames, packed = image.shape
    coils = sens.shape[1]
    length, pairs, _ = kspace.shape
    half = packed // 2
    devices = lax.axis_size("coil")
    device = lax.axis_index("coil")
    cols = half // devices

    def table(size):
        values = dft(np.arange(size), np.arange(size), size) / np.sqrt(size)
        return jnp.asarray(values.real, jnp.float32), jnp.asarray(values.imag, jnp.float32)

    inverse_rows, inverse_cols = table(length), table(half)
    forward_rows = (inverse_rows[0], -inverse_rows[1])

    both = jnp.concatenate([sens, image], 1).reshape(rows, coils + frames, 2, devices, cols)
    both = lax.all_to_all(both.transpose(3, 1, 2, 4, 0), "coil", 0, 0, tiled=True)
    both = both.transpose(1, 2, 3, 0, 4).reshape(coils + frames, 2, cols, length)
    maps, field = both[:coils], both[coils:]

    own = max(1, pairs // frames)
    repeats = devices * own // coils
    spread = jnp.repeat(sens.reshape(rows, coils // own, own, packed), repeats, axis=1)
    spread = spread.transpose(1, 0, 2, 3)
    coil_maps = lax.all_to_all(spread, "coil", 0, 0, tiled=True).reshape(length, own, packed)

    ids = device * pairs + lax.iota(jnp.int32, pairs)
    onehot = (ids[:, None] % frames == lax.iota(jnp.int32, frames)[None, :]).astype(jnp.float32)
    sampled = mask.astype(jnp.float32)
    data = einsum("pf,fk->kp", onehot, sampled)[:, :, None] * kspace
    data = (data[..., :half], data[..., half:])
    data = complex_einsum("kpz,zx->kpx", data, inverse_cols)
    data = complex_einsum("yk,kpx->ypx", inverse_rows, data)
    pair_maps = jnp.repeat(coil_maps, pairs // own, axis=1)
    m_re, m_im = pair_maps[..., :half], pair_maps[..., half:]
    weighted = jnp.stack(
        [m_re * data[0] + m_im * data[1], m_re * data[1] - m_im * data[0]], 2
    ).reshape(length, pairs, 2, devices, cols)
    term = einsum("ypcdx,pf->dfcxy", weighted, onehot)
    term = lax.psum_scatter(term, "coil", scatter_dimension=0, tiled=True)[0]

    masked = (
        sampled[:, :, None] * forward_rows[0][None],
        sampled[:, :, None] * forward_rows[1][None],
    )
    project = complex_einsum("yk,fkv->fyv", inverse_rows, masked)
    for sweep in range(OUTER):
        u_re = maps[:, None, 0] * field[None, :, 0] - maps[:, None, 1] * field[None, :, 1]
        u_im = maps[:, None, 0] * field[None, :, 1] + maps[:, None, 1] * field[None, :, 0]
        v_re, v_im = complex_einsum("fyv,cfxv->cfxy", project, (u_re, u_im))
        grad = jnp.stack(
            [
                jnp.sum(maps[:, None, 0] * v_re + maps[:, None, 1] * v_im, 0),
                jnp.sum(maps[:, None, 0] * v_im - maps[:, None, 1] * v_re, 0),
            ],
            1,
        )
        target = field - step_size * (grad - term)
        dual_time = jnp.zeros_like(target)
        dual_rows = jnp.zeros_like(target)
        field = target
        for repeat in range(INNER):
            diff_time = jnp.concatenate([field[1:] - field[:-1], jnp.zeros_like(field[:1])], 0)
            diff_rows = jnp.concatenate(
                [field[..., 1:] - field[..., :-1], jnp.zeros_like(field[..., :1])], -1
            )
            dual_time = jnp.clip(dual_time + dual_step * diff_time, -1.0, 1.0)
            dual_rows = jnp.clip(dual_rows + dual_step * diff_rows, -1.0, 1.0)
            inner_time, inner_rows = dual_time[:-1], dual_rows[..., :-1]
            none_time, none_rows = jnp.zeros_like(field[:1]), jnp.zeros_like(field[..., :1])
            divergence = (
                jnp.concatenate([none_time, inner_time], 0)
                - jnp.concatenate([inner_time, none_time], 0)
                + jnp.concatenate([none_rows, inner_rows], -1)
                - jnp.concatenate([inner_rows, none_rows], -1)
            )
            field = target - tv_weight * divergence

    result = field.reshape(frames, 2, cols, devices, rows).transpose(3, 0, 1, 2, 4)
    result = lax.all_to_all(result, "coil", 0, 0, tiled=True)
    return result.transpose(4, 1, 2, 0, 3).reshape(rows, frames, packed)


def fits_kernels(image, sens, kspace, devices):
    rows, frames, packed = image.shape
    coils = sens.shape[1]
    length, pairs, _ = kspace.shape
    per = LANES // rows
    return (
        devices & (devices - 1) == 0
        and devices >= 4
        and rows % 8 == 0
        and rows * per == LANES
        and frames == per
        and frames % 2 == 0
        and coils % per == 0
        and devices % per == 0
        and pairs % frames == 0
        and pairs * devices == coils * frames
        and length == 2 * LANES
        and packed % (16 * devices) == 0
        and packed % (4 * LANES) == 0
    )


def per_device(image, sens, kspace, mask):
    if fits_kernels(image, sens, kspace, lax.axis_size("coil")):
        return kernel_path(image, sens, kspace, mask)
    return general_path(image, sens, kspace, mask)


def solution(mesh):
    return jax.shard_map(
        per_device,
        mesh=mesh,
        in_specs=(
            P(("plane", "coil"), None, None),
            P(("plane", "coil"), None, None),
            P("plane", "coil", None),
            P(),
        ),
        out_specs=P(("plane", "coil"), None, None),
        check_vma=False,
    )
```

```python
import functools

import jax
import jax.numpy as jnp
import ml_dtypes
import numpy as np
from jax import lax
from jax.experimental import pallas as pl
from jax.experimental.pallas import tpu as pltpu
from jax.sharding import PartitionSpec as P

OUTER = 2
INNER = 2
LANES = 128
VMEM_LIMIT = 16 * 1024 * 1024
TRANSFORM_LIMIT = 52 * 1024 * 1024
WEIGH_LIMIT = 60 * 1024 * 1024

step_size = 0.5
tv_weight = 0.1
dual_step = 1.25
highest = lax.Precision.HIGHEST


def two_terms(table):
    first = table.astype(ml_dtypes.bfloat16)
    second = (table - first.astype(np.float64)).astype(ml_dtypes.bfloat16)
    return first, second


def dft(out_index, in_index, length):
    product = np.outer(out_index, in_index) % length
    return np.exp(2j * np.pi / length * product)


def packed_left(matrix):
    return np.block([[matrix.real, -matrix.imag], [matrix.imag, matrix.real]])


def packed_right(matrix):
    return packed_left(matrix).T


def split(value):
    first = value.astype(jnp.bfloat16)
    second = (value - first.astype(jnp.float32)).astype(jnp.bfloat16)
    return first, second


def dot3(left, right, contract=((1,), (0,))):
    dims = (contract, ((), ()))

    return lax.dot_general(
        jnp.concatenate([left[0], left[0], left[1]], contract[0][0]),
        jnp.concatenate([right[0], right[1], right[0]], contract[1][0]),
        dims,
        preferred_element_type=jnp.float32,
    )


def lane_exchange(parts, width):
    parts = list(parts)
    lane = lax.broadcasted_iota(jnp.int32, parts[0].shape, parts[0].ndim - 1)
    axis = parts[0].ndim - 1
    bit = 1
    while bit < len(parts):
        odd = (lane // width) & bit != 0
        for s in range(len(parts)):
            if s & bit:
                continue
            low, high = parts[s], parts[s | bit]
            parts[s] = jnp.where(odd, pltpu.roll(high, width * bit, axis), low)
            parts[s | bit] = jnp.where(odd, high, pltpu.roll(low, LANES - width * bit, axis))
        bit *= 2
    return parts


def roll_last(value, distance):
    shape = value.shape
    flat = value.reshape(-1, shape[-1])
    return pltpu.roll(flat, distance % shape[-1], 1).reshape(shape)


def tv_step(target):
    length = target.shape[-1]
    row = lax.broadcasted_iota(jnp.int32, target.shape, target.ndim - 1)
    last, first = row == length - 1, row == 0
    nothing = jnp.zeros_like(target[:1])

    def adjoint(dual_time, dual_rows):
        from_time = jnp.concatenate([nothing, dual_time[:-1]], 0) - jnp.concatenate(
            [dual_time[:-1], nothing], 0
        )
        from_rows = jnp.where(first, 0.0, roll_last(dual_rows, 1)) - jnp.where(last, 0.0, dual_rows)
        return from_time + from_rows

    dual_time = jnp.zeros_like(target)
    dual_rows = jnp.zeros_like(target)
    primal = target
    for repeat in range(INNER):
        diff_time = jnp.concatenate([primal[1:] - primal[:-1], nothing], 0)
        diff_rows = jnp.where(last, 0.0, roll_last(primal, -1) - primal)
        dual_time = jnp.clip(dual_time + dual_step * diff_time, -1.0, 1.0)
        dual_rows = jnp.clip(dual_rows + dual_step * diff_rows, -1.0, 1.0)
        primal = target - tv_weight * adjoint(dual_time, dual_rows)
    return primal


def mask_responses(mask_ref, wave_hi, wave_lo, out_ref):
    for side in range(2):
        mask = mask_ref[side].astype(jnp.bfloat16)
        terms = [
            jnp.dot(mask, wave[side], preferred_element_type=jnp.float32)
            for wave in (wave_hi, wave_lo)
        ]
        out_ref[side] = terms[0] + terms[1]


def frame_tables(response_ref, f):
    half = response_ref.shape[-1] // 2
    tables = []
    for side in range(2):
        row = response_ref[side, pl.ds(f, 1), :]
        parts = []
        for at in (0, half):
            spread = jnp.broadcast_to(row[:, at : at + half], (half, half))
            turned = pltpu.roll(spread, 0, 1, stride=1, stride_axis=0)
            if side:
                before = lax.broadcasted_iota(jnp.int32, (half, half), 1) < (
                    lax.broadcasted_iota(jnp.int32, (half, half), 0)
                )
                turned = jnp.where(before, -turned, turned)
            parts.append(turned)
        re, im = parts
        tables.append(
            split(jnp.concatenate([jnp.concatenate([re, im], 1), jnp.concatenate([-im, re], 1)], 0))
        )
    return tables


def normal_frame(maps_ref, field_re, field_im, tables):
    coils, _, cols, length = maps_ref.shape
    half = length // 2
    maps_re, maps_im = maps_ref[:, 0], maps_ref[:, 1]
    u_re = maps_re * field_re[None] - maps_im * field_im[None]
    u_im = maps_re * field_im[None] + maps_im * field_re[None]
    flat_re = u_re.reshape(coils * cols, length)
    flat_im = u_im.reshape(coils * cols, length)
    outs = []
    for sign, table in zip((1.0, -1.0), tables):
        packed = jnp.concatenate(
            [
                flat_re[:, :half] + sign * flat_re[:, half:],
                flat_im[:, :half] + sign * flat_im[:, half:],
            ],
            1,
        )
        outs.append(dot3(split(packed), table))
    plus, minus = outs
    v_re = jnp.concatenate(
        [plus[:, :half] + minus[:, :half], plus[:, :half] - minus[:, :half]], 1
    ).reshape(coils, cols, length)
    v_im = jnp.concatenate(
        [plus[:, half:] + minus[:, half:], plus[:, half:] - minus[:, half:]], 1
    ).reshape(coils, cols, length)
    return (
        jnp.sum(maps_re * v_re + maps_im * v_im, 0),
        jnp.sum(maps_re * v_im - maps_im * v_re, 0),
    )


def coil_blocks_kernel(coils, *refs):
    *tiles, out_ref = refs
    devices, pair_coils, rows, lanes = out_ref.shape
    halves = len(tiles) // 2
    each = lanes // (2 * LANES)
    for d in range(devices):
        for c in range(pair_coils):
            for part in range(2):
                for t in range(each):
                    at = (part * each + t) * LANES
                    out_ref[d, c, :, at : at + LANES] = tiles[part * halves + (d & 1) * each + t][
                        pl.ds((d >> 1) * pair_coils + c, rows, stride=coils), :
                    ]


def with_bit(index, bit, value):
    return ((index >> bit) << (bit + 1)) | (value << bit) | (index & ((1 << bit) - 1))


def column_blocks_kernel(coils, frames, chunk_of, level, device_ref, *refs):
    *tiles, keep_ref, send_ref, turned = refs
    sens_tiles, image_tiles = tiles[: len(tiles) // 2], tiles[len(tiles) // 2 :]
    blocks, early, _, cols, _ = send_ref.shape
    groups = (keep_ref.shape[1] + early) // 2
    rows = sens_tiles[0].shape[0] // coils
    per = LANES // rows
    half = len(sens_tiles) // 2
    mine = (device_ref[0] >> level) & 1
    far = chunk_of[1 << level] * cols
    for g in range(groups):
        if g * per < coils:
            tiles, count, base = sens_tiles, coils, g * per
        else:
            tiles, count, base = image_tiles, frames, g * per - coils
        for t, ref in enumerate(tiles):
            turned[t // half, pl.ds(t % half * LANES, LANES)] = jnp.concatenate(
                [ref[pl.ds(base + c, rows, stride=count), :] for c in range(per)], 0
            ).T
        other = (send_ref, g) if g < early else (keep_ref, g + groups - early)
        for (out, unit), side in (((keep_ref, g), mine), (other, 1 - mine)):
            for e in range(blocks):
                at = pl.multiple_of(chunk_of[with_bit(e, level, 0)] * cols + side * far, cols)
                for part in range(2):
                    out[e, unit, part] = turned[part, pl.ds(at, cols)]


def base_kernel(start, frames, device_ref, kspace_ref, mask_ref, *refs):
    col_hi, col_lo, row_hi, row_lo, keep_ref, send_ref, data, near_hi, near_lo, arrived = refs
    own, _, _, span, length = keep_ref.shape
    bit = device_ref[0] & 1
    half = length // 2
    frame = pl.program_id(0)

    def fetch(f, slot):
        return [
            pltpu.make_async_copy(
                kspace_ref.at[:, odd, start + f + c * frames, :],
                data.at[slot, c, pl.ds(odd * half, half)],
                arrived.at[slot, c, odd],
            )
            for c in range(own)
            for odd in range(2)
        ]

    @pl.when(frame == 0)
    def _():
        for copy in fetch(0, 0):
            copy.start()
        for far, near in ((col_hi, near_hi), (col_lo, near_lo)):
            for i, which in enumerate((bit, 1 - bit)):
                for part in range(2):
                    at = pl.multiple_of((2 * part + which) * span, span)
                    near[pl.ds((2 * i + part) * span, span)] = far[pl.ds(at, span)]

    @pl.when(frame + 1 < pl.num_programs(0))
    def _():
        for copy in fetch(frame + 1, (frame + 1) % 2):
            copy.start()

    slot = frame % 2
    for copy in fetch(frame, slot):
        copy.wait()
    columns = [
        dot3((near_hi[...], near_lo[...]), split(data[slot, c]), ((1,), (1,))) * mask_ref[0]
        for c in range(own)
    ]
    blocks = [v[2 * i * span : (2 * i + 2) * span] for v in columns for i in range(2)]
    sides = []
    for odd in range(2):
        at = odd * half
        stacked = jnp.concatenate(
            [
                jnp.concatenate([v[:span, at : at + half], v[span:, at : at + half]], 1)
                for v in blocks
            ],
            0,
        )
        sides.append(dot3(split(stacked), (row_hi[odd], row_lo[odd])))
    for c in range(own):
        for i, ref in enumerate((keep_ref, send_ref)):
            rows = (2 * c + i) * span
            even, odd = [side[rows : rows + span] for side in sides]
            for part in range(2):
                e = even[:, part * half : (part + 1) * half]
                o = odd[:, part * half : (part + 1) * half]
                ref[c, 0, part] = jnp.concatenate([e + o, e - o], 1)


def weigh_kernel(outer, level, flip, device_ref, maps_ref, kept_ref, got_ref, out_ref, *refs):
    turned, kept, got, total, arrived, left = refs
    devices, pair_coils, rows, lanes = maps_ref.shape
    own, count = got_ref.shape[:2]
    inner, _, _, cols, length = total.shape
    inner //= outer
    span = inner * cols
    bit, which = device_ref[0] & 1, ((device_ref[0] >> level) & 1) ^ flip
    far = [pl.multiple_of((2 * i + which) * span, span) for i in range(outer)]

    copies = [
        [
            pltpu.make_async_copy(
                src.at[:, f, :, pl.ds(far[i], span)],
                dst.at[:, f, :, pl.ds(i * span, span)],
                arrived.at[j, f, i],
            )
            for j, (src, dst) in enumerate(((kept_ref, kept), (got_ref, got)))
            for i in range(outer)
        ]
        for f in range(count)
    ]
    for group in copies:
        for copy in group:
            copy.start()
    for c in range(pair_coils):
        one = maps_ref[:, c].reshape(length, lanes).T
        turned[c, 0] = one[: lanes // 2]
        turned[c, 1] = one[lanes // 2 :]

    results = []
    for f in range(count):
        for copy in copies[f]:
            copy.wait()
        for i in range(outer):
            here = slice(i * span, (i + 1) * span)
            total_re = total_im = 0.0
            for base, first in ((kept, bit * own), (got, (1 - bit) * own)):
                for c in range(own):
                    s_re = turned[first + c, 0, pl.ds(far[i], span), :]
                    s_im = turned[first + c, 1, pl.ds(far[i], span), :]
                    b_re, b_im = base[c, f, 0, here, :], base[c, f, 1, here, :]
                    total_re += s_re * b_re + s_im * b_im
                    total_im += s_re * b_im - s_im * b_re
            total[i * inner : (i + 1) * inner, f, 0] = total_re.reshape(inner, cols, length)
            total[i * inner : (i + 1) * inner, f, 1] = total_im.reshape(inner, cols, length)
        results.append(pltpu.make_async_copy(total.at[:, f], out_ref.at[:, f], left.at[f]))
        results[-1].start()
    for copy in results:
        copy.wait()


def first_normal_kernel(
    coils, level, device_ref, got_ref, late_ref, mask_ref, wave_hi, wave_lo, *refs
):
    maps_out, field_out, grad_out, responses = refs[-4:]
    mask_responses(mask_ref, wave_hi, wave_lo, responses)
    blocks, units, _, cols, lanes = got_ref.shape
    groups = units // 2
    early = groups - late_ref.shape[1]
    devices = 2 * blocks
    mine = (device_ref[0] >> level) & 1
    frames = field_out.shape[0]

    def block(s, g):
        e = ((s >> (level + 1)) << level) | (s & ((1 << level) - 1))
        across = ((s >> level) & 1) ^ mine
        if g < early:
            return got_ref[e, g + across * (units - early)]
        return jnp.where(across == 0, got_ref[e, g], late_ref[e, g - early])

    per = (coils + frames) // groups
    width = lanes // per
    for g in range(groups):
        out, base = (maps_out, g * per) if g * per < coils else (field_out, g * per - coils)
        for h in range(devices // per):
            exchanged = lane_exchange([block(h * per + s, g) for s in range(per)], width)
            for c in range(per):
                out[base + c, :, :, h * lanes : (h + 1) * lanes] = exchanged[c]

    def one(f, _):
        grad_out[f, 0], grad_out[f, 1] = normal_frame(
            maps_out, field_out[f, 0], field_out[f, 1], frame_tables(responses, f)
        )
        return 0

    lax.fori_loop(0, frames, one, 0, unroll=2)


def steps_kernel(field_ref, grad_ref, maps_ref, mask_ref, *refs):
    wave_hi, wave_lo, *terms, out_ref, field, grad, responses = refs
    frames, _, cols, length = field_ref.shape
    devices, _, _, lanes = out_ref.shape
    mask_responses(mask_ref, wave_hi, wave_lo, responses)
    data_term = jnp.concatenate(
        [keep[...] + got[...] for keep, got in zip(terms[0::2], terms[1::2])], 0
    )
    field[...] = tv_step(field_ref[...] - step_size * (grad_ref[...] - data_term))
    for sweep in range(1, OUTER):

        def one(f, _):
            grad[f, 0], grad[f, 1] = normal_frame(
                maps_ref, field[f, 0], field[f, 1], frame_tables(responses, f)
            )
            return 0

        lax.fori_loop(0, frames, one, 0, unroll=2)
        field[...] = tv_step(field[...] - step_size * (grad[...] - data_term))
    per = frames
    for h in range(devices // per):
        parts = [field[f, :, :, h * lanes : (h + 1) * lanes] for f in range(per)]
        exchanged = lane_exchange(parts, lanes // per)
        for s in range(per):
            out_ref[h * per + s] = exchanged[s]


def rows_out_kernel(chunk_of, frames, got_ref, out_ref, tiles):
    devices, _, cols, lanes = got_ref.shape
    count = tiles.shape[0]
    rows = lanes // frames
    order = sorted(range(devices), key=lambda d: chunk_of[d])
    each = LANES // cols
    for t in range(count):
        at = t % (count // 2) * each
        turned = jnp.concatenate([got_ref[d, t // (count // 2)] for d in order[at : at + each]], 0).T
        for f in range(frames):
            tiles[t, pl.ds(f, rows, stride=frames), :] = turned[f * rows : (f + 1) * rows]
        out_ref[:, t * LANES : (t + 1) * LANES] = tiles[t]


def params(limit=VMEM_LIMIT):
    return pltpu.CompilerParams(vmem_limit_bytes=limit)


def cost(flops, moved):
    return pl.CostEstimate(flops=int(flops), bytes_accessed=int(moved), transcendentals=0)


def whole(shape):
    return pl.BlockSpec(shape, lambda *_: (0,) * len(shape))


def lane_tiles(rows, lanes):
    return [
        pl.BlockSpec((rows, LANES), lambda *_, t=t: (0, t), pipeline_mode=pl.Buffered(1))
        for t in range(lanes // LANES)
    ]


def f32(*shape):
    return jax.ShapeDtypeStruct(shape, jnp.float32)


def exchange(send, bit):
    devices = lax.axis_size("coil")
    return lax.ppermute(send, "coil", [(i, i ^ (1 << bit)) for i in range(devices)])


def halve(keep, got, bit, device):
    mine = (device >> bit) & 1

    def part(which):
        return lax.dynamic_index_in_dim(
            keep, which, bit - 1, keepdims=True
        ) + lax.dynamic_index_in_dim(got, which, bit - 1, keepdims=True)

    send = part(1 - mine)
    return part(mine), send


def kernel_path(image, sens, kspace, mask):
    rows, frames, packed = image.shape
    coils = sens.shape[1]
    length, pairs, _ = kspace.shape
    half = packed // 2
    hl = length // 2
    devices = lax.axis_size("coil")
    device = lax.axis_index("coil")
    bits = devices.bit_length() - 1
    own = pairs // frames
    cols = half // devices
    per = LANES // rows
    groups = (coils + frames) // per
    chunk_of = [sum(((d >> b) & 1) << (bits - 1 - b) for b in range(bits)) for d in range(devices)]

    k = np.arange(length)
    z = np.arange(half)
    y = np.arange(hl)
    col_hi, col_lo = two_terms(packed_left(dft(z, z, half) / np.sqrt(half)))
    lanes_k = [k[0::2], k[1::2]]
    inverse = [packed_right(dft(y, ks, length)) for ks in lanes_k]
    row_hi, row_lo = two_terms(np.stack(inverse) / np.sqrt(length))
    waves = [dft(ks, y, length) * 0.5 / hl for ks in lanes_k]
    wave_hi, wave_lo = two_terms(np.stack([np.concatenate([w.real, w.imag], 1) for w in waves]))

    sampled = mask.astype(jnp.float32)
    mask_sides = jnp.stack([sampled[:, 0::2], sampled[:, 1::2]])
    mask_lanes = jnp.concatenate([mask_sides[0], mask_sides[1]], 1)[:, None, :]

    sens_rows = sens.reshape(rows * coils, packed)
    image_rows = image.reshape(rows * frames, packed)

    with jax.named_scope("coil_maps"):
        blocks = pl.pallas_call(
            functools.partial(coil_blocks_kernel, coils),
            grid=(1,),
            out_shape=f32(devices, 2 * own, rows, half),
            in_specs=lane_tiles(rows * coils, packed),
            out_specs=whole((devices, 2 * own, rows, half)),
            compiler_params=params(),
            cost_estimate=cost(0, 2 * sens.size * 4),
        )(*[sens_rows] * (packed // LANES))
        blocks, device = lax.optimization_barrier((blocks, device))
        coil_maps = lax.all_to_all(blocks, "coil", 0, 0, tiled=True)

    with jax.named_scope("column_maps"):
        level = 1
        early = (groups + 1) // 2
        keep_block = (devices // 2, 2 * groups - early, 2, cols, LANES)
        send_block = (devices // 2, early, 2, cols, LANES)
        column_keep, column_send = pl.pallas_call(
            functools.partial(column_blocks_kernel, coils, frames, chunk_of, level),
            grid=(1,),
            out_shape=(f32(*keep_block), f32(*send_block)),
            in_specs=[pl.BlockSpec(memory_space=pltpu.SMEM)]
            + lane_tiles(rows * coils, packed)
            + lane_tiles(rows * frames, packed),
            out_specs=(whole(keep_block), whole(send_block)),
            scratch_shapes=[pltpu.VMEM((2, half, LANES), jnp.float32)],
            compiler_params=params(),
            cost_estimate=cost(0, 2 * (sens.size + image.size) * 4),
        )(device[None], *[sens_rows] * (packed // LANES), *[image_rows] * (packed // LANES))
        column_send, device = lax.optimization_barrier((column_send, device))
        column_blocks = jnp.concatenate([column_keep, exchange(column_send, level)], 1)
        sides = [[with_bit(e, level, side) for e in range(devices // 2)] for side in range(2)]

    plans = [
        (frames // 2, list(range(1, bits))),
        (frames // 2, list(range(1, bits))),
    ]
    firsts = [sum(count for count, _ in plans[:i]) for i in range(len(plans))]
    span = half // 2
    smem = pl.BlockSpec(memory_space=pltpu.SMEM)
    kept, got = [], []
    for start, (count, _) in zip(firsts, plans):
        with jax.named_scope("data_transform"):
            block = pl.BlockSpec((own, 1, 2, span, length), lambda f: (0, f, 0, 0, 0))
            keep, send = pl.pallas_call(
                functools.partial(base_kernel, start, frames),
                grid=(count,),
                out_shape=(f32(own, count, 2, span, length),) * 2,
                in_specs=[
                    smem,
                    pl.BlockSpec(memory_space=pltpu.HBM),
                    pl.BlockSpec((1, 1, length), lambda f, start=start: (start + f, 0, 0)),
                    whole((packed, packed)),
                    whole((packed, packed)),
                    whole((2, length, length)),
                    whole((2, length, length)),
                ],
                out_specs=(block, block),
                scratch_shapes=[
                    pltpu.VMEM((2, own, length, packed), jnp.float32),
                    pltpu.VMEM((packed, packed), jnp.bfloat16),
                    pltpu.VMEM((packed, packed), jnp.bfloat16),
                    pltpu.SemaphoreType.DMA((2, own, 2)),
                ],
                compiler_params=params(TRANSFORM_LIMIT),
                cost_estimate=cost(
                    own * count * 36 * half * half * length, 16 * own * count * half * length
                ),
            )(
                device[None],
                kspace.reshape(hl, 2, pairs, packed),
                mask_lanes,
                col_hi,
                col_lo,
                row_hi,
                row_lo,
            )
        if len(kept) == len(plans) - 1:
            column_blocks, send = lax.optimization_barrier((column_blocks, send))
        kept.append(keep)
        got.append(exchange(send, 0))
    with jax.named_scope("column_maps"):
        column_maps = lax.all_to_all(
            column_blocks, "coil", 0, 0, tiled=True, axis_index_groups=sides
        )
        column_late = exchange(column_maps[:, groups : 2 * groups - early], level)

    field = f32(frames, 2, cols, length)
    normal_cost = 6 * 2 * frames * coils * cols * length * length

    responses = pltpu.VMEM((2, frames, length), jnp.float32)

    anywhere = pl.BlockSpec(memory_space=pl.ANY)

    def first_gradient(column_maps, before):
        return pl.pallas_call(
            functools.partial(first_normal_kernel, coils, level),
            in_specs=[smem]
            + [pl.BlockSpec(memory_space=pltpu.VMEM)] * 5
            + [pl.BlockSpec(memory_space=pl.ANY)] * len(before),
            out_shape=(f32(coils, 2, cols, length), field, field),
            scratch_shapes=[responses],
            compiler_params=params(),
            cost_estimate=cost(normal_cost, 4 * sens.size * 4),
            name="first_gradient",
        )(device[None], column_maps, column_late, mask_sides, wave_hi, wave_lo, *before)

    with jax.named_scope("data_term"):

        def weigh(stream, flip):
            count, order = plans[stream]
            outer = 2 ** (order[0] - 1)
            out = f32(devices // 4, count, 2, cols, length)
            vmem, anywhere = pl.BlockSpec(memory_space=pltpu.VMEM), pl.BlockSpec(memory_space=pl.ANY)
            base = pltpu.VMEM((own, count, 2, span // 2, length), jnp.float32)
            value = pl.pallas_call(
                functools.partial(weigh_kernel, outer, order[0], flip),
                out_shape=out,
                in_specs=[smem, vmem, anywhere, anywhere],
                out_specs=anywhere,
                scratch_shapes=[
                    pltpu.VMEM((2 * own, 2, span, length), jnp.float32),
                    base,
                    base,
                    pltpu.VMEM(out.shape, jnp.float32),
                    pltpu.SemaphoreType.DMA((2, count, outer)),
                    pltpu.SemaphoreType.DMA((count,)),
                ],
                compiler_params=params(WEIGH_LIMIT),
                cost_estimate=cost(0, kept[stream].size * 4 + out.size * 4),
            )(device[None], coil_maps, kept[stream], got[stream])
            dims = [2] * (bits - 1)
            dims[order[0] - 1] = 1
            return value.reshape(*dims, *out.shape[1:])

        received = [exchange(weigh(i, 1), plans[i][1][0]) for i in range(len(plans))]
        terms = [(weigh(i, 0), received[i]) for i in range(len(plans))]
        sent = [None] * len(plans)

        def advance(stream, step):
            order = plans[stream][1]
            keep, sent[stream] = halve(*terms[stream], order[step], device)
            terms[stream] = (keep, exchange(sent[stream], order[step]))

        for step in range(1, bits - 1):
            for stream in range(len(plans)):
                advance(stream, step)
        maps, field0, grad0 = first_gradient(column_maps, sent)
        terms = [value.reshape(-1, 2, cols, length) for term in terms for value in term]

    with jax.named_scope("outer_steps"):
        blocks = pl.pallas_call(
            steps_kernel,
            out_shape=f32(devices, 2, cols, LANES),
            scratch_shapes=[pltpu.VMEM(field.shape, jnp.float32)] * 2 + [responses],
            compiler_params=params(),
            cost_estimate=cost(normal_cost, 4 * sens.size * 4),
        )(field0, grad0, maps, mask_sides, wave_hi, wave_lo, *terms)

    with jax.named_scope("result_rows"):
        got = lax.all_to_all(blocks, "coil", 0, 0, tiled=True)
        recon = pl.pallas_call(
            functools.partial(rows_out_kernel, chunk_of, frames),
            out_shape=f32(rows * frames, packed),
            scratch_shapes=[pltpu.VMEM((packed // LANES, rows * frames, LANES), jnp.float32)],
            compiler_params=params(),
            cost_estimate=cost(0, 2 * image.size * 4),
        )(got)
    return recon.reshape(rows, frames, packed)


def einsum(form, left, right):
    return jnp.einsum(form, left, right, precision=highest, preferred_element_type=jnp.float32)


def complex_einsum(form, left, right):
    (a, b), (c, d) = left, right
    return (
        einsum(form, a, c) - einsum(form, b, d),
        einsum(form, a, d) + einsum(form, b, c),
    )


def general_path(image, sens, kspace, mask):
    rows, frames, packed = image.shape
    coils = sens.shape[1]
    length, pairs, _ = kspace.shape
    half = packed // 2
    devices = lax.axis_size("coil")
    device = lax.axis_index("coil")
    cols = half // devices

    def table(size):
        values = dft(np.arange(size), np.arange(size), size) / np.sqrt(size)
        return jnp.asarray(values.real, jnp.float32), jnp.asarray(values.imag, jnp.float32)

    inverse_rows, inverse_cols = table(length), table(half)
    forward_rows = (inverse_rows[0], -inverse_rows[1])

    both = jnp.concatenate([sens, image], 1).reshape(rows, coils + frames, 2, devices, cols)
    both = lax.all_to_all(both.transpose(3, 1, 2, 4, 0), "coil", 0, 0, tiled=True)
    both = both.transpose(1, 2, 3, 0, 4).reshape(coils + frames, 2, cols, length)
    maps, field = both[:coils], both[coils:]

    own = max(1, pairs // frames)
    repeats = devices * own // coils
    spread = jnp.repeat(sens.reshape(rows, coils // own, own, packed), repeats, axis=1)
    spread = spread.transpose(1, 0, 2, 3)
    coil_maps = lax.all_to_all(spread, "coil", 0, 0, tiled=True).reshape(length, own, packed)

    ids = device * pairs + lax.iota(jnp.int32, pairs)
    onehot = (ids[:, None] % frames == lax.iota(jnp.int32, frames)[None, :]).astype(jnp.float32)
    sampled = mask.astype(jnp.float32)
    data = einsum("pf,fk->kp", onehot, sampled)[:, :, None] * kspace
    data = (data[..., :half], data[..., half:])
    data = complex_einsum("kpz,zx->kpx", data, inverse_cols)
    data = complex_einsum("yk,kpx->ypx", inverse_rows, data)
    pair_maps = jnp.repeat(coil_maps, pairs // own, axis=1)
    m_re, m_im = pair_maps[..., :half], pair_maps[..., half:]
    weighted = jnp.stack(
        [m_re * data[0] + m_im * data[1], m_re * data[1] - m_im * data[0]], 2
    ).reshape(length, pairs, 2, devices, cols)
    term = einsum("ypcdx,pf->dfcxy", weighted, onehot)
    term = lax.psum_scatter(term, "coil", scatter_dimension=0, tiled=True)[0]

    masked = (
        sampled[:, :, None] * forward_rows[0][None],
        sampled[:, :, None] * forward_rows[1][None],
    )
    project = complex_einsum("yk,fkv->fyv", inverse_rows, masked)
    for sweep in range(OUTER):
        u_re = maps[:, None, 0] * field[None, :, 0] - maps[:, None, 1] * field[None, :, 1]
        u_im = maps[:, None, 0] * field[None, :, 1] + maps[:, None, 1] * field[None, :, 0]
        v_re, v_im = complex_einsum("fyv,cfxv->cfxy", project, (u_re, u_im))
        grad = jnp.stack(
            [
                jnp.sum(maps[:, None, 0] * v_re + maps[:, None, 1] * v_im, 0),
                jnp.sum(maps[:, None, 0] * v_im - maps[:, None, 1] * v_re, 0),
            ],
            1,
        )
        target = field - step_size * (grad - term)
        dual_time = jnp.zeros_like(target)
        dual_rows = jnp.zeros_like(target)
        field = target
        for repeat in range(INNER):
            diff_time = jnp.concatenate([field[1:] - field[:-1], jnp.zeros_like(field[:1])], 0)
            diff_rows = jnp.concatenate(
                [field[..., 1:] - field[..., :-1], jnp.zeros_like(field[..., :1])], -1
            )
            dual_time = jnp.clip(dual_time + dual_step * diff_time, -1.0, 1.0)
            dual_rows = jnp.clip(dual_rows + dual_step * diff_rows, -1.0, 1.0)
            inner_time, inner_rows = dual_time[:-1], dual_rows[..., :-1]
            none_time, none_rows = jnp.zeros_like(field[:1]), jnp.zeros_like(field[..., :1])
            divergence = (
                jnp.concatenate([none_time, inner_time], 0)
                - jnp.concatenate([inner_time, none_time], 0)
                + jnp.concatenate([none_rows, inner_rows], -1)
                - jnp.concatenate([inner_rows, none_rows], -1)
            )
            field = target - tv_weight * divergence

    result = field.reshape(frames, 2, cols, devices, rows).transpose(3, 0, 1, 2, 4)
    result = lax.all_to_all(result, "coil", 0, 0, tiled=True)
    return result.transpose(4, 1, 2, 0, 3).reshape(rows, frames, packed)


def fits_kernels(image, sens, kspace, devices):
    rows, frames, packed = image.shape
    coils = sens.shape[1]
    length, pairs, _ = kspace.shape
    per = LANES // rows
    return (
        devices & (devices - 1) == 0
        and devices >= 4
        and rows % 8 == 0
        and rows * per == LANES
        and frames == per
        and frames % 2 == 0
        and coils % per == 0
        and devices % per == 0
        and pairs % frames == 0
        and pairs * devices == coils * frames
        and length == 2 * LANES
        and packed % (16 * devices) == 0
        and packed % (4 * LANES) == 0
    )


def per_device(image, sens, kspace, mask):
    if fits_kernels(image, sens, kspace, lax.axis_size("coil")):
        return kernel_path(image, sens, kspace, mask)
    return general_path(image, sens, kspace, mask)


def solution(mesh):
    return jax.shard_map(
        per_device,
        mesh=mesh,
        in_specs=(
            P(("plane", "coil"), None, None),
            P(("plane", "coil"), None, None),
            P("plane", "coil", None),
            P(),
        ),
        out_specs=P(("plane", "coil"), None, None),
        check_vma=False,
    )
```

```python
import functools

import jax
import jax.numpy as jnp
import ml_dtypes
import numpy as np
from jax import lax
from jax.experimental import pallas as pl
from jax.experimental.pallas import tpu as pltpu
from jax.sharding import PartitionSpec as P

OUTER = 2
INNER = 2
LANES = 128
VMEM_LIMIT = 16 * 1024 * 1024
TRANSFORM_LIMIT = 52 * 1024 * 1024
WEIGH_LIMIT = 60 * 1024 * 1024

step_size = 0.5
tv_weight = 0.1
dual_step = 1.25
highest = lax.Precision.HIGHEST


def two_terms(table):
    first = table.astype(ml_dtypes.bfloat16)
    second = (table - first.astype(np.float64)).astype(ml_dtypes.bfloat16)
    return first, second


def dft(out_index, in_index, length):
    product = np.outer(out_index, in_index) % length
    return np.exp(2j * np.pi / length * product)


def packed_left(matrix):
    return np.block([[matrix.real, -matrix.imag], [matrix.imag, matrix.real]])


def packed_right(matrix):
    return packed_left(matrix).T


def split(value):
    first = value.astype(jnp.bfloat16)
    second = (value - first.astype(jnp.float32)).astype(jnp.bfloat16)
    return first, second


def dot3(left, right, contract=((1,), (0,))):
    dims = (contract, ((), ()))

    return lax.dot_general(
        jnp.concatenate([left[0], left[0], left[1]], contract[0][0]),
        jnp.concatenate([right[0], right[1], right[0]], contract[1][0]),
        dims,
        preferred_element_type=jnp.float32,
    )


def lane_exchange(parts, width):
    parts = list(parts)
    lane = lax.broadcasted_iota(jnp.int32, parts[0].shape, parts[0].ndim - 1)
    axis = parts[0].ndim - 1
    bit = 1
    while bit < len(parts):
        odd = (lane // width) & bit != 0
        for s in range(len(parts)):
            if s & bit:
                continue
            low, high = parts[s], parts[s | bit]
            parts[s] = jnp.where(odd, pltpu.roll(high, width * bit, axis), low)
            parts[s | bit] = jnp.where(odd, high, pltpu.roll(low, LANES - width * bit, axis))
        bit *= 2
    return parts


def roll_last(value, distance):
    shape = value.shape
    flat = value.reshape(-1, shape[-1])
    return pltpu.roll(flat, distance % shape[-1], 1).reshape(shape)


def tv_step(target):
    length = target.shape[-1]
    row = lax.broadcasted_iota(jnp.int32, target.shape, target.ndim - 1)
    last, first = row == length - 1, row == 0
    nothing = jnp.zeros_like(target[:1])

    def adjoint(dual_time, dual_rows):
        from_time = jnp.concatenate([nothing, dual_time[:-1]], 0) - jnp.concatenate(
            [dual_time[:-1], nothing], 0
        )
        from_rows = jnp.where(first, 0.0, roll_last(dual_rows, 1)) - jnp.where(last, 0.0, dual_rows)
        return from_time + from_rows

    dual_time = jnp.zeros_like(target)
    dual_rows = jnp.zeros_like(target)
    primal = target
    for repeat in range(INNER):
        diff_time = jnp.concatenate([primal[1:] - primal[:-1], nothing], 0)
        diff_rows = jnp.where(last, 0.0, roll_last(primal, -1) - primal)
        dual_time = jnp.clip(dual_time + dual_step * diff_time, -1.0, 1.0)
        dual_rows = jnp.clip(dual_rows + dual_step * diff_rows, -1.0, 1.0)
        primal = target - tv_weight * adjoint(dual_time, dual_rows)
    return primal


def parted_mask(mask_ref):
    length = mask_ref.shape[1]
    line = lax.broadcasted_iota(jnp.int32, (length, length), 0)
    lane = lax.broadcasted_iota(jnp.int32, (length, length), 1)
    half = length // 2
    place = jnp.where(lane < half, 2 * lane, 2 * (lane - half) + 1)
    permutation = (line == place).astype(jnp.float32).astype(jnp.bfloat16)
    mask = mask_ref[...].astype(jnp.float32).astype(jnp.bfloat16)
    return jnp.dot(mask, permutation, preferred_element_type=jnp.float32)


def mask_responses(mask_ref, wave_hi, wave_lo, out_ref):
    parted = parted_mask(mask_ref).astype(jnp.bfloat16)
    half = parted.shape[1] // 2
    for side in range(2):
        mask = parted[:, side * half : (side + 1) * half]
        terms = [
            jnp.dot(mask, wave[side], preferred_element_type=jnp.float32)
            for wave in (wave_hi, wave_lo)
        ]
        out_ref[side] = terms[0] + terms[1]


def frame_tables(response_ref, f):
    half = response_ref.shape[-1] // 2
    tables = []
    for side in range(2):
        row = response_ref[side, pl.ds(f, 1), :]
        parts = []
        for at in (0, half):
            spread = jnp.broadcast_to(row[:, at : at + half], (half, half))
            turned = pltpu.roll(spread, 0, 1, stride=1, stride_axis=0)
            if side:
                before = lax.broadcasted_iota(jnp.int32, (half, half), 1) < (
                    lax.broadcasted_iota(jnp.int32, (half, half), 0)
                )
                turned = jnp.where(before, -turned, turned)
            parts.append(turned)
        re, im = parts
        tables.append(
            split(jnp.concatenate([jnp.concatenate([re, im], 1), jnp.concatenate([-im, re], 1)], 0))
        )
    return tables


def normal_frame(maps_ref, field_re, field_im, tables):
    coils, _, cols, length = maps_ref.shape
    half = length // 2
    maps_re, maps_im = maps_ref[:, 0], maps_ref[:, 1]
    u_re = maps_re * field_re[None] - maps_im * field_im[None]
    u_im = maps_re * field_im[None] + maps_im * field_re[None]
    flat_re = u_re.reshape(coils * cols, length)
    flat_im = u_im.reshape(coils * cols, length)
    outs = []
    for sign, table in zip((1.0, -1.0), tables):
        packed = jnp.concatenate(
            [
                flat_re[:, :half] + sign * flat_re[:, half:],
                flat_im[:, :half] + sign * flat_im[:, half:],
            ],
            1,
        )
        outs.append(dot3(split(packed), table))
    plus, minus = outs
    v_re = jnp.concatenate(
        [plus[:, :half] + minus[:, :half], plus[:, :half] - minus[:, :half]], 1
    ).reshape(coils, cols, length)
    v_im = jnp.concatenate(
        [plus[:, half:] + minus[:, half:], plus[:, half:] - minus[:, half:]], 1
    ).reshape(coils, cols, length)
    return (
        jnp.sum(maps_re * v_re + maps_im * v_im, 0),
        jnp.sum(maps_re * v_im - maps_im * v_re, 0),
    )


def coil_blocks_kernel(coils, *refs):
    *tiles, out_ref = refs
    devices, pair_coils, rows, lanes = out_ref.shape
    halves = len(tiles) // 2
    each = lanes // (2 * LANES)
    for d in range(devices):
        for c in range(pair_coils):
            for part in range(2):
                for t in range(each):
                    at = (part * each + t) * LANES
                    out_ref[d, c, :, at : at + LANES] = tiles[part * halves + (d & 1) * each + t][
                        pl.ds((d >> 1) * pair_coils + c, rows, stride=coils), :
                    ]


def with_bit(index, bit, value):
    return ((index >> bit) << (bit + 1)) | (value << bit) | (index & ((1 << bit) - 1))


def column_blocks_kernel(coils, frames, chunk_of, level, device_ref, *refs):
    *tiles, keep_ref, send_ref, turned = refs
    sens_tiles, image_tiles = tiles[: len(tiles) // 2], tiles[len(tiles) // 2 :]
    blocks, early, _, cols, _ = send_ref.shape
    groups = (keep_ref.shape[1] + early) // 2
    rows = sens_tiles[0].shape[0] // coils
    per = LANES // rows
    half = len(sens_tiles) // 2
    mine = (device_ref[0] >> level) & 1
    far = chunk_of[1 << level] * cols
    for g in range(groups):
        if g * per < coils:
            tiles, count, base = sens_tiles, coils, g * per
        else:
            tiles, count, base = image_tiles, frames, g * per - coils
        for t, ref in enumerate(tiles):
            turned[t // half, pl.ds(t % half * LANES, LANES)] = jnp.concatenate(
                [ref[pl.ds(base + c, rows, stride=count), :] for c in range(per)], 0
            ).T
        other = (send_ref, g) if g < early else (keep_ref, g + groups - early)
        for (out, unit), side in (((keep_ref, g), mine), (other, 1 - mine)):
            for e in range(blocks):
                at = pl.multiple_of(chunk_of[with_bit(e, level, 0)] * cols + side * far, cols)
                for part in range(2):
                    out[e, unit, part] = turned[part, pl.ds(at, cols)]


def base_kernel(start, frames, device_ref, kspace_ref, mask_ref, *refs):
    cols_ref, rows_ref, keep_ref, send_ref, data, near_hi, near_lo, masks, arrived = refs
    own, _, _, span, length = keep_ref.shape
    bit = device_ref[0] & 1
    half = length // 2
    frame = pl.program_id(0)

    def fetch(f, slot):
        return [
            pltpu.make_async_copy(
                kspace_ref.at[:, odd, start + f + c * frames, :],
                data.at[slot, c, pl.ds(odd * half, half)],
                arrived.at[slot, c, odd],
            )
            for c in range(own)
            for odd in range(2)
        ]

    @pl.when(frame == 0)
    def _():
        for copy in fetch(0, 0):
            copy.start()
        masks[...] = parted_mask(mask_ref)
        for term, near in enumerate((near_hi, near_lo)):
            for i, which in enumerate((bit, 1 - bit)):
                for part in range(2):
                    at = pl.multiple_of((2 * part + which) * span, span)
                    near[pl.ds((2 * i + part) * span, span)] = cols_ref[term, pl.ds(at, span)]

    @pl.when(frame + 1 < pl.num_programs(0))
    def _():
        for copy in fetch(frame + 1, (frame + 1) % 2):
            copy.start()

    slot = frame % 2
    for copy in fetch(frame, slot):
        copy.wait()
    columns = [
        dot3((near_hi[...], near_lo[...]), split(data[slot, c]), ((1,), (1,)))
        * masks[pl.ds(start + frame, 1), :]
        for c in range(own)
    ]
    blocks = [v[2 * i * span : (2 * i + 2) * span] for v in columns for i in range(2)]
    sides = []
    for odd in range(2):
        at = odd * half
        stacked = jnp.concatenate(
            [
                jnp.concatenate([v[:span, at : at + half], v[span:, at : at + half]], 1)
                for v in blocks
            ],
            0,
        )
        sides.append(dot3(split(stacked), (rows_ref[0, odd], rows_ref[1, odd])))
    for c in range(own):
        for i, ref in enumerate((keep_ref, send_ref)):
            rows = (2 * c + i) * span
            even, odd = [side[rows : rows + span] for side in sides]
            for part in range(2):
                e = even[:, part * half : (part + 1) * half]
                o = odd[:, part * half : (part + 1) * half]
                ref[c, 0, part] = jnp.concatenate([e + o, e - o], 1)


def weigh_kernel(outer, level, flip, device_ref, maps_ref, kept_ref, got_ref, out_ref, *refs):
    turned, maps, kept, got, total, maps_arrived, arrived, left = refs
    devices, pair_coils, rows, lanes = maps_ref.shape
    own, count = got_ref.shape[:2]
    inner, _, _, cols, length = total.shape
    inner //= outer
    span = inner * cols
    bit, which = device_ref[0] & 1, ((device_ref[0] >> level) & 1) ^ flip
    far = [pl.multiple_of((2 * i + which) * span, span) for i in range(outer)]

    map_copies = [
        pltpu.make_async_copy(maps_ref.at[:, c], maps.at[c], maps_arrived.at[c])
        for c in range(pair_coils)
    ]
    for copy in map_copies:
        copy.start()
    copies = [
        [
            pltpu.make_async_copy(
                src.at[:, f, :, pl.ds(far[i], span)],
                dst.at[:, f, :, pl.ds(i * span, span)],
                arrived.at[j, f, i],
            )
            for j, (src, dst) in enumerate(((kept_ref, kept), (got_ref, got)))
            for i in range(outer)
        ]
        for f in range(count)
    ]
    for group in copies:
        for copy in group:
            copy.start()
    for c in range(pair_coils):
        map_copies[c].wait()
        one = maps[c].reshape(length, lanes).T
        turned[c, 0] = one[: lanes // 2]
        turned[c, 1] = one[lanes // 2 :]

    results = []
    for f in range(count):
        for copy in copies[f]:
            copy.wait()
        for i in range(outer):
            here = slice(i * span, (i + 1) * span)
            total_re = total_im = 0.0
            for base, first in ((kept, bit * own), (got, (1 - bit) * own)):
                for c in range(own):
                    s_re = turned[first + c, 0, pl.ds(far[i], span), :]
                    s_im = turned[first + c, 1, pl.ds(far[i], span), :]
                    b_re, b_im = base[c, f, 0, here, :], base[c, f, 1, here, :]
                    total_re += s_re * b_re + s_im * b_im
                    total_im += s_re * b_im - s_im * b_re
            total[i * inner : (i + 1) * inner, f, 0] = total_re.reshape(inner, cols, length)
            total[i * inner : (i + 1) * inner, f, 1] = total_im.reshape(inner, cols, length)
        results.append(pltpu.make_async_copy(total.at[:, f], out_ref.at[:, f], left.at[f]))
        results[-1].start()
    for copy in results:
        copy.wait()


def first_normal_kernel(
    coils, level, device_ref, got_ref, late_ref, mask_ref, wave_hi, wave_lo, *refs
):
    maps_out, field_out, grad_out, responses = refs[-4:]
    mask_responses(mask_ref, wave_hi, wave_lo, responses)
    blocks, units, _, cols, lanes = got_ref.shape
    groups = units // 2
    early = groups - late_ref.shape[1]
    devices = 2 * blocks
    mine = (device_ref[0] >> level) & 1
    frames = field_out.shape[0]

    def block(s, g):
        e = ((s >> (level + 1)) << level) | (s & ((1 << level) - 1))
        across = ((s >> level) & 1) ^ mine
        if g < early:
            return got_ref[e, g + across * (units - early)]
        return jnp.where(across == 0, got_ref[e, g], late_ref[e, g - early])

    per = (coils + frames) // groups
    width = lanes // per
    for g in range(groups):
        out, base = (maps_out, g * per) if g * per < coils else (field_out, g * per - coils)
        for h in range(devices // per):
            exchanged = lane_exchange([block(h * per + s, g) for s in range(per)], width)
            for c in range(per):
                out[base + c, :, :, h * lanes : (h + 1) * lanes] = exchanged[c]

    def one(f, _):
        grad_out[f, 0], grad_out[f, 1] = normal_frame(
            maps_out, field_out[f, 0], field_out[f, 1], frame_tables(responses, f)
        )
        return 0

    lax.fori_loop(0, frames, one, 0, unroll=4)


def steps_kernel(field_ref, grad_ref, maps_ref, mask_ref, *refs):
    wave_hi, wave_lo, *terms, out_ref, field, grad, responses = refs
    frames, _, cols, length = field_ref.shape
    devices, _, _, lanes = out_ref.shape
    mask_responses(mask_ref, wave_hi, wave_lo, responses)
    data_term = jnp.concatenate(
        [keep[...] + got[...] for keep, got in zip(terms[0::2], terms[1::2])], 0
    )
    field[...] = tv_step(field_ref[...] - step_size * (grad_ref[...] - data_term))
    for sweep in range(1, OUTER):

        def one(f, _):
            grad[f, 0], grad[f, 1] = normal_frame(
                maps_ref, field[f, 0], field[f, 1], frame_tables(responses, f)
            )
            return 0

        lax.fori_loop(0, frames, one, 0, unroll=4)
        field[...] = tv_step(field[...] - step_size * (grad[...] - data_term))
    per = frames
    for h in range(devices // per):
        parts = [field[f, :, :, h * lanes : (h + 1) * lanes] for f in range(per)]
        exchanged = lane_exchange(parts, lanes // per)
        for s in range(per):
            out_ref[h * per + s] = exchanged[s]


def rows_out_kernel(chunk_of, frames, got_ref, out_ref, tiles):
    devices, _, cols, lanes = got_ref.shape
    count = tiles.shape[0]
    rows = lanes // frames
    order = sorted(range(devices), key=lambda d: chunk_of[d])
    each = LANES // cols
    for t in range(count):
        at = t % (count // 2) * each
        turned = jnp.concatenate([got_ref[d, t // (count // 2)] for d in order[at : at + each]], 0).T
        for f in range(frames):
            tiles[t, pl.ds(f, rows, stride=frames), :] = turned[f * rows : (f + 1) * rows]
        out_ref[:, t * LANES : (t + 1) * LANES] = tiles[t]


def params(limit=VMEM_LIMIT):
    return pltpu.CompilerParams(vmem_limit_bytes=limit)


def cost(flops, moved):
    return pl.CostEstimate(flops=int(flops), bytes_accessed=int(moved), transcendentals=0)


def whole(shape):
    return pl.BlockSpec(shape, lambda *_: (0,) * len(shape))


def lane_tiles(rows, lanes):
    return [
        pl.BlockSpec((rows, LANES), lambda *_, t=t: (0, t), pipeline_mode=pl.Buffered(1))
        for t in range(lanes // LANES)
    ]


def f32(*shape):
    return jax.ShapeDtypeStruct(shape, jnp.float32)


def exchange(send, bit):
    devices = lax.axis_size("coil")
    return lax.ppermute(send, "coil", [(i, i ^ (1 << bit)) for i in range(devices)])


def halve(keep, got, bit, device):
    mine = (device >> bit) & 1

    def part(which):
        return lax.dynamic_index_in_dim(
            keep, which, bit - 1, keepdims=True
        ) + lax.dynamic_index_in_dim(got, which, bit - 1, keepdims=True)

    send = part(1 - mine)
    return part(mine), send


def kernel_path(image, sens, kspace, mask):
    rows, frames, packed = image.shape
    coils = sens.shape[1]
    length, pairs, _ = kspace.shape
    half = packed // 2
    hl = length // 2
    devices = lax.axis_size("coil")
    device = lax.axis_index("coil")
    bits = devices.bit_length() - 1
    own = pairs // frames
    cols = half // devices
    per = LANES // rows
    groups = (coils + frames) // per
    chunk_of = [sum(((d >> b) & 1) << (bits - 1 - b) for b in range(bits)) for d in range(devices)]

    k = np.arange(length)
    z = np.arange(half)
    y = np.arange(hl)
    col_tables = np.stack(two_terms(packed_left(dft(z, z, half) / np.sqrt(half))))
    lanes_k = [k[0::2], k[1::2]]
    inverse = [packed_right(dft(y, ks, length)) for ks in lanes_k]
    row_tables = np.stack(two_terms(np.stack(inverse) / np.sqrt(length)))
    waves = [dft(ks, y, length) * 0.5 / hl for ks in lanes_k]
    wave_hi, wave_lo = two_terms(np.stack([np.concatenate([w.real, w.imag], 1) for w in waves]))

    sens_rows = sens.reshape(rows * coils, packed)
    image_rows = image.reshape(rows * frames, packed)

    with jax.named_scope("coil_maps"):
        blocks = pl.pallas_call(
            functools.partial(coil_blocks_kernel, coils),
            grid=(1,),
            out_shape=f32(devices, 2 * own, rows, half),
            in_specs=lane_tiles(rows * coils, packed),
            out_specs=whole((devices, 2 * own, rows, half)),
            compiler_params=params(),
            cost_estimate=cost(0, 2 * sens.size * 4),
        )(*[sens_rows] * (packed // LANES))
        blocks, device = lax.optimization_barrier((blocks, device))
        coil_maps = lax.all_to_all(blocks, "coil", 0, 0, tiled=True)

    with jax.named_scope("column_maps"):
        level = 1
        early = (groups + 1) // 2
        keep_block = (devices // 2, 2 * groups - early, 2, cols, LANES)
        send_block = (devices // 2, early, 2, cols, LANES)
        column_keep, column_send = pl.pallas_call(
            functools.partial(column_blocks_kernel, coils, frames, chunk_of, level),
            grid=(1,),
            out_shape=(f32(*keep_block), f32(*send_block)),
            in_specs=[pl.BlockSpec(memory_space=pltpu.SMEM)]
            + lane_tiles(rows * coils, packed)
            + lane_tiles(rows * frames, packed),
            out_specs=(whole(keep_block), whole(send_block)),
            scratch_shapes=[pltpu.VMEM((2, half, LANES), jnp.float32)],
            compiler_params=params(),
            cost_estimate=cost(0, 2 * (sens.size + image.size) * 4),
        )(device[None], *[sens_rows] * (packed // LANES), *[image_rows] * (packed // LANES))
        column_send, device = lax.optimization_barrier((column_send, device))
        column_blocks = jnp.concatenate([column_keep, exchange(column_send, level)], 1)
        sides = [[with_bit(e, level, side) for e in range(devices // 2)] for side in range(2)]

    plans = [
        (frames // 2, list(range(1, bits))),
        (frames // 2, list(range(1, bits))),
    ]
    firsts = [sum(count for count, _ in plans[:i]) for i in range(len(plans))]
    span = half // 2
    smem = pl.BlockSpec(memory_space=pltpu.SMEM)
    kept, got = [], []
    for start, (count, _) in zip(firsts, plans):
        with jax.named_scope("data_transform"):
            block = pl.BlockSpec((own, 1, 2, span, length), lambda f: (0, f, 0, 0, 0))
            keep, send = pl.pallas_call(
                functools.partial(base_kernel, start, frames),
                grid=(count,),
                out_shape=(f32(own, count, 2, span, length),) * 2,
                in_specs=[
                    smem,
                    pl.BlockSpec(memory_space=pltpu.HBM),
                    whole((frames, length)),
                    whole((2, packed, packed)),
                    whole((2, 2, length, length)),
                ],
                out_specs=(block, block),
                scratch_shapes=[
                    pltpu.VMEM((2, own, length, packed), jnp.float32),
                    pltpu.VMEM((packed, packed), jnp.bfloat16),
                    pltpu.VMEM((packed, packed), jnp.bfloat16),
                    pltpu.VMEM((frames, length), jnp.float32),
                    pltpu.SemaphoreType.DMA((2, own, 2)),
                ],
                compiler_params=params(TRANSFORM_LIMIT),
                cost_estimate=cost(
                    own * count * 36 * half * half * length, 16 * own * count * half * length
                ),
            )(
                device[None],
                kspace.reshape(hl, 2, pairs, packed),
                mask,
                col_tables,
                row_tables,
            )
        if len(kept) == len(plans) - 1:
            column_blocks, send = lax.optimization_barrier((column_blocks, send))
        kept.append(keep)
        got.append(exchange(send, 0))
    with jax.named_scope("column_maps"):
        column_maps = lax.all_to_all(
            column_blocks, "coil", 0, 0, tiled=True, axis_index_groups=sides
        )
        column_late = exchange(column_maps[:, groups : 2 * groups - early], level)

    field = f32(frames, 2, cols, length)
    normal_cost = 6 * 2 * frames * coils * cols * length * length

    responses = pltpu.VMEM((2, frames, length), jnp.float32)

    anywhere = pl.BlockSpec(memory_space=pl.ANY)

    def first_gradient(column_maps, before):
        return pl.pallas_call(
            functools.partial(first_normal_kernel, coils, level),
            in_specs=[smem]
            + [pl.BlockSpec(memory_space=pltpu.VMEM)] * 5
            + [pl.BlockSpec(memory_space=pl.ANY)] * len(before),
            out_shape=(f32(coils, 2, cols, length), field, field),
            scratch_shapes=[responses],
            compiler_params=params(),
            cost_estimate=cost(normal_cost, 4 * sens.size * 4),
            name="first_gradient",
        )(device[None], column_maps, column_late, mask, wave_hi, wave_lo, *before)

    with jax.named_scope("data_term"):

        def weigh(stream, flip):
            count, order = plans[stream]
            outer = 2 ** (order[0] - 1)
            out = f32(devices // 4, count, 2, cols, length)
            base = pltpu.VMEM((own, count, 2, span // 2, length), jnp.float32)
            value = pl.pallas_call(
                functools.partial(weigh_kernel, outer, order[0], flip),
                out_shape=out,
                in_specs=[smem, anywhere, anywhere, anywhere],
                out_specs=anywhere,
                scratch_shapes=[
                    pltpu.VMEM((2 * own, 2, span, length), jnp.float32),
                    pltpu.VMEM((2 * own, devices, rows, half), jnp.float32),
                    base,
                    base,
                    pltpu.VMEM(out.shape, jnp.float32),
                    pltpu.SemaphoreType.DMA((2 * own,)),
                    pltpu.SemaphoreType.DMA((2, count, outer)),
                    pltpu.SemaphoreType.DMA((count,)),
                ],
                compiler_params=params(WEIGH_LIMIT),
                cost_estimate=cost(0, kept[stream].size * 4 + out.size * 4),
            )(device[None], coil_maps, kept[stream], got[stream])
            dims = [2] * (bits - 1)
            dims[order[0] - 1] = 1
            return value.reshape(*dims, *out.shape[1:])

        received = [exchange(weigh(i, 1), plans[i][1][0]) for i in range(len(plans))]
        terms = [(weigh(i, 0), received[i]) for i in range(len(plans))]
        sent = [None] * len(plans)

        def advance(stream, step):
            order = plans[stream][1]
            keep, sent[stream] = halve(*terms[stream], order[step], device)
            terms[stream] = (keep, exchange(sent[stream], order[step]))

        for step in range(1, bits - 1):
            for stream in range(len(plans)):
                advance(stream, step)
        maps, field0, grad0 = first_gradient(column_maps, sent)
        terms = [value.reshape(-1, 2, cols, length) for term in terms for value in term]

    with jax.named_scope("outer_steps"):
        blocks = pl.pallas_call(
            steps_kernel,
            out_shape=f32(devices, 2, cols, LANES),
            scratch_shapes=[pltpu.VMEM(field.shape, jnp.float32)] * 2 + [responses],
            compiler_params=params(),
            cost_estimate=cost(normal_cost, 4 * sens.size * 4),
        )(field0, grad0, maps, mask, wave_hi, wave_lo, *terms)

    with jax.named_scope("result_rows"):
        got = lax.all_to_all(blocks, "coil", 0, 0, tiled=True)
        recon = pl.pallas_call(
            functools.partial(rows_out_kernel, chunk_of, frames),
            out_shape=f32(rows * frames, packed),
            scratch_shapes=[pltpu.VMEM((packed // LANES, rows * frames, LANES), jnp.float32)],
            compiler_params=params(),
            cost_estimate=cost(0, 2 * image.size * 4),
        )(got)
    return recon.reshape(rows, frames, packed)


def einsum(form, left, right):
    return jnp.einsum(form, left, right, precision=highest, preferred_element_type=jnp.float32)


def complex_einsum(form, left, right):
    (a, b), (c, d) = left, right
    return (
        einsum(form, a, c) - einsum(form, b, d),
        einsum(form, a, d) + einsum(form, b, c),
    )


def general_path(image, sens, kspace, mask):
    rows, frames, packed = image.shape
    coils = sens.shape[1]
    length, pairs, _ = kspace.shape
    half = packed // 2
    devices = lax.axis_size("coil")
    device = lax.axis_index("coil")
    cols = half // devices

    def table(size):
        values = dft(np.arange(size), np.arange(size), size) / np.sqrt(size)
        return jnp.asarray(values.real, jnp.float32), jnp.asarray(values.imag, jnp.float32)

    inverse_rows, inverse_cols = table(length), table(half)
    forward_rows = (inverse_rows[0], -inverse_rows[1])

    both = jnp.concatenate([sens, image], 1).reshape(rows, coils + frames, 2, devices, cols)
    both = lax.all_to_all(both.transpose(3, 1, 2, 4, 0), "coil", 0, 0, tiled=True)
    both = both.transpose(1, 2, 3, 0, 4).reshape(coils + frames, 2, cols, length)
    maps, field = both[:coils], both[coils:]

    own = max(1, pairs // frames)
    repeats = devices * own // coils
    spread = jnp.repeat(sens.reshape(rows, coils // own, own, packed), repeats, axis=1)
    spread = spread.transpose(1, 0, 2, 3)
    coil_maps = lax.all_to_all(spread, "coil", 0, 0, tiled=True).reshape(length, own, packed)

    ids = device * pairs + lax.iota(jnp.int32, pairs)
    onehot = (ids[:, None] % frames == lax.iota(jnp.int32, frames)[None, :]).astype(jnp.float32)
    sampled = mask.astype(jnp.float32)
    data = einsum("pf,fk->kp", onehot, sampled)[:, :, None] * kspace
    data = (data[..., :half], data[..., half:])
    data = complex_einsum("kpz,zx->kpx", data, inverse_cols)
    data = complex_einsum("yk,kpx->ypx", inverse_rows, data)
    pair_maps = jnp.repeat(coil_maps, pairs // own, axis=1)
    m_re, m_im = pair_maps[..., :half], pair_maps[..., half:]
    weighted = jnp.stack(
        [m_re * data[0] + m_im * data[1], m_re * data[1] - m_im * data[0]], 2
    ).reshape(length, pairs, 2, devices, cols)
    term = einsum("ypcdx,pf->dfcxy", weighted, onehot)
    term = lax.psum_scatter(term, "coil", scatter_dimension=0, tiled=True)[0]

    masked = (
        sampled[:, :, None] * forward_rows[0][None],
        sampled[:, :, None] * forward_rows[1][None],
    )
    project = complex_einsum("yk,fkv->fyv", inverse_rows, masked)
    for sweep in range(OUTER):
        u_re = maps[:, None, 0] * field[None, :, 0] - maps[:, None, 1] * field[None, :, 1]
        u_im = maps[:, None, 0] * field[None, :, 1] + maps[:, None, 1] * field[None, :, 0]
        v_re, v_im = complex_einsum("fyv,cfxv->cfxy", project, (u_re, u_im))
        grad = jnp.stack(
            [
                jnp.sum(maps[:, None, 0] * v_re + maps[:, None, 1] * v_im, 0),
                jnp.sum(maps[:, None, 0] * v_im - maps[:, None, 1] * v_re, 0),
            ],
            1,
        )
        target = field - step_size * (grad - term)
        dual_time = jnp.zeros_like(target)
        dual_rows = jnp.zeros_like(target)
        field = target
        for repeat in range(INNER):
            diff_time = jnp.concatenate([field[1:] - field[:-1], jnp.zeros_like(field[:1])], 0)
            diff_rows = jnp.concatenate(
                [field[..., 1:] - field[..., :-1], jnp.zeros_like(field[..., :1])], -1
            )
            dual_time = jnp.clip(dual_time + dual_step * diff_time, -1.0, 1.0)
            dual_rows = jnp.clip(dual_rows + dual_step * diff_rows, -1.0, 1.0)
            inner_time, inner_rows = dual_time[:-1], dual_rows[..., :-1]
            none_time, none_rows = jnp.zeros_like(field[:1]), jnp.zeros_like(field[..., :1])
            divergence = (
                jnp.concatenate([none_time, inner_time], 0)
                - jnp.concatenate([inner_time, none_time], 0)
                + jnp.concatenate([none_rows, inner_rows], -1)
                - jnp.concatenate([inner_rows, none_rows], -1)
            )
            field = target - tv_weight * divergence

    result = field.reshape(frames, 2, cols, devices, rows).transpose(3, 0, 1, 2, 4)
    result = lax.all_to_all(result, "coil", 0, 0, tiled=True)
    return result.transpose(4, 1, 2, 0, 3).reshape(rows, frames, packed)


def fits_kernels(image, sens, kspace, devices):
    rows, frames, packed = image.shape
    coils = sens.shape[1]
    length, pairs, _ = kspace.shape
    per = LANES // rows
    return (
        devices & (devices - 1) == 0
        and devices >= 4
        and rows % 8 == 0
        and rows * per == LANES
        and frames == per
        and frames % 2 == 0
        and coils % per == 0
        and devices % per == 0
        and pairs % frames == 0
        and pairs * devices == coils * frames
        and length == 2 * LANES
        and packed % (16 * devices) == 0
        and packed % (4 * LANES) == 0
    )


def per_device(image, sens, kspace, mask):
    if fits_kernels(image, sens, kspace, lax.axis_size("coil")):
        return kernel_path(image, sens, kspace, mask)
    return general_path(image, sens, kspace, mask)


def solution(mesh):
    return jax.shard_map(
        per_device,
        mesh=mesh,
        in_specs=(
            P(("plane", "coil"), None, None),
            P(("plane", "coil"), None, None),
            P("plane", "coil", None),
            P(),
        ),
        out_specs=P(("plane", "coil"), None, None),
        check_vma=False,
    )
```

```python
import functools

import jax
import jax.numpy as jnp
import ml_dtypes
import numpy as np
from jax import lax
from jax.experimental import pallas as pl
from jax.experimental.pallas import tpu as pltpu
from jax.sharding import PartitionSpec as P

OUTER = 2
INNER = 2
LANES = 128
VMEM_LIMIT = 16 * 1024 * 1024
TRANSFORM_LIMIT = 52 * 1024 * 1024
WEIGH_LIMIT = 60 * 1024 * 1024

step_size = 0.5
tv_weight = 0.1
dual_step = 1.25
highest = lax.Precision.HIGHEST


def two_terms(table):
    first = table.astype(ml_dtypes.bfloat16)
    second = (table - first.astype(np.float64)).astype(ml_dtypes.bfloat16)
    return first, second


def dft(out_index, in_index, length):
    product = np.outer(out_index, in_index) % length
    return np.exp(2j * np.pi / length * product)


def packed_left(matrix):
    return np.block([[matrix.real, -matrix.imag], [matrix.imag, matrix.real]])


def packed_right(matrix):
    return packed_left(matrix).T


def split(value):
    first = value.astype(jnp.bfloat16)
    second = (value - first.astype(jnp.float32)).astype(jnp.bfloat16)
    return first, second


def dot3(left, right, contract=((1,), (0,))):
    dims = (contract, ((), ()))

    return lax.dot_general(
        jnp.concatenate([left[0], left[0], left[1]], contract[0][0]),
        jnp.concatenate([right[0], right[1], right[0]], contract[1][0]),
        dims,
        preferred_element_type=jnp.float32,
    )


def lane_exchange(parts, width):
    parts = list(parts)
    lane = lax.broadcasted_iota(jnp.int32, parts[0].shape, parts[0].ndim - 1)
    axis = parts[0].ndim - 1
    bit = 1
    while bit < len(parts):
        odd = (lane // width) & bit != 0
        for s in range(len(parts)):
            if s & bit:
                continue
            low, high = parts[s], parts[s | bit]
            parts[s] = jnp.where(odd, pltpu.roll(high, width * bit, axis), low)
            parts[s | bit] = jnp.where(odd, high, pltpu.roll(low, LANES - width * bit, axis))
        bit *= 2
    return parts


def roll_last(value, distance):
    shape = value.shape
    flat = value.reshape(-1, shape[-1])
    return pltpu.roll(flat, distance % shape[-1], 1).reshape(shape)


def tv_step(target):
    length = target.shape[-1]
    row = lax.broadcasted_iota(jnp.int32, target.shape, target.ndim - 1)
    last, first = row == length - 1, row == 0
    nothing = jnp.zeros_like(target[:1])

    def adjoint(dual_time, dual_rows):
        from_time = jnp.concatenate([nothing, dual_time[:-1]], 0) - jnp.concatenate(
            [dual_time[:-1], nothing], 0
        )
        from_rows = jnp.where(first, 0.0, roll_last(dual_rows, 1)) - jnp.where(last, 0.0, dual_rows)
        return from_time + from_rows

    dual_time = jnp.zeros_like(target)
    dual_rows = jnp.zeros_like(target)
    primal = target
    for repeat in range(INNER):
        diff_time = jnp.concatenate([primal[1:] - primal[:-1], nothing], 0)
        diff_rows = jnp.where(last, 0.0, roll_last(primal, -1) - primal)
        dual_time = jnp.clip(dual_time + dual_step * diff_time, -1.0, 1.0)
        dual_rows = jnp.clip(dual_rows + dual_step * diff_rows, -1.0, 1.0)
        primal = target - tv_weight * adjoint(dual_time, dual_rows)
    return primal


def parted_mask(mask_ref):
    length = mask_ref.shape[1]
    line = lax.broadcasted_iota(jnp.int32, (length, length), 0)
    lane = lax.broadcasted_iota(jnp.int32, (length, length), 1)
    half = length // 2
    place = jnp.where(lane < half, 2 * lane, 2 * (lane - half) + 1)
    permutation = (line == place).astype(jnp.float32).astype(jnp.bfloat16)
    mask = mask_ref[...].astype(jnp.float32).astype(jnp.bfloat16)
    return jnp.dot(mask, permutation, preferred_element_type=jnp.float32)


def mask_responses(mask_ref, wave_hi, wave_lo, out_ref):
    parted = parted_mask(mask_ref).astype(jnp.bfloat16)
    half = parted.shape[1] // 2
    for side in range(2):
        mask = parted[:, side * half : (side + 1) * half]
        terms = [
            jnp.dot(mask, wave[side], preferred_element_type=jnp.float32)
            for wave in (wave_hi, wave_lo)
        ]
        out_ref[side] = terms[0] + terms[1]


def frame_tables(response_ref, f):
    half = response_ref.shape[-1] // 2
    tables = []
    for side in range(2):
        row = response_ref[side, pl.ds(f, 1), :]
        parts = []
        for at in (0, half):
            spread = jnp.broadcast_to(row[:, at : at + half], (half, half))
            turned = pltpu.roll(spread, 0, 1, stride=1, stride_axis=0)
            if side:
                before = lax.broadcasted_iota(jnp.int32, (half, half), 1) < (
                    lax.broadcasted_iota(jnp.int32, (half, half), 0)
                )
                turned = jnp.where(before, -turned, turned)
            parts.append(turned)
        re, im = parts
        tables.append(
            split(jnp.concatenate([jnp.concatenate([re, im], 1), jnp.concatenate([-im, re], 1)], 0))
        )
    return tables


def normal_coils(maps_ref, field_re, field_im, tables):
    coils, _, cols, length = maps_ref.shape
    half = length // 2
    maps_re, maps_im = maps_ref[:, 0], maps_ref[:, 1]
    u_re = maps_re * field_re[None] - maps_im * field_im[None]
    u_im = maps_re * field_im[None] + maps_im * field_re[None]
    flat_re = u_re.reshape(coils * cols, length)
    flat_im = u_im.reshape(coils * cols, length)
    outs = []
    for sign, table in zip((1.0, -1.0), tables):
        packed = jnp.concatenate(
            [
                flat_re[:, :half] + sign * flat_re[:, half:],
                flat_im[:, :half] + sign * flat_im[:, half:],
            ],
            1,
        )
        outs.append(dot3(split(packed), table))
    plus, minus = outs
    v_re = jnp.concatenate(
        [plus[:, :half] + minus[:, :half], plus[:, :half] - minus[:, :half]], 1
    ).reshape(coils, cols, length)
    v_im = jnp.concatenate(
        [plus[:, half:] + minus[:, half:], plus[:, half:] - minus[:, half:]], 1
    ).reshape(coils, cols, length)
    return (
        jnp.sum(maps_re * v_re + maps_im * v_im, 0),
        jnp.sum(maps_re * v_im - maps_im * v_re, 0),
    )


def normal_frame(maps_ref, field_re, field_im, tables):
    middle = maps_ref.shape[0] // 2
    first = normal_coils(maps_ref.at[:middle], field_re, field_im, tables)
    second = normal_coils(maps_ref.at[middle:], field_re, field_im, tables)
    return first[0] + second[0], first[1] + second[1]


def coil_blocks_kernel(coils, *refs):
    *tiles, out_ref = refs
    devices, pair_coils, rows, lanes = out_ref.shape
    halves = len(tiles) // 2
    each = lanes // (2 * LANES)
    for d in range(devices):
        for c in range(pair_coils):
            for part in range(2):
                for t in range(each):
                    at = (part * each + t) * LANES
                    out_ref[d, c, :, at : at + LANES] = tiles[part * halves + (d & 1) * each + t][
                        pl.ds((d >> 1) * pair_coils + c, rows, stride=coils), :
                    ]


def with_bit(index, bit, value):
    return ((index >> bit) << (bit + 1)) | (value << bit) | (index & ((1 << bit) - 1))


def column_blocks_kernel(coils, frames, chunk_of, level, device_ref, *refs):
    *tiles, keep_ref, send_ref, turned = refs
    sens_tiles, image_tiles = tiles[: len(tiles) // 2], tiles[len(tiles) // 2 :]
    blocks, early, _, cols, _ = send_ref.shape
    groups = (keep_ref.shape[1] + early) // 2
    rows = sens_tiles[0].shape[0] // coils
    per = LANES // rows
    half = len(sens_tiles) // 2
    mine = (device_ref[0] >> level) & 1
    far = chunk_of[1 << level] * cols
    for g in range(groups):
        if g * per < coils:
            tiles, count, base = sens_tiles, coils, g * per
        else:
            tiles, count, base = image_tiles, frames, g * per - coils
        for t, ref in enumerate(tiles):
            turned[t // half, pl.ds(t % half * LANES, LANES)] = jnp.concatenate(
                [ref[pl.ds(base + c, rows, stride=count), :] for c in range(per)], 0
            ).T
        other = (send_ref, g) if g < early else (keep_ref, g + groups - early)
        for (out, unit), side in (((keep_ref, g), mine), (other, 1 - mine)):
            for e in range(blocks):
                at = pl.multiple_of(chunk_of[with_bit(e, level, 0)] * cols + side * far, cols)
                for part in range(2):
                    out[e, unit, part] = turned[part, pl.ds(at, cols)]


def base_kernel(start, frames, device_ref, kspace_ref, mask_ref, *refs):
    cols_ref, rows_ref, keep_ref, send_ref, data, near_hi, near_lo, masks, arrived = refs
    own, _, _, span, length = keep_ref.shape
    bit = device_ref[0] & 1
    half = length // 2
    frame = pl.program_id(0)

    def fetch(f, slot):
        return [
            pltpu.make_async_copy(
                kspace_ref.at[:, odd, start + f + c * frames, :],
                data.at[slot, c, pl.ds(odd * half, half)],
                arrived.at[slot, c, odd],
            )
            for c in range(own)
            for odd in range(2)
        ]

    @pl.when(frame == 0)
    def _():
        for copy in fetch(0, 0):
            copy.start()
        masks[...] = parted_mask(mask_ref)
        for term, near in enumerate((near_hi, near_lo)):
            for i, which in enumerate((bit, 1 - bit)):
                for part in range(2):
                    at = pl.multiple_of((2 * part + which) * span, span)
                    near[pl.ds((2 * i + part) * span, span)] = cols_ref[term, pl.ds(at, span)]

    @pl.when(frame + 1 < pl.num_programs(0))
    def _():
        for copy in fetch(frame + 1, (frame + 1) % 2):
            copy.start()

    slot = frame % 2
    for copy in fetch(frame, slot):
        copy.wait()
    columns = [
        dot3((near_hi[...], near_lo[...]), split(data[slot, c]), ((1,), (1,)))
        * masks[pl.ds(start + frame, 1), :]
        for c in range(own)
    ]
    blocks = [v[2 * i * span : (2 * i + 2) * span] for v in columns for i in range(2)]
    sides = []
    for odd in range(2):
        at = odd * half
        stacked = jnp.concatenate(
            [
                jnp.concatenate([v[:span, at : at + half], v[span:, at : at + half]], 1)
                for v in blocks
            ],
            0,
        )
        sides.append(dot3(split(stacked), (rows_ref[0, odd], rows_ref[1, odd])))
    for c in range(own):
        for i, ref in enumerate((keep_ref, send_ref)):
            rows = (2 * c + i) * span
            even, odd = [side[rows : rows + span] for side in sides]
            for part in range(2):
                e = even[:, part * half : (part + 1) * half]
                o = odd[:, part * half : (part + 1) * half]
                ref[c, 0, part] = jnp.concatenate([e + o, e - o], 1)


def weigh_kernel(outer, level, flip, device_ref, maps_ref, kept_ref, got_ref, out_ref, *refs):
    turned, maps, kept, got, total, maps_arrived, arrived, left = refs
    devices, pair_coils, rows, lanes = maps_ref.shape
    own, count = got_ref.shape[:2]
    inner, _, _, cols, length = total.shape
    inner //= outer
    span = inner * cols
    bit, which = device_ref[0] & 1, ((device_ref[0] >> level) & 1) ^ flip
    far = [pl.multiple_of((2 * i + which) * span, span) for i in range(outer)]

    map_copies = [
        pltpu.make_async_copy(maps_ref.at[:, c], maps.at[c], maps_arrived.at[c])
        for c in range(pair_coils)
    ]
    for copy in map_copies:
        copy.start()
    copies = [
        [
            pltpu.make_async_copy(
                src.at[:, f, :, pl.ds(far[i], span)],
                dst.at[:, f, :, pl.ds(i * span, span)],
                arrived.at[j, f, i],
            )
            for j, (src, dst) in enumerate(((kept_ref, kept), (got_ref, got)))
            for i in range(outer)
        ]
        for f in range(count)
    ]
    for group in copies:
        for copy in group:
            copy.start()
    for c in range(pair_coils):
        map_copies[c].wait()
        one = maps[c].reshape(length, lanes).T
        turned[c, 0] = one[: lanes // 2]
        turned[c, 1] = one[lanes // 2 :]

    results = []
    for f in range(count):
        for copy in copies[f]:
            copy.wait()
        for i in range(outer):
            here = slice(i * span, (i + 1) * span)
            total_re = total_im = 0.0
            for base, first in ((kept, bit * own), (got, (1 - bit) * own)):
                for c in range(own):
                    s_re = turned[first + c, 0, pl.ds(far[i], span), :]
                    s_im = turned[first + c, 1, pl.ds(far[i], span), :]
                    b_re, b_im = base[c, f, 0, here, :], base[c, f, 1, here, :]
                    total_re += s_re * b_re + s_im * b_im
                    total_im += s_re * b_im - s_im * b_re
            total[i * inner : (i + 1) * inner, f, 0] = total_re.reshape(inner, cols, length)
            total[i * inner : (i + 1) * inner, f, 1] = total_im.reshape(inner, cols, length)
        results.append(pltpu.make_async_copy(total.at[:, f], out_ref.at[:, f], left.at[f]))
        results[-1].start()
    for copy in results:
        copy.wait()


def first_normal_kernel(
    coils, level, device_ref, got_ref, late_ref, mask_ref, wave_hi, wave_lo, *refs
):
    maps_out, field_out, grad_out, responses = refs[-4:]
    mask_responses(mask_ref, wave_hi, wave_lo, responses)
    blocks, units, _, cols, lanes = got_ref.shape
    groups = units // 2
    early = groups - late_ref.shape[1]
    devices = 2 * blocks
    mine = (device_ref[0] >> level) & 1
    frames = field_out.shape[0]

    def block(s, g):
        e = ((s >> (level + 1)) << level) | (s & ((1 << level) - 1))
        across = ((s >> level) & 1) ^ mine
        if g < early:
            return got_ref[e, g + across * (units - early)]
        return jnp.where(across == 0, got_ref[e, g], late_ref[e, g - early])

    per = (coils + frames) // groups
    width = lanes // per
    for g in range(groups):
        out, base = (maps_out, g * per) if g * per < coils else (field_out, g * per - coils)
        for h in range(devices // per):
            exchanged = lane_exchange([block(h * per + s, g) for s in range(per)], width)
            for c in range(per):
                out[base + c, :, :, h * lanes : (h + 1) * lanes] = exchanged[c]

    def one(f, _):
        grad_out[f, 0], grad_out[f, 1] = normal_frame(
            maps_out, field_out[f, 0], field_out[f, 1], frame_tables(responses, f)
        )
        return 0

    lax.fori_loop(0, frames, one, 0, unroll=frames)


def steps_kernel(field_ref, grad_ref, maps_ref, mask_ref, *refs):
    wave_hi, wave_lo, *terms, out_ref, field, grad, responses = refs
    frames, _, cols, length = field_ref.shape
    devices, _, _, lanes = out_ref.shape
    mask_responses(mask_ref, wave_hi, wave_lo, responses)
    data_term = jnp.concatenate(
        [keep[...] + got[...] for keep, got in zip(terms[0::2], terms[1::2])], 0
    )
    field[...] = tv_step(field_ref[...] - step_size * (grad_ref[...] - data_term))
    for sweep in range(1, OUTER):

        def one(f, _):
            grad[f, 0], grad[f, 1] = normal_frame(
                maps_ref, field[f, 0], field[f, 1], frame_tables(responses, f)
            )
            return 0

        lax.fori_loop(0, frames, one, 0, unroll=frames)
        field[...] = tv_step(field[...] - step_size * (grad[...] - data_term))
    per = frames
    for h in range(devices // per):
        parts = [field[f, :, :, h * lanes : (h + 1) * lanes] for f in range(per)]
        exchanged = lane_exchange(parts, lanes // per)
        for s in range(per):
            out_ref[h * per + s] = exchanged[s]


def rows_out_kernel(chunk_of, frames, got_ref, out_ref, tiles):
    devices, _, cols, lanes = got_ref.shape
    count = tiles.shape[0]
    rows = lanes // frames
    order = sorted(range(devices), key=lambda d: chunk_of[d])
    each = LANES // cols
    for t in range(count):
        at = t % (count // 2) * each
        turned = jnp.concatenate([got_ref[d, t // (count // 2)] for d in order[at : at + each]], 0).T
        for f in range(frames):
            tiles[t, pl.ds(f, rows, stride=frames), :] = turned[f * rows : (f + 1) * rows]
        out_ref[:, t * LANES : (t + 1) * LANES] = tiles[t]


def params(limit=VMEM_LIMIT):
    return pltpu.CompilerParams(vmem_limit_bytes=limit)


def cost(flops, moved):
    return pl.CostEstimate(flops=int(flops), bytes_accessed=int(moved), transcendentals=0)


def whole(shape):
    return pl.BlockSpec(shape, lambda *_: (0,) * len(shape))


def lane_tiles(rows, lanes):
    return [
        pl.BlockSpec((rows, LANES), lambda *_, t=t: (0, t), pipeline_mode=pl.Buffered(1))
        for t in range(lanes // LANES)
    ]


def f32(*shape):
    return jax.ShapeDtypeStruct(shape, jnp.float32)


def exchange(send, bit):
    devices = lax.axis_size("coil")
    return lax.ppermute(send, "coil", [(i, i ^ (1 << bit)) for i in range(devices)])


def halve(keep, got, bit, device):
    mine = (device >> bit) & 1

    def part(which):
        return lax.dynamic_index_in_dim(
            keep, which, bit - 1, keepdims=True
        ) + lax.dynamic_index_in_dim(got, which, bit - 1, keepdims=True)

    send = part(1 - mine)
    return part(mine), send


def kernel_path(image, sens, kspace, mask):
    rows, frames, packed = image.shape
    coils = sens.shape[1]
    length, pairs, _ = kspace.shape
    half = packed // 2
    hl = length // 2
    devices = lax.axis_size("coil")
    device = lax.axis_index("coil")
    bits = devices.bit_length() - 1
    own = pairs // frames
    cols = half // devices
    per = LANES // rows
    groups = (coils + frames) // per
    chunk_of = [sum(((d >> b) & 1) << (bits - 1 - b) for b in range(bits)) for d in range(devices)]

    k = np.arange(length)
    z = np.arange(half)
    y = np.arange(hl)
    col_tables = np.stack(two_terms(packed_left(dft(z, z, half) / np.sqrt(half))))
    lanes_k = [k[0::2], k[1::2]]
    inverse = [packed_right(dft(y, ks, length)) for ks in lanes_k]
    row_tables = np.stack(two_terms(np.stack(inverse) / np.sqrt(length)))
    waves = [dft(ks, y, length) * 0.5 / hl for ks in lanes_k]
    wave_hi, wave_lo = two_terms(np.stack([np.concatenate([w.real, w.imag], 1) for w in waves]))

    sens_rows = sens.reshape(rows * coils, packed)
    image_rows = image.reshape(rows * frames, packed)

    with jax.named_scope("coil_maps"):
        blocks = pl.pallas_call(
            functools.partial(coil_blocks_kernel, coils),
            grid=(1,),
            out_shape=f32(devices, 2 * own, rows, half),
            in_specs=lane_tiles(rows * coils, packed),
            out_specs=whole((devices, 2 * own, rows, half)),
            compiler_params=params(),
            cost_estimate=cost(0, 2 * sens.size * 4),
        )(*[sens_rows] * (packed // LANES))
        blocks, device = lax.optimization_barrier((blocks, device))
        coil_maps = lax.all_to_all(blocks, "coil", 0, 0, tiled=True)

    with jax.named_scope("column_maps"):
        level = 1
        early = (groups + 1) // 2
        keep_block = (devices // 2, 2 * groups - early, 2, cols, LANES)
        send_block = (devices // 2, early, 2, cols, LANES)
        column_keep, column_send = pl.pallas_call(
            functools.partial(column_blocks_kernel, coils, frames, chunk_of, level),
            grid=(1,),
            out_shape=(f32(*keep_block), f32(*send_block)),
            in_specs=[pl.BlockSpec(memory_space=pltpu.SMEM)]
            + lane_tiles(rows * coils, packed)
            + lane_tiles(rows * frames, packed),
            out_specs=(whole(keep_block), whole(send_block)),
            scratch_shapes=[pltpu.VMEM((2, half, LANES), jnp.float32)],
            compiler_params=params(),
            cost_estimate=cost(0, 2 * (sens.size + image.size) * 4),
        )(device[None], *[sens_rows] * (packed // LANES), *[image_rows] * (packed // LANES))
        column_send, device = lax.optimization_barrier((column_send, device))
        column_blocks = jnp.concatenate([column_keep, exchange(column_send, level)], 1)
        sides = [[with_bit(e, level, side) for e in range(devices // 2)] for side in range(2)]

    plans = [
        (frames // 2, list(range(1, bits))),
        (frames // 2, list(range(1, bits))),
    ]
    firsts = [sum(count for count, _ in plans[:i]) for i in range(len(plans))]
    span = half // 2
    smem = pl.BlockSpec(memory_space=pltpu.SMEM)
    kept, got = [], []
    for start, (count, _) in zip(firsts, plans):
        with jax.named_scope("data_transform"):
            block = pl.BlockSpec((own, 1, 2, span, length), lambda f: (0, f, 0, 0, 0))
            keep, send = pl.pallas_call(
                functools.partial(base_kernel, start, frames),
                grid=(count,),
                out_shape=(f32(own, count, 2, span, length),) * 2,
                in_specs=[
                    smem,
                    pl.BlockSpec(memory_space=pltpu.HBM),
                    whole((frames, length)),
                    whole((2, packed, packed)),
                    whole((2, 2, length, length)),
                ],
                out_specs=(block, block),
                scratch_shapes=[
                    pltpu.VMEM((2, own, length, packed), jnp.float32),
                    pltpu.VMEM((packed, packed), jnp.bfloat16),
                    pltpu.VMEM((packed, packed), jnp.bfloat16),
                    pltpu.VMEM((frames, length), jnp.float32),
                    pltpu.SemaphoreType.DMA((2, own, 2)),
                ],
                compiler_params=params(TRANSFORM_LIMIT),
                cost_estimate=cost(
                    own * count * 36 * half * half * length, 16 * own * count * half * length
                ),
            )(
                device[None],
                kspace.reshape(hl, 2, pairs, packed),
                mask,
                col_tables,
                row_tables,
            )
        if len(kept) == len(plans) - 1:
            column_blocks, send = lax.optimization_barrier((column_blocks, send))
        kept.append(keep)
        got.append(exchange(send, 0))
    with jax.named_scope("column_maps"):
        column_maps = lax.all_to_all(
            column_blocks, "coil", 0, 0, tiled=True, axis_index_groups=sides
        )
        column_late = exchange(column_maps[:, groups : 2 * groups - early], level)

    field = f32(frames, 2, cols, length)
    normal_cost = 6 * 2 * frames * coils * cols * length * length

    responses = pltpu.VMEM((2, frames, length), jnp.float32)

    anywhere = pl.BlockSpec(memory_space=pl.ANY)

    def first_gradient(column_maps, before):
        return pl.pallas_call(
            functools.partial(first_normal_kernel, coils, level),
            in_specs=[smem]
            + [pl.BlockSpec(memory_space=pltpu.VMEM)] * 5
            + [pl.BlockSpec(memory_space=pl.ANY)] * len(before),
            out_shape=(f32(coils, 2, cols, length), field, field),
            scratch_shapes=[responses],
            compiler_params=params(),
            cost_estimate=cost(normal_cost, 4 * sens.size * 4),
            name="first_gradient",
        )(device[None], column_maps, column_late, mask, wave_hi, wave_lo, *before)

    with jax.named_scope("data_term"):

        def weigh(stream, flip):
            count, order = plans[stream]
            outer = 2 ** (order[0] - 1)
            out = f32(devices // 4, count, 2, cols, length)
            base = pltpu.VMEM((own, count, 2, span // 2, length), jnp.float32)
            value = pl.pallas_call(
                functools.partial(weigh_kernel, outer, order[0], flip),
                out_shape=out,
                in_specs=[smem, anywhere, anywhere, anywhere],
                out_specs=anywhere,
                scratch_shapes=[
                    pltpu.VMEM((2 * own, 2, span, length), jnp.float32),
                    pltpu.VMEM((2 * own, devices, rows, half), jnp.float32),
                    base,
                    base,
                    pltpu.VMEM(out.shape, jnp.float32),
                    pltpu.SemaphoreType.DMA((2 * own,)),
                    pltpu.SemaphoreType.DMA((2, count, outer)),
                    pltpu.SemaphoreType.DMA((count,)),
                ],
                compiler_params=params(WEIGH_LIMIT),
                cost_estimate=cost(0, kept[stream].size * 4 + out.size * 4),
            )(device[None], coil_maps, kept[stream], got[stream])
            dims = [2] * (bits - 1)
            dims[order[0] - 1] = 1
            return value.reshape(*dims, *out.shape[1:])

        received = [exchange(weigh(i, 1), plans[i][1][0]) for i in range(len(plans))]
        terms = [(weigh(i, 0), received[i]) for i in range(len(plans))]
        sent = [None] * len(plans)

        def advance(stream, step):
            order = plans[stream][1]
            keep, sent[stream] = halve(*terms[stream], order[step], device)
            terms[stream] = (keep, exchange(sent[stream], order[step]))

        for step in range(1, bits - 1):
            for stream in range(len(plans)):
                advance(stream, step)
        maps, field0, grad0 = first_gradient(column_maps, sent)
        terms = [value.reshape(-1, 2, cols, length) for term in terms for value in term]

    with jax.named_scope("outer_steps"):
        blocks = pl.pallas_call(
            steps_kernel,
            out_shape=f32(devices, 2, cols, LANES),
            scratch_shapes=[pltpu.VMEM(field.shape, jnp.float32)] * 2 + [responses],
            compiler_params=params(),
            cost_estimate=cost(normal_cost, 4 * sens.size * 4),
        )(field0, grad0, maps, mask, wave_hi, wave_lo, *terms)

    with jax.named_scope("result_rows"):
        got = lax.all_to_all(blocks, "coil", 0, 0, tiled=True)
        recon = pl.pallas_call(
            functools.partial(rows_out_kernel, chunk_of, frames),
            out_shape=f32(rows * frames, packed),
            scratch_shapes=[pltpu.VMEM((packed // LANES, rows * frames, LANES), jnp.float32)],
            compiler_params=params(),
            cost_estimate=cost(0, 2 * image.size * 4),
        )(got)
    return recon.reshape(rows, frames, packed)


def einsum(form, left, right):
    return jnp.einsum(form, left, right, precision=highest, preferred_element_type=jnp.float32)


def complex_einsum(form, left, right):
    (a, b), (c, d) = left, right
    return (
        einsum(form, a, c) - einsum(form, b, d),
        einsum(form, a, d) + einsum(form, b, c),
    )


def general_path(image, sens, kspace, mask):
    rows, frames, packed = image.shape
    coils = sens.shape[1]
    length, pairs, _ = kspace.shape
    half = packed // 2
    devices = lax.axis_size("coil")
    device = lax.axis_index("coil")
    cols = half // devices

    def table(size):
        values = dft(np.arange(size), np.arange(size), size) / np.sqrt(size)
        return jnp.asarray(values.real, jnp.float32), jnp.asarray(values.imag, jnp.float32)

    inverse_rows, inverse_cols = table(length), table(half)
    forward_rows = (inverse_rows[0], -inverse_rows[1])

    both = jnp.concatenate([sens, image], 1).reshape(rows, coils + frames, 2, devices, cols)
    both = lax.all_to_all(both.transpose(3, 1, 2, 4, 0), "coil", 0, 0, tiled=True)
    both = both.transpose(1, 2, 3, 0, 4).reshape(coils + frames, 2, cols, length)
    maps, field = both[:coils], both[coils:]

    own = max(1, pairs // frames)
    repeats = devices * own // coils
    spread = jnp.repeat(sens.reshape(rows, coils // own, own, packed), repeats, axis=1)
    spread = spread.transpose(1, 0, 2, 3)
    coil_maps = lax.all_to_all(spread, "coil", 0, 0, tiled=True).reshape(length, own, packed)

    ids = device * pairs + lax.iota(jnp.int32, pairs)
    onehot = (ids[:, None] % frames == lax.iota(jnp.int32, frames)[None, :]).astype(jnp.float32)
    sampled = mask.astype(jnp.float32)
    data = einsum("pf,fk->kp", onehot, sampled)[:, :, None] * kspace
    data = (data[..., :half], data[..., half:])
    data = complex_einsum("kpz,zx->kpx", data, inverse_cols)
    data = complex_einsum("yk,kpx->ypx", inverse_rows, data)
    pair_maps = jnp.repeat(coil_maps, pairs // own, axis=1)
    m_re, m_im = pair_maps[..., :half], pair_maps[..., half:]
    weighted = jnp.stack(
        [m_re * data[0] + m_im * data[1], m_re * data[1] - m_im * data[0]], 2
    ).reshape(length, pairs, 2, devices, cols)
    term = einsum("ypcdx,pf->dfcxy", weighted, onehot)
    term = lax.psum_scatter(term, "coil", scatter_dimension=0, tiled=True)[0]

    masked = (
        sampled[:, :, None] * forward_rows[0][None],
        sampled[:, :, None] * forward_rows[1][None],
    )
    project = complex_einsum("yk,fkv->fyv", inverse_rows, masked)
    for sweep in range(OUTER):
        u_re = maps[:, None, 0] * field[None, :, 0] - maps[:, None, 1] * field[None, :, 1]
        u_im = maps[:, None, 0] * field[None, :, 1] + maps[:, None, 1] * field[None, :, 0]
        v_re, v_im = complex_einsum("fyv,cfxv->cfxy", project, (u_re, u_im))
        grad = jnp.stack(
            [
                jnp.sum(maps[:, None, 0] * v_re + maps[:, None, 1] * v_im, 0),
                jnp.sum(maps[:, None, 0] * v_im - maps[:, None, 1] * v_re, 0),
            ],
            1,
        )
        target = field - step_size * (grad - term)
        dual_time = jnp.zeros_like(target)
        dual_rows = jnp.zeros_like(target)
        field = target
        for repeat in range(INNER):
            diff_time = jnp.concatenate([field[1:] - field[:-1], jnp.zeros_like(field[:1])], 0)
            diff_rows = jnp.concatenate(
                [field[..., 1:] - field[..., :-1], jnp.zeros_like(field[..., :1])], -1
            )
            dual_time = jnp.clip(dual_time + dual_step * diff_time, -1.0, 1.0)
            dual_rows = jnp.clip(dual_rows + dual_step * diff_rows, -1.0, 1.0)
            inner_time, inner_rows = dual_time[:-1], dual_rows[..., :-1]
            none_time, none_rows = jnp.zeros_like(field[:1]), jnp.zeros_like(field[..., :1])
            divergence = (
                jnp.concatenate([none_time, inner_time], 0)
                - jnp.concatenate([inner_time, none_time], 0)
                + jnp.concatenate([none_rows, inner_rows], -1)
                - jnp.concatenate([inner_rows, none_rows], -1)
            )
            field = target - tv_weight * divergence

    result = field.reshape(frames, 2, cols, devices, rows).transpose(3, 0, 1, 2, 4)
    result = lax.all_to_all(result, "coil", 0, 0, tiled=True)
    return result.transpose(4, 1, 2, 0, 3).reshape(rows, frames, packed)


def fits_kernels(image, sens, kspace, devices):
    rows, frames, packed = image.shape
    coils = sens.shape[1]
    length, pairs, _ = kspace.shape
    per = LANES // rows
    return (
        devices & (devices - 1) == 0
        and devices >= 4
        and rows % 8 == 0
        and rows * per == LANES
        and frames == per
        and frames % 2 == 0
        and coils % per == 0
        and devices % per == 0
        and pairs % frames == 0
        and pairs * devices == coils * frames
        and length == 2 * LANES
        and packed % (16 * devices) == 0
        and packed % (4 * LANES) == 0
    )


def per_device(image, sens, kspace, mask):
    if fits_kernels(image, sens, kspace, lax.axis_size("coil")):
        return kernel_path(image, sens, kspace, mask)
    return general_path(image, sens, kspace, mask)


def solution(mesh):
    return jax.shard_map(
        per_device,
        mesh=mesh,
        in_specs=(
            P(("plane", "coil"), None, None),
            P(("plane", "coil"), None, None),
            P("plane", "coil", None),
            P(),
        ),
        out_specs=P(("plane", "coil"), None, None),
        check_vma=False,
    )
```

```python
import functools

import jax
import jax.numpy as jnp
import ml_dtypes
import numpy as np
from jax import lax
from jax.experimental import pallas as pl
from jax.experimental.pallas import tpu as pltpu
from jax.sharding import PartitionSpec as P

OUTER = 2
INNER = 2
LANES = 128
VMEM_LIMIT = 16 * 1024 * 1024
TRANSFORM_LIMIT = 52 * 1024 * 1024
WEIGH_LIMIT = 60 * 1024 * 1024

step_size = 0.5
tv_weight = 0.1
dual_step = 1.25
highest = lax.Precision.HIGHEST


def two_terms(table):
    first = table.astype(ml_dtypes.bfloat16)
    second = (table - first.astype(np.float64)).astype(ml_dtypes.bfloat16)
    return first, second


def dft(out_index, in_index, length):
    product = np.outer(out_index, in_index) % length
    return np.exp(2j * np.pi / length * product)


def packed_left(matrix):
    return np.block([[matrix.real, -matrix.imag], [matrix.imag, matrix.real]])


def packed_right(matrix):
    return packed_left(matrix).T


def split(value):
    first = value.astype(jnp.bfloat16)
    second = (value - first.astype(jnp.float32)).astype(jnp.bfloat16)
    return first, second


def dot3(left, right, contract=((1,), (0,))):
    dims = (contract, ((), ()))

    return lax.dot_general(
        jnp.concatenate([left[0], left[0], left[1]], contract[0][0]),
        jnp.concatenate([right[0], right[1], right[0]], contract[1][0]),
        dims,
        preferred_element_type=jnp.float32,
    )


def lane_exchange(parts, width):
    parts = list(parts)
    lane = lax.broadcasted_iota(jnp.int32, parts[0].shape, parts[0].ndim - 1)
    axis = parts[0].ndim - 1
    bit = 1
    while bit < len(parts):
        odd = (lane // width) & bit != 0
        for s in range(len(parts)):
            if s & bit:
                continue
            low, high = parts[s], parts[s | bit]
            parts[s] = jnp.where(odd, pltpu.roll(high, width * bit, axis), low)
            parts[s | bit] = jnp.where(odd, high, pltpu.roll(low, LANES - width * bit, axis))
        bit *= 2
    return parts


def roll_last(value, distance):
    shape = value.shape
    flat = value.reshape(-1, shape[-1])
    return pltpu.roll(flat, distance % shape[-1], 1).reshape(shape)


def tv_step(target):
    length = target.shape[-1]
    row = lax.broadcasted_iota(jnp.int32, target.shape, target.ndim - 1)
    last, first = row == length - 1, row == 0
    nothing = jnp.zeros_like(target[:1])

    def adjoint(dual_time, dual_rows):
        from_time = jnp.concatenate([nothing, dual_time[:-1]], 0) - jnp.concatenate(
            [dual_time[:-1], nothing], 0
        )
        from_rows = jnp.where(first, 0.0, roll_last(dual_rows, 1)) - jnp.where(last, 0.0, dual_rows)
        return from_time + from_rows

    dual_time = jnp.zeros_like(target)
    dual_rows = jnp.zeros_like(target)
    primal = target
    for repeat in range(INNER):
        diff_time = jnp.concatenate([primal[1:] - primal[:-1], nothing], 0)
        diff_rows = jnp.where(last, 0.0, roll_last(primal, -1) - primal)
        dual_time = jnp.clip(dual_time + dual_step * diff_time, -1.0, 1.0)
        dual_rows = jnp.clip(dual_rows + dual_step * diff_rows, -1.0, 1.0)
        primal = target - tv_weight * adjoint(dual_time, dual_rows)
    return primal


def parted_mask(mask_ref):
    length = mask_ref.shape[1]
    line = lax.broadcasted_iota(jnp.int32, (length, length), 0)
    lane = lax.broadcasted_iota(jnp.int32, (length, length), 1)
    half = length // 2
    place = jnp.where(lane < half, 2 * lane, 2 * (lane - half) + 1)
    permutation = (line == place).astype(jnp.float32).astype(jnp.bfloat16)
    mask = mask_ref[...].astype(jnp.float32).astype(jnp.bfloat16)
    return jnp.dot(mask, permutation, preferred_element_type=jnp.float32)


def mask_responses(mask_ref, wave_hi, wave_lo, out_ref):
    parted = parted_mask(mask_ref).astype(jnp.bfloat16)
    half = parted.shape[1] // 2
    for side in range(2):
        mask = parted[:, side * half : (side + 1) * half]
        terms = [
            jnp.dot(mask, wave[side], preferred_element_type=jnp.float32)
            for wave in (wave_hi, wave_lo)
        ]
        out_ref[side] = terms[0] + terms[1]


def frame_tables(response_ref, f):
    half = response_ref.shape[-1] // 2
    tables = []
    for side in range(2):
        row = response_ref[side, pl.ds(f, 1), :]
        parts = []
        for at in (0, half):
            spread = jnp.broadcast_to(row[:, at : at + half], (half, half))
            turned = pltpu.roll(spread, 0, 1, stride=1, stride_axis=0)
            if side:
                before = lax.broadcasted_iota(jnp.int32, (half, half), 1) < (
                    lax.broadcasted_iota(jnp.int32, (half, half), 0)
                )
                turned = jnp.where(before, -turned, turned)
            parts.append(turned)
        re, im = parts
        tables.append(
            split(jnp.concatenate([jnp.concatenate([re, im], 1), jnp.concatenate([-im, re], 1)], 0))
        )
    return tables


def normal_coils(maps_ref, field_re, field_im, tables):
    coils, _, cols, length = maps_ref.shape
    half = length // 2
    maps_re, maps_im = maps_ref[:, 0], maps_ref[:, 1]
    u_re = maps_re * field_re[None] - maps_im * field_im[None]
    u_im = maps_re * field_im[None] + maps_im * field_re[None]
    flat_re = u_re.reshape(coils * cols, length)
    flat_im = u_im.reshape(coils * cols, length)
    outs = []
    for sign, table in zip((1.0, -1.0), tables):
        packed = jnp.concatenate(
            [
                flat_re[:, :half] + sign * flat_re[:, half:],
                flat_im[:, :half] + sign * flat_im[:, half:],
            ],
            1,
        )
        outs.append(dot3(split(packed), table))
    plus, minus = outs
    v_re = jnp.concatenate(
        [plus[:, :half] + minus[:, :half], plus[:, :half] - minus[:, :half]], 1
    ).reshape(coils, cols, length)
    v_im = jnp.concatenate(
        [plus[:, half:] + minus[:, half:], plus[:, half:] - minus[:, half:]], 1
    ).reshape(coils, cols, length)
    return (
        jnp.sum(maps_re * v_re + maps_im * v_im, 0),
        jnp.sum(maps_re * v_im - maps_im * v_re, 0),
    )


def normal_frame(maps_ref, field_re, field_im, tables):
    middle = maps_ref.shape[0] // 2
    first = normal_coils(maps_ref.at[:middle], field_re, field_im, tables)
    second = normal_coils(maps_ref.at[middle:], field_re, field_im, tables)
    return first[0] + second[0], first[1] + second[1]


def coil_blocks_kernel(coils, *refs):
    *tiles, out_ref = refs
    devices, pair_coils, rows, lanes = out_ref.shape
    halves = len(tiles) // 2
    each = lanes // (2 * LANES)
    step = 8
    for part in range(2):
        for side in range(2):
            for t in range(each):
                ref = tiles[part * halves + side * each + t]
                at = (part * each + t) * LANES
                for first in range(0, coils, step):
                    for row in range(0, rows, step):
                        turned = jnp.swapaxes(ref[row : row + step, first : first + step], 0, 1)
                        for c in range(first, first + step):
                            d = c // pair_coils * 2 + side
                            out_ref[d, c % pair_coils, row : row + step, at : at + LANES] = turned[
                                c - first
                            ]


def with_bit(index, bit, value):
    return ((index >> bit) << (bit + 1)) | (value << bit) | (index & ((1 << bit) - 1))


def column_blocks_kernel(coils, frames, chunk_of, level, device_ref, *refs):
    *tiles, keep_ref, send_ref, turned = refs
    sens_tiles, image_tiles = tiles[: len(tiles) // 2], tiles[len(tiles) // 2 :]
    blocks, early, _, cols, _ = send_ref.shape
    groups = (keep_ref.shape[1] + early) // 2
    rows = sens_tiles[0].shape[0] // coils
    per = LANES // rows
    half = len(sens_tiles) // 2
    mine = (device_ref[0] >> level) & 1
    far = chunk_of[1 << level] * cols
    for g in range(groups):
        if g * per < coils:
            tiles, count, base = sens_tiles, coils, g * per
        else:
            tiles, count, base = image_tiles, frames, g * per - coils
        for t, ref in enumerate(tiles):
            turned[t // half, pl.ds(t % half * LANES, LANES)] = jnp.concatenate(
                [ref[pl.ds(base + c, rows, stride=count), :] for c in range(per)], 0
            ).T
        other = (send_ref, g) if g < early else (keep_ref, g + groups - early)
        for (out, unit), side in (((keep_ref, g), mine), (other, 1 - mine)):
            for e in range(blocks):
                at = pl.multiple_of(chunk_of[with_bit(e, level, 0)] * cols + side * far, cols)
                for part in range(2):
                    out[e, unit, part] = turned[part, pl.ds(at, cols)]


def base_kernel(start, frames, device_ref, kspace_ref, mask_ref, *refs):
    cols_ref, rows_ref, keep_ref, send_ref, data, near_hi, near_lo, masks, arrived = refs
    own, _, _, span, length = keep_ref.shape
    bit = device_ref[0] & 1
    half = length // 2
    frame = pl.program_id(0)

    def fetch(f, slot):
        return [
            pltpu.make_async_copy(
                kspace_ref.at[:, odd, start + f + c * frames, :],
                data.at[slot, c, pl.ds(odd * half, half)],
                arrived.at[slot, c, odd],
            )
            for c in range(own)
            for odd in range(2)
        ]

    @pl.when(frame == 0)
    def _():
        for copy in fetch(0, 0):
            copy.start()
        masks[...] = parted_mask(mask_ref)
        for term, near in enumerate((near_hi, near_lo)):
            for i, which in enumerate((bit, 1 - bit)):
                for part in range(2):
                    at = pl.multiple_of((2 * part + which) * span, span)
                    near[pl.ds((2 * i + part) * span, span)] = cols_ref[term, pl.ds(at, span)]

    @pl.when(frame + 1 < pl.num_programs(0))
    def _():
        for copy in fetch(frame + 1, (frame + 1) % 2):
            copy.start()

    slot = frame % 2
    for copy in fetch(frame, slot):
        copy.wait()
    columns = [
        dot3((near_hi[...], near_lo[...]), split(data[slot, c]), ((1,), (1,)))
        * masks[pl.ds(start + frame, 1), :]
        for c in range(own)
    ]
    blocks = [v[2 * i * span : (2 * i + 2) * span] for v in columns for i in range(2)]
    sides = []
    for odd in range(2):
        at = odd * half
        stacked = jnp.concatenate(
            [
                jnp.concatenate([v[:span, at : at + half], v[span:, at : at + half]], 1)
                for v in blocks
            ],
            0,
        )
        sides.append(dot3(split(stacked), (rows_ref[0, odd], rows_ref[1, odd])))
    for c in range(own):
        for i, ref in enumerate((keep_ref, send_ref)):
            rows = (2 * c + i) * span
            even, odd = [side[rows : rows + span] for side in sides]
            for part in range(2):
                e = even[:, part * half : (part + 1) * half]
                o = odd[:, part * half : (part + 1) * half]
                ref[c, 0, part] = jnp.concatenate([e + o, e - o], 1)


def weigh_kernel(outer, level, flip, device_ref, maps_ref, kept_ref, got_ref, out_ref, *refs):
    turned, maps, kept, got, total, maps_arrived, arrived, left = refs
    devices, pair_coils, rows, lanes = maps_ref.shape
    own, count = got_ref.shape[:2]
    inner, _, _, cols, length = total.shape
    inner //= outer
    span = inner * cols
    bit, which = device_ref[0] & 1, ((device_ref[0] >> level) & 1) ^ flip
    far = [pl.multiple_of((2 * i + which) * span, span) for i in range(outer)]

    map_copies = [
        pltpu.make_async_copy(maps_ref.at[:, c], maps.at[c], maps_arrived.at[c])
        for c in range(pair_coils)
    ]
    for copy in map_copies:
        copy.start()
    copies = [
        [
            pltpu.make_async_copy(
                src.at[:, f, :, pl.ds(far[i], span)],
                dst.at[:, f, :, pl.ds(i * span, span)],
                arrived.at[j, f, i],
            )
            for j, (src, dst) in enumerate(((kept_ref, kept), (got_ref, got)))
            for i in range(outer)
        ]
        for f in range(count)
    ]
    for group in copies:
        for copy in group:
            copy.start()
    for c in range(pair_coils):
        map_copies[c].wait()
        one = maps[c].reshape(length, lanes).T
        turned[c, 0] = one[: lanes // 2]
        turned[c, 1] = one[lanes // 2 :]

    results = []
    for f in range(count):
        for copy in copies[f]:
            copy.wait()
        for i in range(outer):
            here = slice(i * span, (i + 1) * span)
            total_re = total_im = 0.0
            for base, first in ((kept, bit * own), (got, (1 - bit) * own)):
                for c in range(own):
                    s_re = turned[first + c, 0, pl.ds(far[i], span), :]
                    s_im = turned[first + c, 1, pl.ds(far[i], span), :]
                    b_re, b_im = base[c, f, 0, here, :], base[c, f, 1, here, :]
                    total_re += s_re * b_re + s_im * b_im
                    total_im += s_re * b_im - s_im * b_re
            total[i * inner : (i + 1) * inner, f, 0] = total_re.reshape(inner, cols, length)
            total[i * inner : (i + 1) * inner, f, 1] = total_im.reshape(inner, cols, length)
        results.append(pltpu.make_async_copy(total.at[:, f], out_ref.at[:, f], left.at[f]))
        results[-1].start()
    for copy in results:
        copy.wait()


def first_normal_kernel(
    coils, level, device_ref, got_ref, late_ref, mask_ref, wave_hi, wave_lo, *refs
):
    maps_out, field_out, grad_out, responses = refs[-4:]
    mask_responses(mask_ref, wave_hi, wave_lo, responses)
    blocks, units, _, cols, lanes = got_ref.shape
    groups = units // 2
    early = groups - late_ref.shape[1]
    devices = 2 * blocks
    mine = (device_ref[0] >> level) & 1
    frames = field_out.shape[0]

    def block(s, g):
        e = ((s >> (level + 1)) << level) | (s & ((1 << level) - 1))
        across = ((s >> level) & 1) ^ mine
        if g < early:
            return got_ref[e, g + across * (units - early)]
        return jnp.where(across == 0, got_ref[e, g], late_ref[e, g - early])

    per = (coils + frames) // groups
    width = lanes // per
    for g in range(groups):
        out, base = (maps_out, g * per) if g * per < coils else (field_out, g * per - coils)
        for h in range(devices // per):
            exchanged = lane_exchange([block(h * per + s, g) for s in range(per)], width)
            for c in range(per):
                out[base + c, :, :, h * lanes : (h + 1) * lanes] = exchanged[c]

    def one(f, _):
        grad_out[f, 0], grad_out[f, 1] = normal_frame(
            maps_out, field_out[f, 0], field_out[f, 1], frame_tables(responses, f)
        )
        return 0

    lax.fori_loop(0, frames, one, 0, unroll=frames)


def steps_kernel(field_ref, grad_ref, maps_ref, mask_ref, *refs):
    wave_hi, wave_lo, *terms, out_ref, field, grad, responses = refs
    frames, _, cols, length = field_ref.shape
    devices, _, _, lanes = out_ref.shape
    mask_responses(mask_ref, wave_hi, wave_lo, responses)
    data_term = jnp.concatenate(
        [keep[...] + got[...] for keep, got in zip(terms[0::2], terms[1::2])], 0
    )
    field[...] = tv_step(field_ref[...] - step_size * (grad_ref[...] - data_term))
    for sweep in range(1, OUTER):

        def one(f, _):
            grad[f, 0], grad[f, 1] = normal_frame(
                maps_ref, field[f, 0], field[f, 1], frame_tables(responses, f)
            )
            return 0

        lax.fori_loop(0, frames, one, 0, unroll=frames)
        field[...] = tv_step(field[...] - step_size * (grad[...] - data_term))
    per = frames
    for h in range(devices // per):
        parts = [field[f, :, :, h * lanes : (h + 1) * lanes] for f in range(per)]
        exchanged = lane_exchange(parts, lanes // per)
        for s in range(per):
            out_ref[h * per + s] = exchanged[s]


def rows_out_kernel(chunk_of, frames, got_ref, out_ref, tiles):
    devices, _, cols, lanes = got_ref.shape
    count = tiles.shape[0]
    rows = lanes // frames
    order = sorted(range(devices), key=lambda d: chunk_of[d])
    each = LANES // cols
    for t in range(count):
        at = t % (count // 2) * each
        turned = jnp.concatenate([got_ref[d, t // (count // 2)] for d in order[at : at + each]], 0).T
        for f in range(frames):
            tiles[t, pl.ds(f, rows, stride=frames), :] = turned[f * rows : (f + 1) * rows]
        out_ref[:, t * LANES : (t + 1) * LANES] = tiles[t]


def params(limit=VMEM_LIMIT):
    return pltpu.CompilerParams(vmem_limit_bytes=limit)


def cost(flops, moved):
    return pl.CostEstimate(flops=int(flops), bytes_accessed=int(moved), transcendentals=0)


def whole(shape):
    return pl.BlockSpec(shape, lambda *_: (0,) * len(shape))


def lane_tiles(rows, lanes):
    return [
        pl.BlockSpec((rows, LANES), lambda *_, t=t: (0, t), pipeline_mode=pl.Buffered(1))
        for t in range(lanes // LANES)
    ]


def f32(*shape):
    return jax.ShapeDtypeStruct(shape, jnp.float32)


def exchange(send, bit):
    devices = lax.axis_size("coil")
    return lax.ppermute(send, "coil", [(i, i ^ (1 << bit)) for i in range(devices)])


def halve(keep, got, bit, device):
    mine = (device >> bit) & 1

    def part(which):
        return lax.dynamic_index_in_dim(
            keep, which, bit - 1, keepdims=True
        ) + lax.dynamic_index_in_dim(got, which, bit - 1, keepdims=True)

    send = part(1 - mine)
    return part(mine), send


def kernel_path(image, sens, kspace, mask):
    rows, frames, packed = image.shape
    coils = sens.shape[1]
    length, pairs, _ = kspace.shape
    half = packed // 2
    hl = length // 2
    devices = lax.axis_size("coil")
    device = lax.axis_index("coil")
    bits = devices.bit_length() - 1
    own = pairs // frames
    cols = half // devices
    per = LANES // rows
    groups = (coils + frames) // per
    chunk_of = [sum(((d >> b) & 1) << (bits - 1 - b) for b in range(bits)) for d in range(devices)]

    k = np.arange(length)
    z = np.arange(half)
    y = np.arange(hl)
    col_tables = np.stack(two_terms(packed_left(dft(z, z, half) / np.sqrt(half))))
    lanes_k = [k[0::2], k[1::2]]
    inverse = [packed_right(dft(y, ks, length)) for ks in lanes_k]
    row_tables = np.stack(two_terms(np.stack(inverse) / np.sqrt(length)))
    waves = [dft(ks, y, length) * 0.5 / hl for ks in lanes_k]
    wave_hi, wave_lo = two_terms(np.stack([np.concatenate([w.real, w.imag], 1) for w in waves]))

    sens_rows = sens.reshape(rows * coils, packed)
    image_rows = image.reshape(rows * frames, packed)

    with jax.named_scope("coil_maps"):
        blocks = pl.pallas_call(
            functools.partial(coil_blocks_kernel, coils),
            grid=(1,),
            out_shape=f32(devices, 2 * own, rows, half),
            in_specs=[
                pl.BlockSpec((rows, coils, LANES), lambda *_, t=t: (0, 0, t))
                for t in range(packed // LANES)
            ],
            out_specs=whole((devices, 2 * own, rows, half)),
            compiler_params=params(),
            cost_estimate=cost(0, 2 * sens.size * 4),
        )(*[sens] * (packed // LANES))
        blocks, device = lax.optimization_barrier((blocks, device))
        coil_maps = lax.all_to_all(blocks, "coil", 0, 0, tiled=True)

    with jax.named_scope("column_maps"):
        level = 1
        early = (groups + 1) // 2
        keep_block = (devices // 2, 2 * groups - early, 2, cols, LANES)
        send_block = (devices // 2, early, 2, cols, LANES)
        column_keep, column_send = pl.pallas_call(
            functools.partial(column_blocks_kernel, coils, frames, chunk_of, level),
            grid=(1,),
            out_shape=(f32(*keep_block), f32(*send_block)),
            in_specs=[pl.BlockSpec(memory_space=pltpu.SMEM)]
            + lane_tiles(rows * coils, packed)
            + lane_tiles(rows * frames, packed),
            out_specs=(whole(keep_block), whole(send_block)),
            scratch_shapes=[pltpu.VMEM((2, half, LANES), jnp.float32)],
            compiler_params=params(),
            cost_estimate=cost(0, 2 * (sens.size + image.size) * 4),
        )(device[None], *[sens_rows] * (packed // LANES), *[image_rows] * (packed // LANES))
        column_send, device = lax.optimization_barrier((column_send, device))
        column_blocks = jnp.concatenate([column_keep, exchange(column_send, level)], 1)
        sides = [[with_bit(e, level, side) for e in range(devices // 2)] for side in range(2)]

    plans = [
        (frames // 2, list(range(1, bits))),
        (frames // 2, list(range(1, bits))),
    ]
    firsts = [sum(count for count, _ in plans[:i]) for i in range(len(plans))]
    span = half // 2
    smem = pl.BlockSpec(memory_space=pltpu.SMEM)
    kept, got = [], []
    for start, (count, _) in zip(firsts, plans):
        with jax.named_scope("data_transform"):
            block = pl.BlockSpec((own, 1, 2, span, length), lambda f: (0, f, 0, 0, 0))
            keep, send = pl.pallas_call(
                functools.partial(base_kernel, start, frames),
                grid=(count,),
                out_shape=(f32(own, count, 2, span, length),) * 2,
                in_specs=[
                    smem,
                    pl.BlockSpec(memory_space=pltpu.HBM),
                    whole((frames, length)),
                    whole((2, packed, packed)),
                    whole((2, 2, length, length)),
                ],
                out_specs=(block, block),
                scratch_shapes=[
                    pltpu.VMEM((2, own, length, packed), jnp.float32),
                    pltpu.VMEM((packed, packed), jnp.bfloat16),
                    pltpu.VMEM((packed, packed), jnp.bfloat16),
                    pltpu.VMEM((frames, length), jnp.float32),
                    pltpu.SemaphoreType.DMA((2, own, 2)),
                ],
                compiler_params=params(TRANSFORM_LIMIT),
                cost_estimate=cost(
                    own * count * 36 * half * half * length, 16 * own * count * half * length
                ),
            )(
                device[None],
                kspace.reshape(hl, 2, pairs, packed),
                mask,
                col_tables,
                row_tables,
            )
        if len(kept) == len(plans) - 1:
            column_blocks, send = lax.optimization_barrier((column_blocks, send))
        kept.append(keep)
        got.append(exchange(send, 0))
    with jax.named_scope("column_maps"):
        column_maps = lax.all_to_all(
            column_blocks, "coil", 0, 0, tiled=True, axis_index_groups=sides
        )
        column_late = exchange(column_maps[:, groups : 2 * groups - early], level)

    field = f32(frames, 2, cols, length)
    normal_cost = 6 * 2 * frames * coils * cols * length * length

    responses = pltpu.VMEM((2, frames, length), jnp.float32)

    anywhere = pl.BlockSpec(memory_space=pl.ANY)

    def first_gradient(column_maps, before):
        return pl.pallas_call(
            functools.partial(first_normal_kernel, coils, level),
            in_specs=[smem]
            + [pl.BlockSpec(memory_space=pltpu.VMEM)] * 5
            + [pl.BlockSpec(memory_space=pl.ANY)] * len(before),
            out_shape=(f32(coils, 2, cols, length), field, field),
            scratch_shapes=[responses],
            compiler_params=params(),
            cost_estimate=cost(normal_cost, 4 * sens.size * 4),
            name="first_gradient",
        )(device[None], column_maps, column_late, mask, wave_hi, wave_lo, *before)

    with jax.named_scope("data_term"):

        def weigh(stream, flip):
            count, order = plans[stream]
            outer = 2 ** (order[0] - 1)
            out = f32(devices // 4, count, 2, cols, length)
            base = pltpu.VMEM((own, count, 2, span // 2, length), jnp.float32)
            value = pl.pallas_call(
                functools.partial(weigh_kernel, outer, order[0], flip),
                out_shape=out,
                in_specs=[smem, anywhere, anywhere, anywhere],
                out_specs=anywhere,
                scratch_shapes=[
                    pltpu.VMEM((2 * own, 2, span, length), jnp.float32),
                    pltpu.VMEM((2 * own, devices, rows, half), jnp.float32),
                    base,
                    base,
                    pltpu.VMEM(out.shape, jnp.float32),
                    pltpu.SemaphoreType.DMA((2 * own,)),
                    pltpu.SemaphoreType.DMA((2, count, outer)),
                    pltpu.SemaphoreType.DMA((count,)),
                ],
                compiler_params=params(WEIGH_LIMIT),
                cost_estimate=cost(0, kept[stream].size * 4 + out.size * 4),
            )(device[None], coil_maps, kept[stream], got[stream])
            dims = [2] * (bits - 1)
            dims[order[0] - 1] = 1
            return value.reshape(*dims, *out.shape[1:])

        received = [exchange(weigh(i, 1), plans[i][1][0]) for i in range(len(plans))]
        terms = [(weigh(i, 0), received[i]) for i in range(len(plans))]
        sent = [None] * len(plans)

        def advance(stream, step):
            order = plans[stream][1]
            keep, sent[stream] = halve(*terms[stream], order[step], device)
            terms[stream] = (keep, exchange(sent[stream], order[step]))

        for step in range(1, bits - 1):
            for stream in range(len(plans)):
                advance(stream, step)
        maps, field0, grad0 = first_gradient(column_maps, sent)
        terms = [value.reshape(-1, 2, cols, length) for term in terms for value in term]

    with jax.named_scope("outer_steps"):
        blocks = pl.pallas_call(
            steps_kernel,
            out_shape=f32(devices, 2, cols, LANES),
            scratch_shapes=[pltpu.VMEM(field.shape, jnp.float32)] * 2 + [responses],
            compiler_params=params(),
            cost_estimate=cost(normal_cost, 4 * sens.size * 4),
        )(field0, grad0, maps, mask, wave_hi, wave_lo, *terms)

    with jax.named_scope("result_rows"):
        got = lax.all_to_all(blocks, "coil", 0, 0, tiled=True)
        recon = pl.pallas_call(
            functools.partial(rows_out_kernel, chunk_of, frames),
            out_shape=f32(rows * frames, packed),
            scratch_shapes=[pltpu.VMEM((packed // LANES, rows * frames, LANES), jnp.float32)],
            compiler_params=params(),
            cost_estimate=cost(0, 2 * image.size * 4),
        )(got)
    return recon.reshape(rows, frames, packed)


def einsum(form, left, right):
    return jnp.einsum(form, left, right, precision=highest, preferred_element_type=jnp.float32)


def complex_einsum(form, left, right):
    (a, b), (c, d) = left, right
    return (
        einsum(form, a, c) - einsum(form, b, d),
        einsum(form, a, d) + einsum(form, b, c),
    )


def general_path(image, sens, kspace, mask):
    rows, frames, packed = image.shape
    coils = sens.shape[1]
    length, pairs, _ = kspace.shape
    half = packed // 2
    devices = lax.axis_size("coil")
    device = lax.axis_index("coil")
    cols = half // devices

    def table(size):
        values = dft(np.arange(size), np.arange(size), size) / np.sqrt(size)
        return jnp.asarray(values.real, jnp.float32), jnp.asarray(values.imag, jnp.float32)

    inverse_rows, inverse_cols = table(length), table(half)
    forward_rows = (inverse_rows[0], -inverse_rows[1])

    both = jnp.concatenate([sens, image], 1).reshape(rows, coils + frames, 2, devices, cols)
    both = lax.all_to_all(both.transpose(3, 1, 2, 4, 0), "coil", 0, 0, tiled=True)
    both = both.transpose(1, 2, 3, 0, 4).reshape(coils + frames, 2, cols, length)
    maps, field = both[:coils], both[coils:]

    own = max(1, pairs // frames)
    repeats = devices * own // coils
    spread = jnp.repeat(sens.reshape(rows, coils // own, own, packed), repeats, axis=1)
    spread = spread.transpose(1, 0, 2, 3)
    coil_maps = lax.all_to_all(spread, "coil", 0, 0, tiled=True).reshape(length, own, packed)

    ids = device * pairs + lax.iota(jnp.int32, pairs)
    onehot = (ids[:, None] % frames == lax.iota(jnp.int32, frames)[None, :]).astype(jnp.float32)
    sampled = mask.astype(jnp.float32)
    data = einsum("pf,fk->kp", onehot, sampled)[:, :, None] * kspace
    data = (data[..., :half], data[..., half:])
    data = complex_einsum("kpz,zx->kpx", data, inverse_cols)
    data = complex_einsum("yk,kpx->ypx", inverse_rows, data)
    pair_maps = jnp.repeat(coil_maps, pairs // own, axis=1)
    m_re, m_im = pair_maps[..., :half], pair_maps[..., half:]
    weighted = jnp.stack(
        [m_re * data[0] + m_im * data[1], m_re * data[1] - m_im * data[0]], 2
    ).reshape(length, pairs, 2, devices, cols)
    term = einsum("ypcdx,pf->dfcxy", weighted, onehot)
    term = lax.psum_scatter(term, "coil", scatter_dimension=0, tiled=True)[0]

    masked = (
        sampled[:, :, None] * forward_rows[0][None],
        sampled[:, :, None] * forward_rows[1][None],
    )
    project = complex_einsum("yk,fkv->fyv", inverse_rows, masked)
    for sweep in range(OUTER):
        u_re = maps[:, None, 0] * field[None, :, 0] - maps[:, None, 1] * field[None, :, 1]
        u_im = maps[:, None, 0] * field[None, :, 1] + maps[:, None, 1] * field[None, :, 0]
        v_re, v_im = complex_einsum("fyv,cfxv->cfxy", project, (u_re, u_im))
        grad = jnp.stack(
            [
                jnp.sum(maps[:, None, 0] * v_re + maps[:, None, 1] * v_im, 0),
                jnp.sum(maps[:, None, 0] * v_im - maps[:, None, 1] * v_re, 0),
            ],
            1,
        )
        target = field - step_size * (grad - term)
        dual_time = jnp.zeros_like(target)
        dual_rows = jnp.zeros_like(target)
        field = target
        for repeat in range(INNER):
            diff_time = jnp.concatenate([field[1:] - field[:-1], jnp.zeros_like(field[:1])], 0)
            diff_rows = jnp.concatenate(
                [field[..., 1:] - field[..., :-1], jnp.zeros_like(field[..., :1])], -1
            )
            dual_time = jnp.clip(dual_time + dual_step * diff_time, -1.0, 1.0)
            dual_rows = jnp.clip(dual_rows + dual_step * diff_rows, -1.0, 1.0)
            inner_time, inner_rows = dual_time[:-1], dual_rows[..., :-1]
            none_time, none_rows = jnp.zeros_like(field[:1]), jnp.zeros_like(field[..., :1])
            divergence = (
                jnp.concatenate([none_time, inner_time], 0)
                - jnp.concatenate([inner_time, none_time], 0)
                + jnp.concatenate([none_rows, inner_rows], -1)
                - jnp.concatenate([inner_rows, none_rows], -1)
            )
            field = target - tv_weight * divergence

    result = field.reshape(frames, 2, cols, devices, rows).transpose(3, 0, 1, 2, 4)
    result = lax.all_to_all(result, "coil", 0, 0, tiled=True)
    return result.transpose(4, 1, 2, 0, 3).reshape(rows, frames, packed)


def fits_kernels(image, sens, kspace, devices):
    rows, frames, packed = image.shape
    coils = sens.shape[1]
    length, pairs, _ = kspace.shape
    per = LANES // rows
    return (
        devices & (devices - 1) == 0
        and devices >= 4
        and rows % 8 == 0
        and rows * per == LANES
        and frames == per
        and frames % 2 == 0
        and coils % per == 0
        and devices % per == 0
        and pairs % frames == 0
        and pairs * devices == coils * frames
        and length == 2 * LANES
        and packed % (16 * devices) == 0
        and packed % (4 * LANES) == 0
    )


def per_device(image, sens, kspace, mask):
    if fits_kernels(image, sens, kspace, lax.axis_size("coil")):
        return kernel_path(image, sens, kspace, mask)
    return general_path(image, sens, kspace, mask)


def solution(mesh):
    return jax.shard_map(
        per_device,
        mesh=mesh,
        in_specs=(
            P(("plane", "coil"), None, None),
            P(("plane", "coil"), None, None),
            P("plane", "coil", None),
            P(),
        ),
        out_specs=P(("plane", "coil"), None, None),
        check_vma=False,
    )
```

```python
import functools

import jax
import jax.numpy as jnp
import ml_dtypes
import numpy as np
from jax import lax
from jax.experimental import pallas as pl
from jax.experimental.pallas import tpu as pltpu
from jax.sharding import PartitionSpec as P

OUTER = 2
INNER = 2
LANES = 128
VMEM_LIMIT = 16 * 1024 * 1024
TRANSFORM_LIMIT = 52 * 1024 * 1024
WEIGH_LIMIT = 60 * 1024 * 1024

step_size = 0.5
tv_weight = 0.1
dual_step = 1.25
highest = lax.Precision.HIGHEST


def two_terms(table):
    first = table.astype(ml_dtypes.bfloat16)
    second = (table - first.astype(np.float64)).astype(ml_dtypes.bfloat16)
    return first, second


def dft(out_index, in_index, length):
    product = np.outer(out_index, in_index) % length
    return np.exp(2j * np.pi / length * product)


def packed_left(matrix):
    return np.block([[matrix.real, -matrix.imag], [matrix.imag, matrix.real]])


def packed_right(matrix):
    return packed_left(matrix).T


def split(value):
    first = value.astype(jnp.bfloat16)
    second = (value - first.astype(jnp.float32)).astype(jnp.bfloat16)
    return first, second


def dot3(left, right, contract=((1,), (0,))):
    dims = (contract, ((), ()))

    return lax.dot_general(
        jnp.concatenate([left[0], left[0], left[1]], contract[0][0]),
        jnp.concatenate([right[0], right[1], right[0]], contract[1][0]),
        dims,
        preferred_element_type=jnp.float32,
    )


def lane_exchange(parts, width):
    parts = list(parts)
    lane = lax.broadcasted_iota(jnp.int32, parts[0].shape, parts[0].ndim - 1)
    axis = parts[0].ndim - 1
    bit = 1
    while bit < len(parts):
        odd = (lane // width) & bit != 0
        for s in range(len(parts)):
            if s & bit:
                continue
            low, high = parts[s], parts[s | bit]
            parts[s] = jnp.where(odd, pltpu.roll(high, width * bit, axis), low)
            parts[s | bit] = jnp.where(odd, high, pltpu.roll(low, LANES - width * bit, axis))
        bit *= 2
    return parts


def roll_last(value, distance):
    shape = value.shape
    flat = value.reshape(-1, shape[-1])
    return pltpu.roll(flat, distance % shape[-1], 1).reshape(shape)


def tv_step(target):
    length = target.shape[-1]
    row = lax.broadcasted_iota(jnp.int32, target.shape, target.ndim - 1)
    last, first = row == length - 1, row == 0
    nothing = jnp.zeros_like(target[:1])

    def adjoint(dual_time, dual_rows):
        from_time = jnp.concatenate([nothing, dual_time[:-1]], 0) - jnp.concatenate(
            [dual_time[:-1], nothing], 0
        )
        from_rows = jnp.where(first, 0.0, roll_last(dual_rows, 1)) - jnp.where(last, 0.0, dual_rows)
        return from_time + from_rows

    dual_time = jnp.zeros_like(target)
    dual_rows = jnp.zeros_like(target)
    primal = target
    for repeat in range(INNER):
        diff_time = jnp.concatenate([primal[1:] - primal[:-1], nothing], 0)
        diff_rows = jnp.where(last, 0.0, roll_last(primal, -1) - primal)
        dual_time = jnp.clip(dual_time + dual_step * diff_time, -1.0, 1.0)
        dual_rows = jnp.clip(dual_rows + dual_step * diff_rows, -1.0, 1.0)
        primal = target - tv_weight * adjoint(dual_time, dual_rows)
    return primal


def parted_mask(mask_ref):
    length = mask_ref.shape[1]
    line = lax.broadcasted_iota(jnp.int32, (length, length), 0)
    lane = lax.broadcasted_iota(jnp.int32, (length, length), 1)
    half = length // 2
    place = jnp.where(lane < half, 2 * lane, 2 * (lane - half) + 1)
    permutation = (line == place).astype(jnp.float32).astype(jnp.bfloat16)
    mask = mask_ref[...].astype(jnp.float32).astype(jnp.bfloat16)
    return jnp.dot(mask, permutation, preferred_element_type=jnp.float32)


def mask_responses(mask_ref, wave_hi, wave_lo, out_ref):
    parted = parted_mask(mask_ref).astype(jnp.bfloat16)
    half = parted.shape[1] // 2
    for side in range(2):
        mask = parted[:, side * half : (side + 1) * half]
        terms = [
            jnp.dot(mask, wave[side], preferred_element_type=jnp.float32)
            for wave in (wave_hi, wave_lo)
        ]
        out_ref[side] = terms[0] + terms[1]


def frame_tables(response_ref, f):
    half = response_ref.shape[-1] // 2
    tables = []
    for side in range(2):
        row = response_ref[side, pl.ds(f, 1), :]
        parts = []
        for at in (0, half):
            spread = jnp.broadcast_to(row[:, at : at + half], (half, half))
            turned = pltpu.roll(spread, 0, 1, stride=1, stride_axis=0)
            if side:
                before = lax.broadcasted_iota(jnp.int32, (half, half), 1) < (
                    lax.broadcasted_iota(jnp.int32, (half, half), 0)
                )
                turned = jnp.where(before, -turned, turned)
            parts.append(turned)
        re, im = parts
        tables.append(
            split(jnp.concatenate([jnp.concatenate([re, im], 1), jnp.concatenate([-im, re], 1)], 0))
        )
    return tables


def normal_coils(maps_ref, field_re, field_im, tables):
    coils, _, cols, length = maps_ref.shape
    half = length // 2
    maps_re, maps_im = maps_ref[:, 0], maps_ref[:, 1]
    u_re = maps_re * field_re[None] - maps_im * field_im[None]
    u_im = maps_re * field_im[None] + maps_im * field_re[None]
    flat_re = u_re.reshape(coils * cols, length)
    flat_im = u_im.reshape(coils * cols, length)
    outs = []
    for sign, table in zip((1.0, -1.0), tables):
        packed = jnp.concatenate(
            [
                flat_re[:, :half] + sign * flat_re[:, half:],
                flat_im[:, :half] + sign * flat_im[:, half:],
            ],
            1,
        )
        outs.append(dot3(split(packed), table))
    plus, minus = outs
    v_re = jnp.concatenate(
        [plus[:, :half] + minus[:, :half], plus[:, :half] - minus[:, :half]], 1
    ).reshape(coils, cols, length)
    v_im = jnp.concatenate(
        [plus[:, half:] + minus[:, half:], plus[:, half:] - minus[:, half:]], 1
    ).reshape(coils, cols, length)
    return (
        jnp.sum(maps_re * v_re + maps_im * v_im, 0),
        jnp.sum(maps_re * v_im - maps_im * v_re, 0),
    )


def normal_frame(maps_ref, field_re, field_im, tables):
    middle = maps_ref.shape[0] // 2
    first = normal_coils(maps_ref.at[:middle], field_re, field_im, tables)
    second = normal_coils(maps_ref.at[middle:], field_re, field_im, tables)
    return first[0] + second[0], first[1] + second[1]


def coil_blocks_kernel(coils, *refs):
    *tiles, out_ref = refs
    devices, pair_coils, rows, lanes = out_ref.shape
    halves = len(tiles) // 2
    each = lanes // (2 * LANES)
    step = 8
    for part in range(2):
        for side in range(2):
            for t in range(each):
                ref = tiles[part * halves + side * each + t]
                at = (part * each + t) * LANES
                for first in range(0, coils, step):
                    for row in range(0, rows, step):
                        turned = jnp.swapaxes(ref[row : row + step, first : first + step], 0, 1)
                        for c in range(first, first + step):
                            d = c // pair_coils * 2 + side
                            out_ref[d, c % pair_coils, row : row + step, at : at + LANES] = turned[
                                c - first
                            ]


def with_bit(index, bit, value):
    return ((index >> bit) << (bit + 1)) | (value << bit) | (index & ((1 << bit) - 1))


def column_blocks_kernel(coils, frames, chunk_of, level, device_ref, *refs):
    *tiles, keep_ref, send_ref, turned = refs
    sens_tiles, image_tiles = tiles[: len(tiles) // 2], tiles[len(tiles) // 2 :]
    blocks, early, _, cols, _ = send_ref.shape
    groups = (keep_ref.shape[1] + early) // 2
    rows = sens_tiles[0].shape[0] // coils
    per = LANES // rows
    half = len(sens_tiles) // 2
    mine = (device_ref[0] >> level) & 1
    far = chunk_of[1 << level] * cols
    for g in range(groups):
        if g * per < coils:
            tiles, count, base = sens_tiles, coils, g * per
        else:
            tiles, count, base = image_tiles, frames, g * per - coils
        for t, ref in enumerate(tiles):
            turned[t // half, pl.ds(t % half * LANES, LANES)] = jnp.concatenate(
                [ref[pl.ds(base + c, rows, stride=count), :] for c in range(per)], 0
            ).T
        other = (send_ref, g) if g < early else (keep_ref, g + groups - early)
        for (out, unit), side in (((keep_ref, g), mine), (other, 1 - mine)):
            for e in range(blocks):
                at = pl.multiple_of(chunk_of[with_bit(e, level, 0)] * cols + side * far, cols)
                for part in range(2):
                    out[e, unit, part] = turned[part, pl.ds(at, cols)]


def base_kernel(start, frames, device_ref, kspace_ref, mask_ref, *refs):
    cols_ref, rows_ref, keep_ref, send_ref, data, near_hi, near_lo, masks, arrived = refs
    own, _, _, span, length = keep_ref.shape
    bit = device_ref[0] & 1
    half = length // 2
    frame = pl.program_id(0)

    def fetch(f, slot):
        return [
            pltpu.make_async_copy(
                kspace_ref.at[:, odd, start + f + c * frames, :],
                data.at[slot, c, pl.ds(odd * half, half)],
                arrived.at[slot, c, odd],
            )
            for c in range(own)
            for odd in range(2)
        ]

    @pl.when(frame == 0)
    def _():
        for copy in fetch(0, 0):
            copy.start()
        masks[...] = parted_mask(mask_ref)
        for term, near in enumerate((near_hi, near_lo)):
            for i, which in enumerate((bit, 1 - bit)):
                for part in range(2):
                    at = pl.multiple_of((2 * part + which) * span, span)
                    near[pl.ds((2 * i + part) * span, span)] = cols_ref[term, pl.ds(at, span)]

    @pl.when(frame + 1 < pl.num_programs(0))
    def _():
        for copy in fetch(frame + 1, (frame + 1) % 2):
            copy.start()

    slot = frame % 2
    for copy in fetch(frame, slot):
        copy.wait()
    columns = [
        dot3((near_hi[...], near_lo[...]), split(data[slot, c]), ((1,), (1,)))
        * masks[pl.ds(start + frame, 1), :]
        for c in range(own)
    ]
    blocks = [v[2 * i * span : (2 * i + 2) * span] for v in columns for i in range(2)]
    sides = []
    for odd in range(2):
        at = odd * half
        stacked = jnp.concatenate(
            [
                jnp.concatenate([v[:span, at : at + half], v[span:, at : at + half]], 1)
                for v in blocks
            ],
            0,
        )
        sides.append(dot3(split(stacked), (rows_ref[0, odd], rows_ref[1, odd])))
    for c in range(own):
        for i, ref in enumerate((keep_ref, send_ref)):
            rows = (2 * c + i) * span
            even, odd = [side[rows : rows + span] for side in sides]
            for part in range(2):
                e = even[:, part * half : (part + 1) * half]
                o = odd[:, part * half : (part + 1) * half]
                ref[c, 0, part] = jnp.concatenate([e + o, e - o], 1)


def weigh_kernel(outer, level, flip, device_ref, maps_ref, kept_ref, got_ref, out_ref, *refs):
    turned, maps, kept, got, total, maps_arrived, arrived, left = refs
    devices, pair_coils, rows, lanes = maps_ref.shape
    own, count = got_ref.shape[:2]
    inner, _, _, cols, length = total.shape
    inner //= outer
    span = inner * cols
    bit, which = device_ref[0] & 1, ((device_ref[0] >> level) & 1) ^ flip
    far = [pl.multiple_of((2 * i + which) * span, span) for i in range(outer)]

    map_copies = [
        pltpu.make_async_copy(maps_ref.at[:, c], maps.at[c], maps_arrived.at[c])
        for c in range(pair_coils)
    ]
    for copy in map_copies:
        copy.start()
    copies = [
        [
            pltpu.make_async_copy(
                src.at[:, f, :, pl.ds(far[i], span)],
                dst.at[:, f, :, pl.ds(i * span, span)],
                arrived.at[j, f, i],
            )
            for j, (src, dst) in enumerate(((kept_ref, kept), (got_ref, got)))
            for i in range(outer)
        ]
        for f in range(count)
    ]
    for group in copies:
        for copy in group:
            copy.start()
    for c in range(pair_coils):
        map_copies[c].wait()
        one = maps[c].reshape(length, lanes).T
        turned[c, 0] = one[: lanes // 2]
        turned[c, 1] = one[lanes // 2 :]

    results = []
    for f in range(count):
        for copy in copies[f]:
            copy.wait()
        for i in range(outer):
            here = slice(i * span, (i + 1) * span)
            total_re = total_im = 0.0
            for base, first in ((kept, bit * own), (got, (1 - bit) * own)):
                for c in range(own):
                    s_re = turned[first + c, 0, pl.ds(far[i], span), :]
                    s_im = turned[first + c, 1, pl.ds(far[i], span), :]
                    b_re, b_im = base[c, f, 0, here, :], base[c, f, 1, here, :]
                    total_re += s_re * b_re + s_im * b_im
                    total_im += s_re * b_im - s_im * b_re
            total[i * inner : (i + 1) * inner, f, 0] = total_re.reshape(inner, cols, length)
            total[i * inner : (i + 1) * inner, f, 1] = total_im.reshape(inner, cols, length)
        results.append(pltpu.make_async_copy(total.at[:, f], out_ref.at[:, f], left.at[f]))
        results[-1].start()
    for copy in results:
        copy.wait()


def first_normal_kernel(
    coils, level, device_ref, got_ref, late_ref, mask_ref, wave_hi, wave_lo, *refs
):
    maps_out, field_out, grad_out, responses = refs[-4:]
    mask_responses(mask_ref, wave_hi, wave_lo, responses)
    blocks, units, _, cols, lanes = got_ref.shape
    groups = units // 2
    early = groups - late_ref.shape[1]
    devices = 2 * blocks
    mine = (device_ref[0] >> level) & 1
    frames = field_out.shape[0]

    def block(s, g):
        e = ((s >> (level + 1)) << level) | (s & ((1 << level) - 1))
        across = ((s >> level) & 1) ^ mine
        if g < early:
            return got_ref[e, g + across * (units - early)]
        return jnp.where(across == 0, got_ref[e, g], late_ref[e, g - early])

    per = (coils + frames) // groups
    width = lanes // per
    for g in range(groups):
        out, base = (maps_out, g * per) if g * per < coils else (field_out, g * per - coils)
        for h in range(devices // per):
            exchanged = lane_exchange([block(h * per + s, g) for s in range(per)], width)
            for c in range(per):
                out[base + c, :, :, h * lanes : (h + 1) * lanes] = exchanged[c]

    def one(f, _):
        grad_out[f, 0], grad_out[f, 1] = normal_frame(
            maps_out, field_out[f, 0], field_out[f, 1], frame_tables(responses, f)
        )
        return 0

    lax.fori_loop(0, frames, one, 0, unroll=frames)


def steps_kernel(field_ref, grad_ref, maps_ref, mask_ref, *refs):
    wave_hi, wave_lo, *terms, out_ref, field, grad, responses = refs
    frames, _, cols, length = field_ref.shape
    devices, _, _, lanes = out_ref.shape
    mask_responses(mask_ref, wave_hi, wave_lo, responses)
    data_term = jnp.concatenate(
        [keep[...] + got[...] for keep, got in zip(terms[0::2], terms[1::2])], 0
    )
    field[...] = tv_step(field_ref[...] - step_size * (grad_ref[...] - data_term))
    for sweep in range(1, OUTER):

        def one(f, _):
            grad[f, 0], grad[f, 1] = normal_frame(
                maps_ref, field[f, 0], field[f, 1], frame_tables(responses, f)
            )
            return 0

        lax.fori_loop(0, frames, one, 0, unroll=frames)
        field[...] = tv_step(field[...] - step_size * (grad[...] - data_term))
    per = frames
    for h in range(devices // per):
        parts = [field[f, :, :, h * lanes : (h + 1) * lanes] for f in range(per)]
        exchanged = lane_exchange(parts, lanes // per)
        for s in range(per):
            out_ref[h * per + s] = exchanged[s]


def rows_out_kernel(chunk_of, frames, got_ref, out_ref, tiles):
    devices, _, cols, lanes = got_ref.shape
    count = tiles.shape[0]
    rows = lanes // frames
    order = sorted(range(devices), key=lambda d: chunk_of[d])
    each = LANES // cols
    for t in range(count):
        at = t % (count // 2) * each
        turned = jnp.concatenate([got_ref[d, t // (count // 2)] for d in order[at : at + each]], 0).T
        for f in range(frames):
            tiles[t, pl.ds(f, rows, stride=frames), :] = turned[f * rows : (f + 1) * rows]
        out_ref[:, t * LANES : (t + 1) * LANES] = tiles[t]


def params(limit=VMEM_LIMIT):
    return pltpu.CompilerParams(vmem_limit_bytes=limit)


def cost(flops, moved):
    return pl.CostEstimate(flops=int(flops), bytes_accessed=int(moved), transcendentals=0)


def whole(shape):
    return pl.BlockSpec(shape, lambda *_: (0,) * len(shape))


def lane_tiles(rows, lanes):
    return [
        pl.BlockSpec((rows, LANES), lambda *_, t=t: (0, t), pipeline_mode=pl.Buffered(1))
        for t in range(lanes // LANES)
    ]


def f32(*shape):
    return jax.ShapeDtypeStruct(shape, jnp.float32)


def exchange(send, bit):
    devices = lax.axis_size("coil")
    return lax.ppermute(send, "coil", [(i, i ^ (1 << bit)) for i in range(devices)])


def halve(keep, got, bit, device):
    mine = (device >> bit) & 1

    def part(which):
        return lax.dynamic_index_in_dim(
            keep, which, bit - 1, keepdims=True
        ) + lax.dynamic_index_in_dim(got, which, bit - 1, keepdims=True)

    send = part(1 - mine)
    return part(mine), send


def kernel_path(image, sens, kspace, mask):
    rows, frames, packed = image.shape
    coils = sens.shape[1]
    length, pairs, _ = kspace.shape
    half = packed // 2
    hl = length // 2
    devices = lax.axis_size("coil")
    device = lax.axis_index("coil")
    bits = devices.bit_length() - 1
    own = pairs // frames
    cols = half // devices
    per = LANES // rows
    groups = (coils + frames) // per
    chunk_of = [sum(((d >> b) & 1) << (bits - 1 - b) for b in range(bits)) for d in range(devices)]

    k = np.arange(length)
    z = np.arange(half)
    y = np.arange(hl)
    col_tables = np.stack(two_terms(packed_left(dft(z, z, half) / np.sqrt(half))))
    lanes_k = [k[0::2], k[1::2]]
    inverse = [packed_right(dft(y, ks, length)) for ks in lanes_k]
    row_tables = np.stack(two_terms(np.stack(inverse) / np.sqrt(length)))
    waves = [dft(ks, y, length) * 0.5 / hl for ks in lanes_k]
    wave_hi, wave_lo = two_terms(np.stack([np.concatenate([w.real, w.imag], 1) for w in waves]))

    sens_rows = sens.reshape(rows * coils, packed)
    image_rows = image.reshape(rows * frames, packed)

    with jax.named_scope("coil_maps"):
        blocks = pl.pallas_call(
            functools.partial(coil_blocks_kernel, coils),
            grid=(1,),
            out_shape=f32(devices, 2 * own, rows, half),
            in_specs=[
                pl.BlockSpec((rows, coils, LANES), lambda *_, t=t: (0, 0, t))
                for t in range(packed // LANES)
            ],
            out_specs=whole((devices, 2 * own, rows, half)),
            compiler_params=params(WEIGH_LIMIT),
            cost_estimate=cost(0, 2 * sens.size * 4),
        )(*[sens] * (packed // LANES))
        blocks, device = lax.optimization_barrier((blocks, device))
        coil_maps = lax.all_to_all(blocks, "coil", 0, 0, tiled=True)

    with jax.named_scope("column_maps"):
        level = 1
        early = (groups + 1) // 2
        keep_block = (devices // 2, 2 * groups - early, 2, cols, LANES)
        send_block = (devices // 2, early, 2, cols, LANES)
        column_keep, column_send = pl.pallas_call(
            functools.partial(column_blocks_kernel, coils, frames, chunk_of, level),
            grid=(1,),
            out_shape=(f32(*keep_block), f32(*send_block)),
            in_specs=[pl.BlockSpec(memory_space=pltpu.SMEM)]
            + lane_tiles(rows * coils, packed)
            + lane_tiles(rows * frames, packed),
            out_specs=(whole(keep_block), whole(send_block)),
            scratch_shapes=[pltpu.VMEM((2, half, LANES), jnp.float32)],
            compiler_params=params(),
            cost_estimate=cost(0, 2 * (sens.size + image.size) * 4),
        )(device[None], *[sens_rows] * (packed // LANES), *[image_rows] * (packed // LANES))
        column_send, device = lax.optimization_barrier((column_send, device))
        column_blocks = jnp.concatenate([column_keep, exchange(column_send, level)], 1)
        sides = [[with_bit(e, level, side) for e in range(devices // 2)] for side in range(2)]

    plans = [
        (frames // 2, list(range(1, bits))),
        (frames // 2, list(range(1, bits))),
    ]
    firsts = [sum(count for count, _ in plans[:i]) for i in range(len(plans))]
    span = half // 2
    smem = pl.BlockSpec(memory_space=pltpu.SMEM)
    kept, got = [], []
    for start, (count, _) in zip(firsts, plans):
        with jax.named_scope("data_transform"):
            block = pl.BlockSpec((own, 1, 2, span, length), lambda f: (0, f, 0, 0, 0))
            keep, send = pl.pallas_call(
                functools.partial(base_kernel, start, frames),
                grid=(count,),
                out_shape=(f32(own, count, 2, span, length),) * 2,
                in_specs=[
                    smem,
                    pl.BlockSpec(memory_space=pltpu.HBM),
                    whole((frames, length)),
                    whole((2, packed, packed)),
                    whole((2, 2, length, length)),
                ],
                out_specs=(block, block),
                scratch_shapes=[
                    pltpu.VMEM((2, own, length, packed), jnp.float32),
                    pltpu.VMEM((packed, packed), jnp.bfloat16),
                    pltpu.VMEM((packed, packed), jnp.bfloat16),
                    pltpu.VMEM((frames, length), jnp.float32),
                    pltpu.SemaphoreType.DMA((2, own, 2)),
                ],
                compiler_params=params(TRANSFORM_LIMIT),
                cost_estimate=cost(
                    own * count * 36 * half * half * length, 16 * own * count * half * length
                ),
            )(
                device[None],
                kspace.reshape(hl, 2, pairs, packed),
                mask,
                col_tables,
                row_tables,
            )
        if len(kept) == len(plans) - 1:
            column_blocks, send = lax.optimization_barrier((column_blocks, send))
        kept.append(keep)
        got.append(exchange(send, 0))
    with jax.named_scope("column_maps"):
        column_maps = lax.all_to_all(
            column_blocks, "coil", 0, 0, tiled=True, axis_index_groups=sides
        )
        column_late = exchange(column_maps[:, groups : 2 * groups - early], level)

    field = f32(frames, 2, cols, length)
    normal_cost = 6 * 2 * frames * coils * cols * length * length

    responses = pltpu.VMEM((2, frames, length), jnp.float32)

    anywhere = pl.BlockSpec(memory_space=pl.ANY)

    def first_gradient(column_maps, before):
        return pl.pallas_call(
            functools.partial(first_normal_kernel, coils, level),
            in_specs=[smem]
            + [pl.BlockSpec(memory_space=pltpu.VMEM)] * 5
            + [pl.BlockSpec(memory_space=pl.ANY)] * len(before),
            out_shape=(f32(coils, 2, cols, length), field, field),
            scratch_shapes=[responses],
            compiler_params=params(),
            cost_estimate=cost(normal_cost, 4 * sens.size * 4),
            name="first_gradient",
        )(device[None], column_maps, column_late, mask, wave_hi, wave_lo, *before)

    with jax.named_scope("data_term"):

        def weigh(stream, flip):
            count, order = plans[stream]
            outer = 2 ** (order[0] - 1)
            out = f32(devices // 4, count, 2, cols, length)
            base = pltpu.VMEM((own, count, 2, span // 2, length), jnp.float32)
            value = pl.pallas_call(
                functools.partial(weigh_kernel, outer, order[0], flip),
                out_shape=out,
                in_specs=[smem, anywhere, anywhere, anywhere],
                out_specs=anywhere,
                scratch_shapes=[
                    pltpu.VMEM((2 * own, 2, span, length), jnp.float32),
                    pltpu.VMEM((2 * own, devices, rows, half), jnp.float32),
                    base,
                    base,
                    pltpu.VMEM(out.shape, jnp.float32),
                    pltpu.SemaphoreType.DMA((2 * own,)),
                    pltpu.SemaphoreType.DMA((2, count, outer)),
                    pltpu.SemaphoreType.DMA((count,)),
                ],
                compiler_params=params(WEIGH_LIMIT),
                cost_estimate=cost(0, kept[stream].size * 4 + out.size * 4),
            )(device[None], coil_maps, kept[stream], got[stream])
            dims = [2] * (bits - 1)
            dims[order[0] - 1] = 1
            return value.reshape(*dims, *out.shape[1:])

        received = [exchange(weigh(i, 1), plans[i][1][0]) for i in range(len(plans))]
        terms = [(weigh(i, 0), received[i]) for i in range(len(plans))]
        sent = [None] * len(plans)

        def advance(stream, step):
            order = plans[stream][1]
            keep, sent[stream] = halve(*terms[stream], order[step], device)
            terms[stream] = (keep, exchange(sent[stream], order[step]))

        for step in range(1, bits - 1):
            for stream in range(len(plans)):
                advance(stream, step)
        maps, field0, grad0 = first_gradient(column_maps, sent)
        terms = [value.reshape(-1, 2, cols, length) for term in terms for value in term]

    with jax.named_scope("outer_steps"):
        blocks = pl.pallas_call(
            steps_kernel,
            out_shape=f32(devices, 2, cols, LANES),
            scratch_shapes=[pltpu.VMEM(field.shape, jnp.float32)] * 2 + [responses],
            compiler_params=params(),
            cost_estimate=cost(normal_cost, 4 * sens.size * 4),
        )(field0, grad0, maps, mask, wave_hi, wave_lo, *terms)

    with jax.named_scope("result_rows"):
        got = lax.all_to_all(blocks, "coil", 0, 0, tiled=True)
        recon = pl.pallas_call(
            functools.partial(rows_out_kernel, chunk_of, frames),
            out_shape=f32(rows * frames, packed),
            scratch_shapes=[pltpu.VMEM((packed // LANES, rows * frames, LANES), jnp.float32)],
            compiler_params=params(),
            cost_estimate=cost(0, 2 * image.size * 4),
        )(got)
    return recon.reshape(rows, frames, packed)


def einsum(form, left, right):
    return jnp.einsum(form, left, right, precision=highest, preferred_element_type=jnp.float32)


def complex_einsum(form, left, right):
    (a, b), (c, d) = left, right
    return (
        einsum(form, a, c) - einsum(form, b, d),
        einsum(form, a, d) + einsum(form, b, c),
    )


def general_path(image, sens, kspace, mask):
    rows, frames, packed = image.shape
    coils = sens.shape[1]
    length, pairs, _ = kspace.shape
    half = packed // 2
    devices = lax.axis_size("coil")
    device = lax.axis_index("coil")
    cols = half // devices

    def table(size):
        values = dft(np.arange(size), np.arange(size), size) / np.sqrt(size)
        return jnp.asarray(values.real, jnp.float32), jnp.asarray(values.imag, jnp.float32)

    inverse_rows, inverse_cols = table(length), table(half)
    forward_rows = (inverse_rows[0], -inverse_rows[1])

    both = jnp.concatenate([sens, image], 1).reshape(rows, coils + frames, 2, devices, cols)
    both = lax.all_to_all(both.transpose(3, 1, 2, 4, 0), "coil", 0, 0, tiled=True)
    both = both.transpose(1, 2, 3, 0, 4).reshape(coils + frames, 2, cols, length)
    maps, field = both[:coils], both[coils:]

    own = max(1, pairs // frames)
    repeats = devices * own // coils
    spread = jnp.repeat(sens.reshape(rows, coils // own, own, packed), repeats, axis=1)
    spread = spread.transpose(1, 0, 2, 3)
    coil_maps = lax.all_to_all(spread, "coil", 0, 0, tiled=True).reshape(length, own, packed)

    ids = device * pairs + lax.iota(jnp.int32, pairs)
    onehot = (ids[:, None] % frames == lax.iota(jnp.int32, frames)[None, :]).astype(jnp.float32)
    sampled = mask.astype(jnp.float32)
    data = einsum("pf,fk->kp", onehot, sampled)[:, :, None] * kspace
    data = (data[..., :half], data[..., half:])
    data = complex_einsum("kpz,zx->kpx", data, inverse_cols)
    data = complex_einsum("yk,kpx->ypx", inverse_rows, data)
    pair_maps = jnp.repeat(coil_maps, pairs // own, axis=1)
    m_re, m_im = pair_maps[..., :half], pair_maps[..., half:]
    weighted = jnp.stack(
        [m_re * data[0] + m_im * data[1], m_re * data[1] - m_im * data[0]], 2
    ).reshape(length, pairs, 2, devices, cols)
    term = einsum("ypcdx,pf->dfcxy", weighted, onehot)
    term = lax.psum_scatter(term, "coil", scatter_dimension=0, tiled=True)[0]

    masked = (
        sampled[:, :, None] * forward_rows[0][None],
        sampled[:, :, None] * forward_rows[1][None],
    )
    project = complex_einsum("yk,fkv->fyv", inverse_rows, masked)
    for sweep in range(OUTER):
        u_re = maps[:, None, 0] * field[None, :, 0] - maps[:, None, 1] * field[None, :, 1]
        u_im = maps[:, None, 0] * field[None, :, 1] + maps[:, None, 1] * field[None, :, 0]
        v_re, v_im = complex_einsum("fyv,cfxv->cfxy", project, (u_re, u_im))
        grad = jnp.stack(
            [
                jnp.sum(maps[:, None, 0] * v_re + maps[:, None, 1] * v_im, 0),
                jnp.sum(maps[:, None, 0] * v_im - maps[:, None, 1] * v_re, 0),
            ],
            1,
        )
        target = field - step_size * (grad - term)
        dual_time = jnp.zeros_like(target)
        dual_rows = jnp.zeros_like(target)
        field = target
        for repeat in range(INNER):
            diff_time = jnp.concatenate([field[1:] - field[:-1], jnp.zeros_like(field[:1])], 0)
            diff_rows = jnp.concatenate(
                [field[..., 1:] - field[..., :-1], jnp.zeros_like(field[..., :1])], -1
            )
            dual_time = jnp.clip(dual_time + dual_step * diff_time, -1.0, 1.0)
            dual_rows = jnp.clip(dual_rows + dual_step * diff_rows, -1.0, 1.0)
            inner_time, inner_rows = dual_time[:-1], dual_rows[..., :-1]
            none_time, none_rows = jnp.zeros_like(field[:1]), jnp.zeros_like(field[..., :1])
            divergence = (
                jnp.concatenate([none_time, inner_time], 0)
                - jnp.concatenate([inner_time, none_time], 0)
                + jnp.concatenate([none_rows, inner_rows], -1)
                - jnp.concatenate([inner_rows, none_rows], -1)
            )
            field = target - tv_weight * divergence

    result = field.reshape(frames, 2, cols, devices, rows).transpose(3, 0, 1, 2, 4)
    result = lax.all_to_all(result, "coil", 0, 0, tiled=True)
    return result.transpose(4, 1, 2, 0, 3).reshape(rows, frames, packed)


def fits_kernels(image, sens, kspace, devices):
    rows, frames, packed = image.shape
    coils = sens.shape[1]
    length, pairs, _ = kspace.shape
    per = LANES // rows
    return (
        devices & (devices - 1) == 0
        and devices >= 4
        and rows % 8 == 0
        and rows * per == LANES
        and frames == per
        and frames % 2 == 0
        and coils % per == 0
        and devices % per == 0
        and pairs % frames == 0
        and pairs * devices == coils * frames
        and length == 2 * LANES
        and packed % (16 * devices) == 0
        and packed % (4 * LANES) == 0
    )


def per_device(image, sens, kspace, mask):
    if fits_kernels(image, sens, kspace, lax.axis_size("coil")):
        return kernel_path(image, sens, kspace, mask)
    return general_path(image, sens, kspace, mask)


def solution(mesh):
    return jax.shard_map(
        per_device,
        mesh=mesh,
        in_specs=(
            P(("plane", "coil"), None, None),
            P(("plane", "coil"), None, None),
            P("plane", "coil", None),
            P(),
        ),
        out_specs=P(("plane", "coil"), None, None),
        check_vma=False,
    )
```
